256 devices in a mesh: trow: 16 (over z, x_lo), tcol: 16 (over y, x_hi, core).
Axes of the slice: x: 4 (x_hi: 2, x_lo: 2; x = x_hi * 2 + x_lo), y: 4, z: 8, core: 2. Of those that a mesh axis runs over, the one named last changes fastest.
Arguments:
- latent: bfloat16 [128, 512, 1152], P('trow', 'tcol'), may hold values from -6 to 6
- control: bfloat16 [16, 64, 144, 1152], P('trow', 'tcol'), may hold values from -4 to 4
- valid: int32 [16, 64, 144], P('trow', 'tcol'), may hold values from 0 to 1, as said below
- radius: int32 [16], replicated, may hold values from 1 to 5
- modulation: float32 [2, 3, 1152], replicated, may hold values from -3 to 3
- w_qkv: bfloat16 [1152, 3456], replicated, as said below
- w_out: bfloat16 [1152, 1152], replicated, may hold values from -0.1875 to 0.1875
Outputs:
- blended: bfloat16 [128, 512, 1152], P('trow', 'tcol')
The draws below stay inside these ranges and needn't reach their ends.
Inputs may be any that keep to these rules, and one draw needn't show every extreme that they name: `valid`: for each tile and each of its four sides a band width of 1 or 2 margin tokens is drawn; a token is 1 when its row and its column each lie in the core or in that side's band, and 0 otherwise; margin tokens outside the image are 0; core tokens are always 1. `w_qkv`: entries lie within -72 / sqrt(1152) and 72 / sqrt(1152).
All inputs are finite; a program needn't handle non-finite values.
Results may differ from the reference program's by a relative error of at most 0.009.
The reference program's roundings to bfloat16 on the way count: a program that leaves them out, or rounds other values in their place, can miss the bound.
Values may be sent and summed in bfloat16 or wider, within the bound.
No kernel may reach another device: no remote copies, remote signals or barrier semaphores. Data moves between devices by JAX's collectives and lax.ppermute only.
A program may use at most 192 MiB of HBM per device.

```python
import jax
import jax.numpy as jnp
from jax import lax

D = 1152
HEADS = 16
HEAD_DIM = 72
CORE = 8
MARGIN = 2
TILE_ROWS = 16
TILE_COLS = 64
GRID_R = 128
GRID_C = 512
TILE_TOK = 144


def draw_valid(key, part):
    key = jax.random.fold_in(key, 1)
    side = CORE + 2 * MARGIN
    widths = jax.random.randint(key, (TILE_ROWS, TILE_COLS, 4), 1, MARGIN + 1)
    index = jnp.arange(side, dtype=jnp.int32)
    tile_r = jnp.arange(TILE_ROWS, dtype=jnp.int32)[:, None, None]
    tile_c = jnp.arange(TILE_COLS, dtype=jnp.int32)[None, :, None]
    core = (index >= MARGIN) & (index < MARGIN + CORE)
    north = (index < MARGIN) & (index >= MARGIN - widths[..., 0:1]) & (tile_r > 0)
    south = (index >= MARGIN + CORE) & (index < MARGIN + CORE + widths[..., 1:2]) & (tile_r < TILE_ROWS - 1)
    west = (index < MARGIN) & (index >= MARGIN - widths[..., 2:3]) & (tile_c > 0)
    east = (index >= MARGIN + CORE) & (index < MARGIN + CORE + widths[..., 3:4]) & (tile_c < TILE_COLS - 1)
    rowok = core[None, None] | north | south
    colok = core[None, None] | west | east
    grid = rowok[..., :, None] & colok[..., None, :]
    return grid.reshape(TILE_ROWS, TILE_COLS, side * side).astype(jnp.int32)


def draw_w_qkv(key, part):
    key = jax.random.fold_in(key, 2)
    base = jax.random.truncated_normal(key, -6.0, 6.0, (D, 3 * D), jnp.float32) * D ** (-0.5)
    return base.astype(jnp.bfloat16)


def plant(result, own_key, low, largest):
    spot = [jax.random.randint(jax.random.fold_in(own_key, axis), (), 0, length) for axis, length in enumerate(result.shape)]
    longest = result.shape.index(max(result.shape))
    next_to = spot[:longest] + [(spot[longest] + 1) % result.shape[longest]] + spot[longest + 1:]
    return result.at[tuple(spot)].set(low).at[tuple(next_to)].set(largest)


def steps_of(rng, extent, pieces, smallest, largest):
    def one(dim, parts):
        steps = jax.random.uniform(jax.random.fold_in(jax.random.fold_in(rng, 6), dim), (parts,), jnp.float32, smallest / len(pieces), largest / len(pieces))
        return jnp.repeat(jnp.exp(steps), extent[dim] // parts).reshape((-1,) + (1,) * (len(extent) - dim - 1))

    gain = one(*pieces[0])
    for cut in pieces[1:]:
        gain = gain * one(*cut)
    return gain


def centred(own_key, extent, scale, bound, pieces=(), kind=jnp.bfloat16):
    result = scale * jax.random.normal(own_key, extent, jnp.float32)
    if pieces:
        result = result * steps_of(own_key, extent, pieces, -0.22, 0.18)
    return jnp.clip(result, -bound, bound).astype(kind)


def setup_inputs(seed: int = 0) -> dict:
    arg_keys = jax.random.split(jax.random.key(seed), 8)
    latent = centred(arg_keys[0], (GRID_R, GRID_C, D), 1.0, 6.0, ((0, 16), (1, 16)))
    control = centred(arg_keys[1], (TILE_ROWS, TILE_COLS, TILE_TOK, D), 0.5, 4.0, ((0, 16), (1, 16)))
    valid = draw_valid(jax.random.fold_in(arg_keys[7], 71), 0)
    radius = plant(jax.random.randint(arg_keys[3], (HEADS,), 1, 6), jax.random.fold_in(arg_keys[3], 1), 1, 5).astype(jnp.int32)
    modulation = centred(arg_keys[4], (2, 3, D), 0.5, 3.0, (), jnp.float32)
    w_qkv = draw_w_qkv(jax.random.fold_in(arg_keys[7], 71), 0)
    w_out = centred(arg_keys[6], (D, D), D ** -0.5, 0.1875)
    return dict(latent=latent, control=control, valid=valid, radius=radius, modulation=modulation, w_qkv=w_qkv, w_out=w_out)


GUIDE = 4.5

def pad_front(array, before, after):
    widths = [(before, after)] + [(0, 0)] * (array.ndim - 1)
    return jnp.pad(array, widths)

def cut_tiles(grid, axis):
    moved = jnp.moveaxis(grid, axis, 0)
    count = (moved.shape[0] - 2 * MARGIN) // CORE
    rest = moved.shape[1:]
    head = moved[:CORE * count].reshape((count, CORE) + rest)
    tail = pad_front(moved[CORE:], 0, CORE - 2 * MARGIN).reshape((count, CORE) + rest)[:, :2 * MARGIN]
    tiles = jnp.concatenate([head, tail], axis=1)
    return jnp.moveaxis(tiles, (0, 1), (axis, axis + 1))

def place_tiles(tiles, axis):
    moved = jnp.moveaxis(tiles, (axis, axis + 1), (0, 1))
    count = moved.shape[0]
    rest = moved.shape[2:]
    head = pad_front(moved[:, :CORE].reshape((count * CORE,) + rest), 0, 2 * MARGIN)
    tail = jnp.moveaxis(pad_front(jnp.moveaxis(moved[:, CORE:], 1, 0), 0, CORE - 2 * MARGIN), 0, 1)
    tail = pad_front(tail.reshape((count * CORE,) + rest), CORE, 0)[:CORE * count + 2 * MARGIN]
    return jnp.moveaxis(head + tail, 0, axis)

def block_rows(tokens, control, valid, radius, modulation, w_qkv, w_out):
    side = CORE + 2 * MARGIN
    count = tokens.shape[0]
    index = jnp.arange(TILE_TOK, dtype=jnp.int32)
    row_pos = index // side
    col_pos = index % side
    dist = jnp.maximum(jnp.abs(row_pos[:, None] - row_pos[None, :]), jnp.abs(col_pos[:, None] - col_pos[None, :]))
    near = dist[None] <= radius[:, None, None]
    itself = index[:, None] == index[None, :]
    keyok = (valid[:, None, :] > 0) | itself[None]
    allowed = near[None] & keyok[:, None]
    xf = tokens.astype(jnp.float32)
    mean = lax.optimization_barrier(jnp.mean(xf, axis=-1, keepdims=True))
    var = lax.optimization_barrier(jnp.mean((xf - mean) ** 2, axis=-1, keepdims=True))
    normed = (xf - mean) * lax.rsqrt(var + 1e-06)
    hidden = (normed[None] * (1.0 + modulation[:, 1][:, None, None]) + modulation[:, 0][:, None, None]).astype(jnp.bfloat16)
    qkv = jnp.einsum('bntd,de->bnte', hidden.astype(jnp.float32), w_qkv.astype(jnp.float32)).astype(jnp.bfloat16)
    query = qkv[..., :D].reshape(2, count, TILE_TOK, HEADS, HEAD_DIM)
    keys = qkv[..., D:2 * D].reshape(2, count, TILE_TOK, HEADS, HEAD_DIM)
    values = qkv[..., 2 * D:].reshape(2, count, TILE_TOK, HEADS, HEAD_DIM)
    scores = jnp.einsum('bnqhd,bnkhd->bnhqk', query.astype(jnp.float32), keys.astype(jnp.float32)) / jnp.sqrt(jnp.float32(HEAD_DIM))
    scores = jnp.where(allowed[None], scores, jnp.float32(-1e+30))
    top = lax.optimization_barrier(jnp.max(scores, axis=-1, keepdims=True))
    expo = jnp.exp(scores - top)
    probs = (expo / lax.optimization_barrier(jnp.sum(expo, axis=-1, keepdims=True))).astype(jnp.bfloat16)
    attn = jnp.einsum('bnhqk,bnkhd->bnqhd', probs.astype(jnp.float32), values.astype(jnp.float32)).astype(jnp.bfloat16)
    attn = attn.reshape(2, count, TILE_TOK, D)
    projected = jnp.einsum('bntd,de->bnte', attn.astype(jnp.float32), w_out.astype(jnp.float32))
    branch_out = xf[None] + modulation[:, 2][:, None, None] * projected + control.astype(jnp.float32)[None]
    guided = branch_out[1] + GUIDE * (branch_out[0] - branch_out[1])
    return guided * valid.astype(jnp.float32)[..., None]

def reference(latent, control, valid, radius, modulation, w_qkv, w_out):
    side = CORE + 2 * MARGIN
    padded = jnp.pad(latent, ((MARGIN, MARGIN), (MARGIN, MARGIN), (0, 0)))
    tiles = cut_tiles(cut_tiles(padded, 0), 2)
    tok = tiles.transpose(0, 2, 1, 3, 4).reshape(TILE_ROWS, TILE_COLS, TILE_TOK, D)

    def one_row(items):
        return block_rows(items[0], items[1], items[2], radius, modulation, w_qkv, w_out)
    terms = lax.map(one_row, (tok, control, valid))
    terms = terms.reshape(TILE_ROWS, TILE_COLS, side, side, D).transpose(0, 2, 1, 3, 4)
    weights = valid.astype(jnp.float32).reshape(TILE_ROWS, TILE_COLS, side, side).transpose(0, 2, 1, 3)
    sums = place_tiles(place_tiles(terms, 0), 1)
    counts = place_tiles(place_tiles(weights, 0), 1)
    core_sum = sums[MARGIN:MARGIN + GRID_R, MARGIN:MARGIN + GRID_C]
    core_count = counts[MARGIN:MARGIN + GRID_R, MARGIN:MARGIN + GRID_C]
    return (core_sum / core_count[..., None]).astype(jnp.bfloat16)
```

```python
import functools

import jax
import jax.numpy as jnp
import numpy as np
from jax import lax
from jax.experimental import pallas as pl
from jax.experimental.pallas import tpu as pltpu
from jax.sharding import PartitionSpec as P

D = 1152
HEADS = 16
HEAD_DIM = 72
CORE = 8
MARGIN = 2
SIDE = 12
TILE_TOK = 144
GUIDE = 4.5
REACH = 5
FAR = 99.0
BF = jnp.bfloat16
F32 = jnp.float32
EXP_SCALE = float(np.log2(np.e) / np.sqrt(72.0))
VMEM = 56 * 1024 * 1024

JR = np.array([j // 4 if j < 32 else (j - 40) // 4 if j < 40 else 8 + (j - 40) // 4 for j in range(48)])
JC = np.arange(48) % 4


def one_hot(rows, depth):
    hot = np.zeros((len(rows), depth), np.float32)
    for i, src in enumerate(rows):
        if src is not None and src >= 0:
            hot[i, src] = 1.0
    return hot


def source(row, col):
    if col < 0:
        return 384 + (row + 2) * REACH + col + REACH if col >= -REACH else None
    if col >= 32:
        return 480 + (row + 2) * REACH + col - 32 if col < 32 + REACH else None
    if row < 0:
        return 256 + (row + 2) * 32 + col
    if row >= 8:
        return 320 + (row - 8) * 32 + col
    return row * 32 + col


def kv_cols(block):
    return 4 * block - 2 + JC


def slots(block):
    cols = kv_cols(block)
    if block == 0:
        return [(0, [(-1, c) if c < 2 else (0, c - 2) for c in JC])]
    if block == 8:
        return [(3, [(3, 30 + c) if c < 2 else (4, 28 + c) for c in JC])]
    if block % 2:
        return [((block - 1) // 2, [((block - 1) // 2, c) for c in cols])]
    return [(block // 2 - 1, [(block // 2 - 1, c) for c in cols]), (block // 2, [(block // 2, c) for c in cols])]


def unit_queries(unit):
    out = []
    for block in range(2 * unit, 2 * unit + 3):
        pairs = dict(slots(block))[unit]
        out += [(int(tile), int(JR[j]), int(pairs[j][1])) for j in range(48)]
    return out


def window_keys(first, count):
    keys = [(int(JR[j]), int(kv_cols(b)[j])) for b in range(first, first + count) for j in range(48)] if False else []
    for b in range(first, first + count):
        cols = kv_cols(b)
        keys += [(int(JR[j]), int(cols[j])) for j in range(48)]
    return keys + [None] * (256 - len(keys))


def unit_queries(unit):
    out = []
    for block in range(2 * unit, 2 * unit + 3):
        pairs = dict(slots(block))[unit]
        out += [(int(pairs[j][0]), int(JR[j]), int(pairs[j][1])) for j in range(48)]
    return out


def tile_token(tile, row, col):
    r, c = row + 2, col - 8 * tile + 2
    return r * SIDE + c if 0 <= r < SIDE and 0 <= c < SIDE else None


def distances(queries, keys):
    dist = np.full((len(queries), 256), FAR, np.float32)
    for i, (tile, row, col) in enumerate(queries):
        for k, key in enumerate(keys):
            if key is not None and tile_token(tile, *key) is not None:
                if -REACH <= key[1] < 32 + REACH:
                    dist[i, k] = max(abs(row - key[0]), abs(col - key[1]))
    return dist


def key_map(tile, keys):
    return one_hot([None if key is None else tile_token(tile, *key) for key in keys], TILE_TOK).T


def query_map(unit, tile):
    return one_hot([tile_token(t, r, c) if t == tile else None for t, r, c in unit_queries(unit)], TILE_TOK)


@functools.cache
def tables():
    bf = lambda a: np.asarray(a, jnp.bfloat16)
    own = lambda b: [(int(JR[j]), int(kv_cols(b)[j])) for j in range(32)]
    rim = lambda b: [(int(JR[j]), int(kv_cols(b)[j])) for j in range(32, 48)]
    every = lambda b: [(int(JR[j]), int(kv_cols(b)[j])) for j in range(48)]
    t = {}
    t["own"] = bf(one_hot([source(*p) for b in range(1, 8) for p in own(b)], 256))
    t["rim"] = bf(one_hot([source(*p) - 256 for b in range(1, 8) for p in rim(b)], 128))
    dup = [(r, c) for _, r, c in unit_queries(0)[:48]] + [(r, c) for _, r, c in unit_queries(3)[96:]]
    edge = [p for b in (-1, 0, 8, 9) for p in every(b)] + dup
    t["edge"] = bf(one_hot([source(*p) for p in edge], 576))
    slot_pos = []
    for b in range(9):
        unit = min(b // 2, 3)
        slot_pos.append(unit_queries(unit)[(b - 2 * unit) * 48 : (b - 2 * unit + 1) * 48])
    t["x_core"] = bf(one_hot([source(r, c) for q in slot_pos for _, r, c in q[:32]], 256))
    t["x_rim"] = bf(one_hot([source(r, c) - 256 for q in slot_pos for _, r, c in q[32:]], 128))
    mid, west, east = window_keys(2, 5), window_keys(-1, 4), window_keys(6, 4)
    t["dist_mid"] = bf(distances(unit_queries(1) + unit_queries(2), mid))
    t["dist_side"] = bf(np.stack([distances(unit_queries(0), west), distances(unit_queries(3), east)]))
    t["key_mid"] = bf(np.stack([key_map(1, mid), key_map(2, mid)]))
    t["key_side"] = bf(np.stack([key_map(0, west), key_map(-1, west), key_map(3, east), key_map(4, east)]))
    t["query"] = bf(np.stack([query_map(u, u) for u in range(4)]))
    t["query_side"] = bf(np.stack([query_map(0, -1), query_map(3, 4)]))
    send = np.zeros((2, 64, 384), np.float32)
    ctl = np.zeros((2, 32, TILE_TOK), np.float32)
    for r in range(SIDE):
        for k in range(REACH):
            send[0, r * REACH + k, source(r - 2, k)] = 1.0
            send[1, r * REACH + k, source(r - 2, 32 - REACH + k)] = 1.0
        for k in range(2):
            ctl[0, r * 2 + k, r * SIDE + k] = 1.0
            ctl[1, r * 2 + k, r * SIDE + 10 + k] = 1.0
    t["send_own"], t["send_rim"] = bf(send[:, :, :256]), bf(send[:, :, 256:])
    t["send_ctl"] = bf(ctl)
    t["valid_pad"] = bf(np.eye(TILE_TOK, 256))
    put = np.zeros((2, 48, 32), np.float32)
    for j in range(48):
        if JC[j] < 2:
            put[0, j, (JR[j] + 2) * 2 + JC[j]] = 1.0
        else:
            put[1, j, (JR[j] + 2) * 2 + JC[j] - 2] = 1.0
    t["put_ctl"] = bf(put)
    back = np.zeros((256, 288), np.float32)
    for b in range(9):
        for j in range(32):
            if (b == 0 and JC[j] < 2) or (b == 8 and JC[j] >= 2):
                continue
            _, r, c = slot_pos[b][j]
            back[r * 32 + c, b * 32 + j] = 1.0
    assert (back.sum(1) == 1).all()
    t["back"] = bf(back)
    return t


def holders(block):
    out = []
    if block % 2 == 0 and block > 0:
        out.append((block // 2 - 1, 2))
    if block % 2 == 0 and block < 8:
        out.append((block // 2, 0))
    if block % 2:
        out.append(((block - 1) // 2, 1))
    return out


def dot(a, b):
    return jnp.dot(a, b, preferred_element_type=F32)


def dot_nt(a, b):
    return lax.dot_general(a, b, (((1,), (1,)), ((), ())), preferred_element_type=F32)


def hidden_rows(x, mod_ref):
    mean = jnp.mean(x, axis=-1, keepdims=True)
    centred = x - mean
    var = jnp.mean(centred * centred, axis=-1, keepdims=True)
    normed = centred * lax.rsqrt(var + 1e-6)
    return [(normed * (1.0 + mod_ref[g, 1:2, :]) + mod_ref[g, 0:1, :]).astype(BF) for g in (0, 1)]


def fill_bias(bias_ref, where, dist, row_a, row_b, second):
    usable = jnp.where(second, row_b, row_a) > 0.5
    usable = usable | (dist == 0.0)
    for r in range(5):
        bias_ref[where + (r,)] = jnp.where(usable & (dist <= r + 1.0), 0.0, -1e30)


def attend(q_ref, k_ref, v_ref, bias, radius_ref, weight, out_ref):
    lane = lax.broadcasted_iota(jnp.int32, (1, 256), 1)
    lane128 = lax.broadcasted_iota(jnp.int32, (1, 128), 1)
    tiles = {}
    for h in range(HEADS):
        lo = HEAD_DIM * h
        base = min(lo // 128, 7) * 128
        keep = ((lane >= lo - base) & (lane < lo + HEAD_DIM - base)).astype(F32).astype(BF)
        q = q_ref[:, base : base + 256] * keep
        s = dot_nt(q, k_ref[:, base : base + 256]) + bias(radius_ref[h] - 1)
        top = jnp.max(s, axis=-1, keepdims=True)
        e = jnp.exp2((s - top) * EXP_SCALE)
        total = jnp.sum(e, axis=-1, keepdims=True)
        o = dot(e.astype(BF), v_ref[:, base : base + 256])
        scale = weight / total
        for half in (0, 1):
            j = base // 128 + half
            start, end = max(lo - j * 128, 0), min(lo + HEAD_DIM - j * 128, 128)
            if start >= end:
                continue
            piece = o[:, half * 128 : half * 128 + 128] * scale
            if j in tiles:
                piece = jnp.where(lane128 >= start, piece, tiles[j])
            tiles[j] = piece
            if end == 128:
                out_ref[:, j * 128 : (j + 1) * 128] = tiles.pop(j).astype(BF)


def own_kernel(latent, control, valid, mod, w, own, send_own, send_ctl, valid_pad, qkv, msg, hid):
    step = pl.program_id(0)

    @pl.when(step == 0)
    def _():
        rows = hidden_rows(dot(own[...], latent[...]), mod)
        hid[:224] = rows[0]
        hid[224:] = rows[1]

    out = dot(hid[...], w[...]).astype(BF)
    qkv[0, 0] = out[:224]
    qkv[0, 1] = out[224:]

    @pl.when(step == 2)
    def _():
        rows = lax.broadcasted_iota(jnp.int32, (32, 1), 0)
        val = valid[...].astype(F32)
        for i, tile in ((0, 0), (1, 3)):
            msg[i, :64] = dot(send_own[i], latent[...]).astype(BF)
            hot = (send_ctl[i].astype(F32) * val[tile : tile + 1]).astype(BF)
            ctl = dot(hot, control[tile])
            row = dot(jnp.broadcast_to(val[tile : tile + 1], (8, TILE_TOK)).astype(BF), valid_pad[...])
            msg[i, 64:, 256:] = ctl[:, 256:].astype(BF)
            msg[i, 64:, :256] = jnp.where(rows == 31, row[0:1], ctl[:, :256]).astype(BF)


def pack_kernel(msg, above, below, send_rim, west, east):
    for i, out in ((0, west), (1, east)):
        rim = dot(send_rim[i, :, :64], above[...]) + dot(send_rim[i, :, 64:], below[...])
        out[:64] = (msg[i, :64].astype(F32) + rim).astype(BF)
        out[64:] = msg[i, 64:]


def middle_kernel(
    radius, above, below, valid, mod, w, qkv_own, rim, dist, key_map_ref, query, qkv, attn, hid, part, qw, kw, vw, bias
):
    step = pl.program_id(0)

    @pl.when(step == 0)
    def _():
        x = dot(rim[:, :64], above[...]) + dot(rim[:, 64:], below[...])
        rows = hidden_rows(x, mod)
        hid[:112] = rows[0]
        hid[112:] = rows[1]

    @pl.when(step < 3)
    def _():
        out = dot(hid[...], w[...]).astype(BF)
        qkv[0, 0] = out[:112]
        qkv[0, 1] = out[112:]
        part[step, 0] = out[:112]
        part[step, 1] = out[112:]

    @pl.when(step == 2)
    def _():
        val = valid[...].astype(F32).astype(BF)
        row_a = dot(val, key_map_ref[0])[1:2]
        row_b = dot(val, key_map_ref[1])[2:3]
        second = lax.broadcasted_iota(jnp.int32, (288, 1), 0) >= 144
        fill_bias(bias, (), dist[...].astype(F32), row_a, row_b, second)
        for g in (0, 1):
            for c, win in ((1, kw), (2, vw)):
                for i in range(5):
                    b = 2 + i
                    win[g, i * 48 : i * 48 + 32] = qkv_own[c, g, (b - 1) * 32 : b * 32]
                    win[g, i * 48 + 32 : i * 48 + 48] = part[c, g, (b - 1) * 16 : b * 16]
                win[g, 240:] = jnp.zeros((16, D), BF)
            for u in (0, 1):
                for i in range(3):
                    b = 2 + 2 * u + i
                    qw[g, u, i * 48 : i * 48 + 32] = qkv_own[0, g, (b - 1) * 32 : b * 32]
                    qw[g, u, i * 48 + 32 : i * 48 + 48] = part[0, g, (b - 1) * 16 : b * 16]

    @pl.when(step >= 3)
    def _():
        g = (step - 3) // 2
        u = (step - 3) % 2
        val = valid[pl.ds(u + 1, 1), :].astype(F32)
        weight = jnp.sum(query[0].astype(F32) * val, axis=1, keepdims=True)
        attend(
            qw.at[g, u], kw.at[g], vw.at[g], lambda r: bias[r, pl.ds(pl.multiple_of(u * 144, 16), 144), :], radius, weight, attn.at[0, 0]
        )


def unit_weights(unit, query, query_side, rows):
    hot = query[unit].astype(F32) * rows[unit]
    weight = jnp.sum(hot, axis=1, keepdims=True)
    if unit in (0, 3):
        i = unit // 3
        weight = weight + jnp.sum(query_side[i].astype(F32) * rows[4 + i], axis=1, keepdims=True)
    return hot, weight


def valid_rows(valid, west, east):
    val = valid[...].astype(F32)
    rows = [val[t : t + 1] for t in range(4)]
    for ref in (west, east):
        rows.append(ref[80:96, :256].astype(F32)[15:16, :TILE_TOK])
    return rows


def edge_kernel(
    radius, latent, above, below, west, east, valid, mod, w, qkv_own, qkv_rim, attn_mid, w_out, control,
    edge, dist, key_side, query, query_side, x_rim, put_ctl,
    up, down, core, count, hid, part, qw, kw, vw, bias, weights, attn,
):
    step = pl.program_id(0)

    @pl.when(step == 0)
    def _():
        x = (
            dot(edge[:, :256], latent[...])
            + dot(edge[:, 256:320], above[...])
            + dot(edge[:, 320:384], below[...])
            + dot(edge[:, 384:480], west[...])
            + dot(edge[:, 480:], east[...])
        )
        rows = hidden_rows(x, mod)
        hid[:192] = rows[0][:192]
        hid[192:384] = rows[1][:192]
        hid[384:480] = rows[0][192:]
        hid[480:] = rows[1][192:]

    @pl.when(step == 0)
    def _():
        out = dot(hid[384:], w[...]).astype(BF)
        for i in (0, 1):
            for g in (0, 1):
                at = g * 96 + i * 48
                qw[i, g, 96 * i : 96 * i + 48] = out[at : at + 48]

    @pl.when((step == 1) | (step == 2))
    def _():
        out = dot(hid[:384], w[...]).astype(BF)
        part[step - 1, 0] = out[:192]
        part[step - 1, 1] = out[192:]

    @pl.when(step == 2)
    def _():
        rows = valid_rows(valid, west, east)
        pair = lax.broadcasted_iota(jnp.int32, (144, 1), 0)
        for i, unit in ((0, 0), (1, 3)):
            eight = lambda r: jnp.broadcast_to(r, (8, TILE_TOK)).astype(BF)
            row_a = dot(eight(rows[unit]), key_side[2 * i])[0:1]
            row_b = dot(eight(rows[4 + i]), key_side[2 * i + 1])[0:1]
            second = (pair < 48) & (pair % 4 < 2) if i == 0 else (pair >= 96) & (pair % 4 >= 2)
            fill_bias(bias, (i,), dist[i].astype(F32), row_a, row_b, second)
            weights[i] = jnp.broadcast_to(unit_weights(unit, query, query_side, rows)[1], (144, 128))
            edges = ((0, 0), (1, 1)) if i == 0 else ((2, 2), (3, 3))
            inner = ((2, 1), (3, 2)) if i == 0 else ((0, 6), (1, 7))
            for g in (0, 1):
                for c, win in ((1, kw), (2, vw)):
                    for at, e in edges:
                        win[i, g, at * 48 : at * 48 + 48] = part[c - 1, g, e * 48 : e * 48 + 48]
                    for at, b in inner:
                        win[i, g, at * 48 : at * 48 + 32] = qkv_own[c, g, (b - 1) * 32 : b * 32]
                        win[i, g, at * 48 + 32 : at * 48 + 48] = qkv_rim[c, g, (b - 1) * 16 : b * 16]
                    win[i, g, 192:] = jnp.zeros((64, D), BF)
                for at, b in ((1, 1), (2, 2)) if i == 0 else ((0, 6), (1, 7)):
                    qw[i, g, at * 48 : at * 48 + 32] = qkv_own[0, g, (b - 1) * 32 : b * 32]
                    qw[i, g, at * 48 + 32 : at * 48 + 48] = qkv_rim[0, g, (b - 1) * 16 : b * 16]

    @pl.when((step >= 3) & (step < 7))
    def _():
        i = (step - 3) // 2
        g = (step - 3) % 2
        attend(qw.at[i, g], kw.at[i, g], vw.at[i, g], lambda r: bias[i, r], radius, weights[i][:, :1], attn.at[i, g])

    @pl.when(step == 7)
    def _():
        rows = valid_rows(valid, west, east)
        hots, wts = zip(*[unit_weights(u, query, query_side, rows) for u in range(4)])
        margin = [[], []]
        for g in (0, 1):
            for b in range(9):
                total = None
                for u, third in holders(b):
                    src = attn[u // 3, g] if u in (0, 3) else attn_mid[g, u - 1]
                    piece = src[third * 48 : third * 48 + 48].astype(F32)
                    total = piece if total is None else total + piece
                total = total.astype(BF)
                core[g, b * 32 : (b + 1) * 32] = total[:32]
                margin[g].append(total[32:])
        proj = dot(jnp.concatenate(margin[0] + margin[1], axis=0), w_out[...])
        sums = (GUIDE * mod[0, 2:3]) * proj[:144] + ((1.0 - GUIDE) * mod[1, 2:3]) * proj[144:]
        ctl = []
        for u in range(4):
            hot = jnp.concatenate([hots[u][i * 48 + 32 : i * 48 + 48] for i in range(3)], axis=0).astype(BF)
            ctl.append(dot(hot, control[u]))
        counts, extra = [], []
        for b in range(9):
            number = sum(wts[u][third * 48 : third * 48 + 48] for u, third in holders(b))
            count[b * 32 : (b + 1) * 32] = jnp.broadcast_to(number[:32], (32, 128))
            counts.append(number[32:])
            term = sum(ctl[u][third * 16 : third * 16 + 16] for u, third in holders(b))
            if b in (0, 8):
                term = term + dot(put_ctl[b // 8, 32:], (west if b == 0 else east)[64:])
            extra.append(term)
        number = jnp.concatenate(counts, axis=0)
        x = dot(x_rim[:, :64], above[...]) + dot(x_rim[:, 64:], below[...])
        sums = sums + number * x + jnp.concatenate(extra, axis=0)
        slot = lax.broadcasted_iota(jnp.int32, (72, D), 0)
        lane = lax.broadcasted_iota(jnp.int32, (72, D), 1)
        for at, out in ((0, up), (8, down)):
            pick = lambda a: jnp.concatenate([a[b * 16 + at : b * 16 + at + 8] for b in range(9)], axis=0)
            tail = jnp.sum(jnp.where(slot == lane, pick(number), 0.0), axis=0, keepdims=True)
            out[...] = jnp.concatenate([pick(sums), jnp.broadcast_to(tail, (8, D))], axis=0).astype(BF)


def core_kernel(core, w_out, mod, latent, control, valid, west, east, count, x_core, query, put_ctl, sums):
    val = valid[...].astype(F32)
    proj = dot(core[...].reshape(576, D), w_out[...])
    ctl = []
    for u in range(4):
        hot = (query[u].astype(F32) * val[u : u + 1]).astype(BF)
        hot = jnp.concatenate([hot[i * 48 : i * 48 + 32] for i in range(3)], axis=0)
        ctl.append(dot(hot, control[u]))
    x = dot(x_core[...], latent[...])
    gate0, gate1 = GUIDE * mod[0, 2:3], (1.0 - GUIDE) * mod[1, 2:3]
    for b in range(9):
        at = slice(b * 32, (b + 1) * 32)
        term = sum(ctl[u][third * 32 : third * 32 + 32] for u, third in holders(b))
        if b in (0, 8):
            term = term + dot(put_ctl[b // 8, :32], (west if b == 0 else east)[64:])
        term = term + gate0 * proj[at] + gate1 * proj[288 + b * 32 : 288 + (b + 1) * 32]
        sums[at] = term + count[at][:, :1] * x[at]


def final_kernel(sums, count, above, below, back, out):
    slot = lax.broadcasted_iota(jnp.int32, (72, 128), 0)
    lane = lax.broadcasted_iota(jnp.int32, (72, 128), 1)
    got = []
    for ref in (above, below):
        body = ref[...].astype(F32)
        number = jnp.sum(jnp.where(slot == lane, body[72:73, :128], 0.0), axis=1, keepdims=True)
        got.append((body[:72], number))
    blocks = []
    for b in range(9):
        total, number = sums[b * 32 : (b + 1) * 32], count[b * 32 : (b + 1) * 32]
        at = slice(b * 8, (b + 1) * 8)
        total = jnp.concatenate([total[:8] + got[0][0][at], total[8:24], total[24:] + got[1][0][at]], axis=0)
        number = jnp.concatenate([number[:8] + got[0][1][at], number[8:24], number[24:] + got[1][1][at]], axis=0)
        if b in (0, 8):
            shift = 2 if b == 0 else 30
            total = total + pltpu.roll(total, shift, 0)
            number = number + pltpu.roll(number, shift, 0)
        blocks.append((total / jnp.maximum(number[:, :1], 1.0)).astype(BF))
    out[...] = dot(back[...], jnp.concatenate(blocks, axis=0)).astype(BF)


def whole(shape):
    return pl.BlockSpec(shape, lambda *_: (0,) * len(shape))


def call(kernel, outs, args, specs=None, out_specs=None, grid=(1,), scratch=(), cost=(1e9, 4e6)):
    specs = specs or {}
    in_specs = [specs.get(i) or whole(a.shape) for i, a in enumerate(args)]
    out_specs = out_specs or [whole(o.shape) for o in outs]
    return pl.pallas_call(
        kernel,
        out_shape=outs,
        grid=grid,
        in_specs=in_specs,
        out_specs=out_specs,
        scratch_shapes=scratch,
        compiler_params=pltpu.CompilerParams(vmem_limit_bytes=VMEM, dimension_semantics=("arbitrary",) * len(grid)),
        cost_estimate=pl.CostEstimate(flops=int(cost[0]), bytes_accessed=int(cost[1]), transcendentals=0),
    )(*args)


def shape(*dims, dtype=BF):
    return jax.ShapeDtypeStruct(dims, dtype)


def local(latent, control, valid, radius, modulation, w_qkv, w_out):
    t = {k: jnp.asarray(v) for k, v in tables().items()}
    size_r, size_c = lax.axis_size("trow"), lax.axis_size("tcol")
    later_r = [(i, i + 1) for i in range(size_r - 1)]
    sooner_r = [(i + 1, i) for i in range(size_r - 1)]
    later_c = [(i, i + 1) for i in range(size_c - 1)]
    sooner_c = [(i + 1, i) for i in range(size_c - 1)]

    x = latent.reshape(256, D)
    control = control.reshape(4, TILE_TOK, D)
    valid = valid.reshape(4, TILE_TOK)
    above = lax.ppermute(x[192:], "trow", later_r)
    below = lax.ppermute(x[:64], "trow", sooner_r)
    smem = pl.BlockSpec(memory_space=pltpu.SMEM)
    chunk = pl.BlockSpec((D, D), lambda i: (0, jnp.minimum(i, 2)))

    qkv_own, msg = call(
        own_kernel,
        [shape(3, 2, 224, D), shape(2, 96, D)],
        [x, control, valid, modulation, w_qkv, t["own"], t["send_own"], t["send_ctl"], t["valid_pad"]],
        specs={4: chunk},
        out_specs=[pl.BlockSpec((1, 2, 224, D), lambda i: (i, 0, 0, 0)), whole((2, 96, D))],
        grid=(3,),
        scratch=[pltpu.VMEM((448, D), BF)],
        cost=(3.6e9, 12e6),
    )
    to_west, to_east = call(
        pack_kernel, [shape(96, D), shape(96, D)], [msg, above, below, t["send_rim"]], cost=(1e8, 1e6)
    )
    west = lax.ppermute(to_east, "tcol", later_c)
    east = lax.ppermute(to_west, "tcol", sooner_c)

    qkv_rim, attn_mid = call(
        middle_kernel,
        [shape(3, 2, 112, D), shape(2, 2, 144, D)],
        [radius, above, below, valid, modulation, w_qkv, qkv_own, t["rim"], t["dist_mid"], t["key_mid"], t["query"][1:2]],
        specs={0: smem, 5: chunk},
        out_specs=[
            pl.BlockSpec((1, 2, 112, D), lambda i: (jnp.minimum(i, 2), 0, 0, 0)),
            pl.BlockSpec((1, 1, 144, D), lambda i: (jnp.maximum(i - 3, 0) // 2, jnp.maximum(i - 3, 0) % 2, 0, 0)),
        ],
        grid=(7,),
        scratch=[
            pltpu.VMEM((224, D), BF),
            pltpu.VMEM((3, 2, 112, D), BF),
            pltpu.VMEM((2, 2, 144, D), BF),
            pltpu.VMEM((2, 256, D), BF),
            pltpu.VMEM((2, 256, D), BF),
            pltpu.VMEM((5, 288, 256), F32),
        ],
        cost=(8e9, 14e6),
    )
    up, down, core, count = call(
        edge_kernel,
        [shape(80, D), shape(80, D), shape(2, 288, D), shape(288, 128, dtype=F32)],
        [
            radius, x, above, below, west, east, valid, modulation, w_qkv, qkv_own, qkv_rim, attn_mid, w_out, control,
            t["edge"], t["dist_side"], t["key_side"], t["query"], t["query_side"], t["x_rim"], t["put_ctl"],
        ],
        specs={0: smem, 8: chunk},
        grid=(8,),
        scratch=[
            pltpu.VMEM((576, D), BF),
            pltpu.VMEM((2, 2, 192, D), BF),
            pltpu.VMEM((2, 2, 144, D), BF),
            pltpu.VMEM((2, 2, 256, D), BF),
            pltpu.VMEM((2, 2, 256, D), BF),
            pltpu.VMEM((2, 5, 144, 256), F32),
            pltpu.VMEM((2, 144, 128), F32),
            pltpu.VMEM((2, 2, 144, D), BF),
        ],
        cost=(1e10, 16e6),
    )
    got_below = lax.ppermute(up, "trow", sooner_r)
    got_above = lax.ppermute(down, "trow", later_r)
    (sums,) = call(
        core_kernel,
        [shape(288, D, dtype=F32)],
        [core, w_out, modulation, x, control, valid, west, east, count, t["x_core"], t["query"], t["put_ctl"]],
        cost=(2e9, 8e6),
    )
    (out,) = call(final_kernel, [shape(256, D)], [sums, count, got_above, got_below, t["back"]], cost=(2e8, 3e6))
    return out.reshape(CORE, 32, D)


def solution(mesh):
    placed = (
        P("trow", "tcol", None),
        P("trow", "tcol", None, None),
        P("trow", "tcol", None),
        P(),
        P(),
        P(),
        P(),
    )
    return jax.shard_map(
        local, mesh=mesh, in_specs=placed, out_specs=P("trow", "tcol", None), check_vma=False
    )
```

```python
import functools

import jax
import jax.numpy as jnp
import numpy as np
from jax import lax
from jax.experimental import pallas as pl
from jax.experimental.pallas import tpu as pltpu
from jax.sharding import PartitionSpec as P

D = 1152
HEADS = 16
HEAD_DIM = 72
CORE = 8
MARGIN = 2
SIDE = 12
TILE_TOK = 144
GUIDE = 4.5
REACH = 5
FAR = 99.0
BF = jnp.bfloat16
F32 = jnp.float32
EXP_SCALE = float(np.log2(np.e) / np.sqrt(72.0))
VMEM = 28 * 1024 * 1024

JR = np.array([j // 4 if j < 32 else (j - 40) // 4 if j < 40 else 8 + (j - 40) // 4 for j in range(48)])
JC = np.arange(48) % 4
FIRST = (-1, 1, 3, 4, 6)
CUTS = (0, 126, 252, 324, 450, 576)
KEYS = 192


def one_hot(rows, depth):
    hot = np.zeros((len(rows), depth), np.float32)
    for i, src in enumerate(rows):
        if src is not None:
            hot[i, src] = 1.0
    return hot


def source(row, col):
    if col < 0:
        return 384 + (row + 2) * REACH + col + REACH if col >= -REACH else None
    if col >= 32:
        return 480 + (row + 2) * REACH + col - 32 if col < 32 + REACH else None
    return natural(row, col)


def natural(row, col):
    if row < 0:
        return 256 + (row + 2) * 32 + col
    if row >= 8:
        return 320 + (row - 8) * 32 + col
    return row * 32 + col


def block_tokens(block):
    return [(int(r), int(4 * block - 2 + c)) for r, c in zip(JR, JC)]


def unit_queries(unit):
    entries = [(-1, 0), (-1, 1)]
    for t in range(4):
        entries += [(t, c) for c in range(max(8 * t - 2, 0), min(8 * t + 10, 32))]
    entries += [(4, 30), (4, 31)]
    flat = [(t, r, c) for t, c in entries for r in range(-2, 10)][CUTS[unit] : CUTS[unit + 1]]
    return flat + [None] * (128 - len(flat))


def unit_keys(unit):
    return [p for b in range(FIRST[unit], FIRST[unit] + 4) for p in block_tokens(b)]


def tile_token(tile, row, col):
    r, c = row + 2, col - 8 * tile + 2
    return r * SIDE + c if 0 <= r < SIDE and 0 <= c < SIDE else None


def distances(unit):
    dist = np.full((KEYS, 128), FAR, np.float32)
    for i, query in enumerate(unit_queries(unit)):
        for k, key in enumerate(unit_keys(unit)):
            if query is not None and -REACH <= key[1] < 32 + REACH and tile_token(query[0], *key) is not None:
                dist[k, i] = max(abs(query[1] - key[0]), abs(query[2] - key[1]))
    return dist


@functools.cache
def tables():
    bf = lambda a: np.asarray(a, jnp.bfloat16)
    t = {}
    t["own"] = bf(one_hot([source(*p) for b in range(1, 8) for p in block_tokens(b)[:32]], 256))
    rim = one_hot([source(*p) for b in range(1, 8) for p in block_tokens(b)[32:]], 384)
    queries = [[None if q is None else source(*q[1:]) for q in unit_queries(u)] for u in range(5)]
    middle = np.concatenate([rim, one_hot(queries[1] + queries[2] + queries[3], 384)])
    t["middle"] = bf(middle)
    edge = one_hot([source(*p) for b in (-1, 0, 8, 9) for p in block_tokens(b)], 576)
    t["edge"] = bf(np.concatenate([edge, one_hot(queries[0] + queries[4], 576)]))
    t["dist"] = bf(np.stack([distances(u) for u in range(5)]))
    t["key"] = bf(
        np.stack([[one_hot([tile_token(u + k, *p) for p in unit_keys(u)], TILE_TOK) for k in (-1, 0)] for u in range(5)])
    )
    slot = np.zeros((5, 2, TILE_TOK, 128), np.float32)
    comb = np.zeros((5, 384, 128), np.float32)
    second = np.zeros((5, 1, 128), np.float32)
    for u in range(5):
        for i, q in enumerate(unit_queries(u)):
            if q is not None:
                which = q[0] - u + 1
                assert which in (0, 1)
                slot[u, which, tile_token(*q), i] = 1.0
                second[u, 0, i] = which
                comb[u, natural(*q[1:]), i] = 1.0
    t["slot"], t["second"] = bf(slot), second
    t["comb_core"], t["comb_rim"] = bf(comb[:, :256]), bf(comb[:, 256:])
    send = np.zeros((2, 64, 384), np.float32)
    send_ctl = np.zeros((2, 32, TILE_TOK), np.float32)
    put = np.zeros((2, 384, 32), np.float32)
    for r in range(SIDE):
        for k in range(REACH):
            send[0, r * REACH + k, source(r - 2, k)] = 1.0
            send[1, r * REACH + k, source(r - 2, 32 - REACH + k)] = 1.0
        for k in range(2):
            send_ctl[0, r * 2 + k, r * SIDE + k] = 1.0
            send_ctl[1, r * 2 + k, r * SIDE + 10 + k] = 1.0
            put[0, natural(r - 2, k), r * 2 + k] = 1.0
            put[1, natural(r - 2, 30 + k), r * 2 + k] = 1.0
    t["send_own"], t["send_rim"], t["send_ctl"] = bf(send[:, :, :256]), bf(send[:, :, 256:]), bf(send_ctl)
    t["put_core"], t["put_rim"] = bf(put[:, :256]), bf(put[:, 256:])
    t["valid_pad"] = bf(np.eye(TILE_TOK, 256))
    ctl = np.zeros((4, 384, TILE_TOK), np.float32)
    for tile in range(4):
        for r in range(-2, 10):
            for c in range(max(8 * tile - 2, 0), min(8 * tile + 10, 32)):
                ctl[tile, natural(r, c), tile_token(tile, r, c)] = 1.0
    t["ctl_core"], t["ctl_rim"] = bf(ctl[:, :256]), bf(ctl[:, 256:])
    return t


def dot(a, b):
    return jnp.dot(a, b, preferred_element_type=F32)


def dot_nt(a, b):
    return lax.dot_general(a, b, (((1,), (1,)), ((), ())), preferred_element_type=F32)


def hidden_rows(x, mod_ref):
    mean = jnp.mean(x, axis=-1, keepdims=True)
    centred = x - mean
    var = jnp.mean(centred * centred, axis=-1, keepdims=True)
    normed = centred * lax.rsqrt(var + 1e-6)
    return [(normed * (1.0 + mod_ref[g, 1:2, :]) + mod_ref[g, 0:1, :]).astype(BF) for g in (0, 1)]


def eight(row):
    return jnp.broadcast_to(row, (8, row.shape[1])).astype(BF)


def fill_bias(bias_ref, unit, dist, key_a, key_b, second, valid_a, valid_b):
    usable_a, usable_b = dot_nt(key_a, eight(valid_a))[:, :1], dot_nt(key_b, eight(valid_b))[:, :1]
    dist = dist.astype(F32)
    usable = (jnp.where(second > 0.5, usable_b, usable_a) > 0.5) | (dist == 0.0)
    dist = jnp.where(usable, dist, FAR)
    for r in range(5):
        bias_ref[unit, r] = jnp.where(dist <= r + 1.0, 0.0, -1e30)


def attend(q_ref, keys, values, bias, radius_ref, out_ref):
    lane = lax.broadcasted_iota(jnp.int32, (1, 256), 1)
    scores, probs = [], []
    for p in range(8):
        lanes = slice(128 * p, 128 * p + 256)
        q = q_ref[:, lanes]
        both = [
            q * ((lane >= 16 * p + at) & (lane < 16 * p + at + HEAD_DIM)).astype(F32).astype(BF) for at in (0, HEAD_DIM)
        ]
        scores.append(dot_nt(keys(lanes), jnp.concatenate(both, axis=0)))
    for p in range(8):
        exps, scales = [], []
        for i in (0, 1):
            s = scores[p][:, 128 * i : 128 * i + 128] + bias(radius_ref[2 * p + i] - 1)
            top = jnp.max(s, axis=0, keepdims=True)
            e = jnp.exp2((s - top) * EXP_SCALE)
            scales.append(1.0 / jnp.sum(e, axis=0, keepdims=True))
            exps.append(e)
        probs.append((jnp.concatenate(exps, axis=1).astype(BF), scales))
    for p in range(8):
        v = values(slice(128 * p, 128 * p + 256)).T[16 * p : 16 * p + 144]
        e, scales = probs[p]
        o = dot(v, e)
        o = jnp.concatenate([o[:72, :128] * scales[0], o[72:, 128:] * scales[1]], axis=0)
        out_ref[144 * p : 144 * p + 144, :] = o.astype(BF)


def inner_window(own, rim, c, g, first, count):
    def get(lanes):
        parts = []
        for i in range(count):
            parts += [own[c, g, first + i, :, lanes], rim[c, g, first + i, :, lanes]]
        return parts

    return get


def own_kernel(latent, control, valid, mod, w, own, send_own, send_ctl, valid_pad, kv, msg, hid):
    rows = hidden_rows(dot(own[...], latent[...]), mod)
    hid[:224] = rows[0]
    hid[224:] = rows[1]
    for c in (0, 1):
        out = dot(hid[...], w[:, (c + 1) * D : (c + 2) * D])
        kv[c] = out.astype(BF).reshape(2, 7, 32, D)
    rows = lax.broadcasted_iota(jnp.int32, (32, 1), 0)
    val = valid[...].astype(F32)
    for i, tile in ((0, 0), (1, 3)):
        msg[i, :64] = dot(send_own[i], latent[...]).astype(BF)
        hot = (send_ctl[i].astype(F32) * val[tile : tile + 1]).astype(BF)
        ctl = dot(hot, control[tile])
        row = dot(eight(val[tile : tile + 1]), valid_pad[...])
        msg[i, 64:, 256:] = ctl[:, 256:].astype(BF)
        msg[i, 64:, :256] = jnp.where(rows == 31, row[0:1], ctl[:, :256]).astype(BF)


def pack_kernel(msg, above, below, send_rim, west, east):
    for i, out in ((0, west), (1, east)):
        rim = dot(send_rim[i, :, :64], above[...]) + dot(send_rim[i, :, 64:], below[...])
        out[:64] = (msg[i, :64].astype(F32) + rim).astype(BF)
        out[64:] = msg[i, 64:]


def middle_kernel(radius, latent, above, below, valid, mod, w, kv_own, middle, dist, key, second, kv_rim, attn, hid, qs, bias):
    x = dot(middle[:, :256], latent[...]) + dot(middle[:, 256:320], above[...]) + dot(middle[:, 320:], below[...])
    rows = hidden_rows(x, mod)
    for g in (0, 1):
        hid[g * 112 : (g + 1) * 112] = rows[g][:112]
        hid[224 + g * 384 : 224 + (g + 1) * 384] = rows[g][112:]
    qs[...] = dot(hid[224:], w[:, :D]).astype(BF).reshape(2, 3, 128, D)
    for c in (0, 1):
        kv_rim[c] = dot(hid[:224], w[:, (c + 1) * D : (c + 2) * D]).astype(BF).reshape(2, 7, 16, D)
    val = valid[...].astype(F32)
    for u in range(3):
        fill_bias(bias, u, dist[u], key[u, 0], key[u, 1], second[u], val[u : u + 1], val[u + 1 : u + 2])

    @pl.loop(0, 6)
    def _(i):
        u, g = i // 2, i % 2
        first = u + jnp.minimum(u, 1)
        keys = inner_window(kv_own, kv_rim, 0, g, first, 4)
        values = inner_window(kv_own, kv_rim, 1, g, first, 4)
        attend(
            qs.at[g, u],
            lambda lanes: jnp.concatenate(keys(lanes), axis=0),
            lambda lanes: jnp.concatenate(values(lanes), axis=0),
            lambda r: bias[u, r],
            radius,
            attn.at[u, g],
        )


def valid_rows(valid, west, east):
    val = valid[...].astype(F32)
    side = [ref[80:96, :256].astype(F32)[15:16, :TILE_TOK] for ref in (west, east)]
    return [side[0]] + [val[t : t + 1] for t in range(4)] + [side[1]]


def gather(unit, slot, comb, rows):
    weight = dot(eight(rows[unit]), slot[unit, 0]) + dot(eight(rows[unit + 1]), slot[unit, 1])
    return comb[unit].astype(F32) * weight[:1]


def block_sums(attn_of, rows, x, w_out, mod, control, west, east, slot, comb, ctl, put):
    weights = [gather(u, slot, comb, rows) for u in range(5)]
    number = sum(jnp.sum(w, axis=1, keepdims=True) for w in weights)
    n = number.shape[0]
    attn = [sum(dot_nt(weights[u].astype(BF), attn_of(u, g)) for u in range(5)).astype(BF) for g in (0, 1)]
    proj = dot(jnp.concatenate(attn, axis=0), w_out[...])
    sums = (GUIDE * mod[0, 2:3]) * proj[:n] + ((1.0 - GUIDE) * mod[1, 2:3]) * proj[n:] + number * x
    for tile in range(4):
        sums = sums + dot((ctl[tile].astype(F32) * rows[tile + 1]).astype(BF), control[tile])
    return sums + dot(put[0], west[64:]) + dot(put[1], east[64:]), number


def edge_kernel(
    radius, latent, above, below, west, east, valid, mod, w, kv_own, kv_rim, attn_mid, w_out, control,
    edge, dist, key, second, slot, comb, ctl, put,
    up, down, attn, hid, qs, kv, bias,
):
    x = (
        dot(edge[:, :256], latent[...])
        + dot(edge[:, 256:320], above[...])
        + dot(edge[:, 320:384], below[...])
        + dot(edge[:, 384:480], west[...])
        + dot(edge[:, 480:], east[...])
    )
    normed = hidden_rows(x, mod)
    for g in (0, 1):
        hid[g * 192 : (g + 1) * 192] = normed[g][:192]
        hid[384 + g * 256 : 384 + (g + 1) * 256] = normed[g][192:]
    qs[...] = dot(hid[384:], w[:, :D]).astype(BF).reshape(2, 2, 128, D)
    for c in (0, 1):
        kv[c] = dot(hid[:384], w[:, (c + 1) * D : (c + 2) * D]).astype(BF).reshape(2, 4, 48, D)
    rows = valid_rows(valid, west, east)
    for i, u in ((0, 0), (1, 4)):
        fill_bias(bias, i, dist[i], key[i, 0], key[i, 1], second[i], rows[u], rows[u + 1])

    for i in (0, 1):

        @pl.loop(0, 2)
        def _(g):
            def window(c):
                inner = inner_window(kv_own, kv_rim, c, g, 5 * i, 2)

                def get(lanes):
                    outer = [kv[c, g, 2 * i, :, lanes], kv[c, g, 2 * i + 1, :, lanes]]
                    parts = inner(lanes) + outer if i else outer + inner(lanes)
                    return jnp.concatenate(parts, axis=0)

                return get

            attend(qs.at[g, i], window(0), window(1), lambda r: bias[i, r], radius, attn.at[i, g])

    attn_of = lambda u, g: attn[u // 4, g] if u in (0, 4) else attn_mid[u - 1, g]
    x = jnp.concatenate([above[...], below[...]], axis=0).astype(F32)
    sums, number = block_sums(attn_of, rows, x, w_out, mod, control, west, east, slot, comb, ctl, put)
    row = lax.broadcasted_iota(jnp.int32, (64, 128), 0)
    lane = lax.broadcasted_iota(jnp.int32, (64, 128), 1)
    for at, out in ((0, up), (64, down)):
        out[:64] = sums[at : at + 64].astype(BF)
        tail = jnp.sum(jnp.where(row == lane, number[at : at + 64], 0.0), axis=0, keepdims=True)
        out[64:, :128] = jnp.broadcast_to(tail, (16, 128)).astype(BF)
        out[64:, 128:] = jnp.zeros((16, D - 128), BF)


def core_kernel(
    attn_mid, attn_edge, latent, west, east, valid, mod, w_out, control, slot, comb, ctl, put, out, rest, count, done, sem
):
    rows = valid_rows(valid, west, east)
    attn_of = lambda u, g: attn_edge[u // 4, g] if u in (0, 4) else attn_mid[u - 1, g]
    sums, number = block_sums(
        attn_of, rows, latent[...].astype(F32), w_out, mod, control, west, east, slot, comb, ctl, put
    )
    done[...] = (sums[64:192] / number[64:192]).astype(BF)
    copy = pltpu.make_async_copy(done, out.at[pl.ds(64, 128)], sem)
    copy.start()
    rest[0] = sums[:64]
    rest[1] = sums[192:]
    count[0] = jnp.broadcast_to(number[:64], (64, 128))
    count[1] = jnp.broadcast_to(number[192:], (64, 128))
    copy.wait()


def final_kernel(rest, count, above, below, whole_out, out, done, sem):
    del whole_out
    row = lax.broadcasted_iota(jnp.int32, (64, 128), 0)
    lane = lax.broadcasted_iota(jnp.int32, (64, 128), 1)
    copies = []
    for i, ref in ((0, above), (1, below)):
        tail = ref[64:80, :128].astype(F32)[:1]
        number = jnp.sum(jnp.where(row == lane, tail, 0.0), axis=1, keepdims=True) + count[i][:, :1]
        done[i] = ((rest[i] + ref[:64].astype(F32)) / number).astype(BF)
        copies.append(pltpu.make_async_copy(done.at[i], out.at[pl.ds(192 * i, 64)], sem.at[i]))
        copies[i].start()
    for copy in copies:
        copy.wait()


def call(kernel, outs, args, specs=None, out_specs=None, scratch=(), cost=(1e9, 4e6), aliases=None, limit=VMEM):
    specs = specs or {}
    out_specs = out_specs or {}
    vmem = pl.BlockSpec(memory_space=pltpu.VMEM)
    return pl.pallas_call(
        kernel,
        out_shape=outs,
        in_specs=[specs.get(i, vmem) for i in range(len(args))],
        out_specs=[out_specs.get(i, vmem) for i in range(len(outs))],
        scratch_shapes=scratch,
        input_output_aliases=aliases or {},
        compiler_params=pltpu.CompilerParams(vmem_limit_bytes=limit),
        cost_estimate=pl.CostEstimate(flops=int(cost[0]), bytes_accessed=int(cost[1]), transcendentals=0),
    )(*[jnp.asarray(a) for a in args])


def shape(*dims, dtype=BF):
    return jax.ShapeDtypeStruct(dims, dtype)


def local(latent, control, valid, radius, modulation, w_qkv, w_out):
    t = tables()
    size_r, size_c = lax.axis_size("trow"), lax.axis_size("tcol")
    later_r = [(i, i + 1) for i in range(size_r - 1)]
    sooner_r = [(i + 1, i) for i in range(size_r - 1)]
    later_c = [(i, i + 1) for i in range(size_c - 1)]
    sooner_c = [(i + 1, i) for i in range(size_c - 1)]

    x = latent.reshape(256, D)
    control = control.reshape(4, TILE_TOK, D)
    valid = valid.reshape(4, TILE_TOK)
    above = lax.ppermute(x[192:], "trow", later_r)
    below = lax.ppermute(x[:64], "trow", sooner_r)
    smem = pl.BlockSpec(memory_space=pltpu.SMEM)
    hbm = pl.BlockSpec(memory_space=pl.ANY)

    kv_own, msg = call(
        own_kernel,
        [shape(2, 2, 7, 32, D), shape(2, 96, D)],
        [x, control, valid, modulation, w_qkv, t["own"], t["send_own"], t["send_ctl"], t["valid_pad"]],
        scratch=[pltpu.VMEM((448, D), BF)],
        cost=(3.6e9, 12e6),
    )
    to_west, to_east = call(
        pack_kernel, [shape(96, D), shape(96, D)], [msg, above, below, t["send_rim"]], cost=(1e8, 1e6)
    )
    west = lax.ppermute(to_east, "tcol", later_c)
    east = lax.ppermute(to_west, "tcol", sooner_c)

    mid = slice(1, 4)
    kv_rim, attn_mid = call(
        middle_kernel,
        [shape(2, 2, 7, 16, D), shape(3, 2, D, 128)],
        [
            radius, x, above, below, valid, modulation, w_qkv, kv_own,
            t["middle"], t["dist"][mid], t["key"][mid], t["second"][mid],
        ],
        specs={0: smem},
        scratch=[
            pltpu.VMEM((992, D), BF),
            pltpu.VMEM((2, 3, 128, D), BF),
            pltpu.VMEM((3, 5, KEYS, 128), F32),
        ],
        cost=(8e9, 14e6),
    )
    ends = slice(0, 5, 4)
    up, down, attn_edge = call(
        edge_kernel,
        [shape(80, D), shape(80, D), shape(2, 2, D, 128)],
        [
            radius, x, above, below, west, east, valid, modulation, w_qkv, kv_own, kv_rim, attn_mid, w_out, control,
            t["edge"], t["dist"][ends], t["key"][ends], t["second"][ends], t["slot"], t["comb_rim"], t["ctl_rim"], t["put_rim"],
        ],
        specs={0: smem},
        scratch=[
            pltpu.VMEM((896, D), BF),
            pltpu.VMEM((2, 2, 128, D), BF),
            pltpu.VMEM((2, 2, 4, 48, D), BF),
            pltpu.VMEM((2, 5, KEYS, 128), F32),
        ],
        cost=(1e10, 16e6),
    )
    got_below = lax.ppermute(up, "trow", sooner_r)
    got_above = lax.ppermute(down, "trow", later_r)
    out, rest, count = call(
        core_kernel,
        [shape(256, D), shape(2, 64, D, dtype=F32), shape(2, 64, 128, dtype=F32)],
        [
            attn_mid, attn_edge, x, west, east, valid, modulation, w_out, control,
            t["slot"], t["comb_core"], t["ctl_core"], t["put_core"],
        ],
        out_specs={0: hbm},
        scratch=[pltpu.VMEM((128, D), BF), pltpu.SemaphoreType.DMA],
        cost=(3e9, 8e6),
    )
    (out,) = call(
        final_kernel,
        [shape(256, D)],
        [rest, count, got_above, got_below, out],
        specs={4: hbm},
        out_specs={0: hbm},
        scratch=[pltpu.VMEM((2, 64, D), BF), pltpu.SemaphoreType.DMA((2,))],
        aliases={4: 0},
        cost=(2e8, 3e6),
    )
    return out.reshape(CORE, 32, D)


def solution(mesh):
    placed = (
        P("trow", "tcol", None),
        P("trow", "tcol", None, None),
        P("trow", "tcol", None),
        P(),
        P(),
        P(),
        P(),
    )
    return jax.shard_map(
        local, mesh=mesh, in_specs=placed, out_specs=P("trow", "tcol", None), check_vma=False
    )
```

```python
import functools

import jax
import jax.numpy as jnp
import numpy as np
from jax import lax
from jax.experimental import pallas as pl
from jax.experimental.pallas import tpu as pltpu
from jax.sharding import PartitionSpec as P

D = 1152
HEADS = 16
HEAD_DIM = 72
CORE = 8
MARGIN = 2
SIDE = 12
TILE_TOK = 144
GUIDE = 4.5
REACH = 5
FAR = 99.0
BF = jnp.bfloat16
F32 = jnp.float32
EXP_SCALE = float(np.log2(np.e) / np.sqrt(72.0))
VMEM = 28 * 1024 * 1024

JR = np.array([j // 4 if j < 32 else (j - 40) // 4 if j < 40 else 8 + (j - 40) // 4 for j in range(48)])
JC = np.arange(48) % 4
FIRST = (-1, 1, 3, 4, 6)
CUTS = (0, 126, 252, 324, 450, 576)
KEYS = 192


def one_hot(rows, depth):
    hot = np.zeros((len(rows), depth), np.float32)
    for i, src in enumerate(rows):
        if src is not None:
            hot[i, src] = 1.0
    return hot


def source(row, col):
    if col < 0:
        return 384 + (row + 2) * REACH + col + REACH if col >= -REACH else None
    if col >= 32:
        return 480 + (row + 2) * REACH + col - 32 if col < 32 + REACH else None
    return natural(row, col)


def natural(row, col):
    if row < 0:
        return 256 + (row + 2) * 32 + col
    if row >= 8:
        return 320 + (row - 8) * 32 + col
    return row * 32 + col


def block_tokens(block):
    return [(int(r), int(4 * block - 2 + c)) for r, c in zip(JR, JC)]


def unit_queries(unit):
    entries = [(-1, 0), (-1, 1)]
    for t in range(4):
        entries += [(t, c) for c in range(max(8 * t - 2, 0), min(8 * t + 10, 32))]
    entries += [(4, 30), (4, 31)]
    flat = [(t, r, c) for t, c in entries for r in range(-2, 10)][CUTS[unit] : CUTS[unit + 1]]
    return flat + [None] * (128 - len(flat))


def unit_keys(unit):
    return [p for b in range(FIRST[unit], FIRST[unit] + 4) for p in block_tokens(b)]


def tile_token(tile, row, col):
    r, c = row + 2, col - 8 * tile + 2
    return r * SIDE + c if 0 <= r < SIDE and 0 <= c < SIDE else None


def distances(unit):
    dist = np.full((KEYS, 128), FAR, np.float32)
    for i, query in enumerate(unit_queries(unit)):
        for k, key in enumerate(unit_keys(unit)):
            if query is not None and -REACH <= key[1] < 32 + REACH and tile_token(query[0], *key) is not None:
                dist[k, i] = max(abs(query[1] - key[0]), abs(query[2] - key[1]))
    return dist


@functools.cache
def tables():
    bf = lambda a: np.asarray(a, jnp.bfloat16)
    t = {}
    t["own"] = bf(one_hot([source(*p) for b in range(1, 8) for p in block_tokens(b)[:32]], 256))
    rim = one_hot([source(*p) for b in range(1, 8) for p in block_tokens(b)[32:]], 384)
    queries = [[None if q is None else source(*q[1:]) for q in unit_queries(u)] for u in range(5)]
    middle = np.concatenate([rim, one_hot(queries[1] + queries[2] + queries[3], 384)])
    t["middle"] = bf(middle)
    edge = one_hot([source(*p) for b in (-1, 0, 8, 9) for p in block_tokens(b)], 576)
    t["edge"] = bf(np.concatenate([edge, one_hot(queries[0] + queries[4], 576)]))
    t["dist"] = bf(np.stack([distances(u) for u in range(5)]))
    t["key"] = bf(
        np.stack([[one_hot([tile_token(u + k, *p) for p in unit_keys(u)], TILE_TOK) for k in (-1, 0)] for u in range(5)])
    )
    slot = np.zeros((5, 2, TILE_TOK, 128), np.float32)
    comb = np.zeros((5, 384, 128), np.float32)
    second = np.zeros((5, 1, 128), np.float32)
    for u in range(5):
        for i, q in enumerate(unit_queries(u)):
            if q is not None:
                which = q[0] - u + 1
                assert which in (0, 1)
                slot[u, which, tile_token(*q), i] = 1.0
                second[u, 0, i] = which
                comb[u, natural(*q[1:]), i] = 1.0
    t["slot"], t["second"] = bf(slot), second
    t["comb_core"], t["comb_rim"] = bf(comb[:, :256]), bf(comb[:, 256:])
    send = np.zeros((2, 64, 384), np.float32)
    send_ctl = np.zeros((2, 32, TILE_TOK), np.float32)
    put = np.zeros((2, 384, 32), np.float32)
    for r in range(SIDE):
        for k in range(REACH):
            send[0, r * REACH + k, source(r - 2, k)] = 1.0
            send[1, r * REACH + k, source(r - 2, 32 - REACH + k)] = 1.0
        for k in range(2):
            send_ctl[0, r * 2 + k, r * SIDE + k] = 1.0
            send_ctl[1, r * 2 + k, r * SIDE + 10 + k] = 1.0
            put[0, natural(r - 2, k), r * 2 + k] = 1.0
            put[1, natural(r - 2, 30 + k), r * 2 + k] = 1.0
    t["send_own"], t["send_rim"], t["send_ctl"] = bf(send[:, :, :256]), bf(send[:, :, 256:]), bf(send_ctl)
    t["put_core"], t["put_rim"] = bf(put[:, :256]), bf(put[:, 256:])
    t["valid_pad"] = bf(np.eye(TILE_TOK, 256))
    ctl = np.zeros((4, 384, TILE_TOK), np.float32)
    for tile in range(4):
        for r in range(-2, 10):
            for c in range(max(8 * tile - 2, 0), min(8 * tile + 10, 32)):
                ctl[tile, natural(r, c), tile_token(tile, r, c)] = 1.0
    t["ctl_core"], t["ctl_rim"] = bf(ctl[:, :256]), bf(ctl[:, 256:])
    return t


def dot(a, b):
    return jnp.dot(a, b, preferred_element_type=F32)


def dot_nt(a, b):
    return lax.dot_general(a, b, (((1,), (1,)), ((), ())), preferred_element_type=F32)


def hidden_rows(x, mod_ref):
    mean = jnp.mean(x, axis=-1, keepdims=True)
    centred = x - mean
    var = jnp.mean(centred * centred, axis=-1, keepdims=True)
    normed = centred * lax.rsqrt(var + 1e-6)
    return [(normed * (1.0 + mod_ref[1, g : g + 1, :]) + mod_ref[0, g : g + 1, :]).astype(BF) for g in (0, 1)]


def eight(row):
    return jnp.broadcast_to(row, (8, row.shape[1])).astype(BF)


def fill_bias(bias_ref, unit, dist, key_a, key_b, second, valid_a, valid_b):
    usable_a, usable_b = dot_nt(key_a, eight(valid_a))[:, :1], dot_nt(key_b, eight(valid_b))[:, :1]
    dist = dist.astype(F32)
    usable = (jnp.where(second > 0.5, usable_b, usable_a) > 0.5) | (dist == 0.0)
    dist = jnp.where(usable, dist, FAR)
    for r in range(5):
        bias_ref[unit, r] = jnp.where(dist <= r + 1.0, 0.0, -1e30)


def attend(q_ref, keys, values, bias, radius_ref, out_ref):
    lane = lax.broadcasted_iota(jnp.int32, (1, 256), 1)
    scores, probs = [], []
    for p in range(8):
        lanes = slice(128 * p, 128 * p + 256)
        q = q_ref[:, lanes]
        both = [
            q * ((lane >= 16 * p + at) & (lane < 16 * p + at + HEAD_DIM)).astype(F32).astype(BF) for at in (0, HEAD_DIM)
        ]
        scores.append(dot_nt(keys(lanes), jnp.concatenate(both, axis=0)))
    for p in range(8):
        exps, scales = [], []
        for i in (0, 1):
            s = scores[p][:, 128 * i : 128 * i + 128] + bias(radius_ref[2 * p + i] - 1)
            top = jnp.max(s, axis=0, keepdims=True)
            e = jnp.exp2((s - top) * EXP_SCALE)
            scales.append(1.0 / jnp.sum(e, axis=0, keepdims=True))
            exps.append(e)
        probs.append((jnp.concatenate(exps, axis=1).astype(BF), scales))
    for p in range(8):
        v = values(slice(128 * p, 128 * p + 256)).T[16 * p : 16 * p + 144]
        e, scales = probs[p]
        o = dot(v, e)
        o = jnp.concatenate([o[:72, :128] * scales[0], o[72:, 128:] * scales[1]], axis=0)
        out_ref[144 * p : 144 * p + 144, :] = o.astype(BF)


def inner_window(own, rim, c, g, first, count):
    def get(lanes):
        parts = []
        for i in range(count):
            parts += [own[c, g, first + i, :, lanes], rim[c, g, first + i, :, lanes]]
        return parts

    return get


def own_kernel(
    latent_h, control_h, valid_h, mod_h, w_h, own_h, send_own_h, send_ctl_h, valid_pad_h,
    kv, msg, w, latent, control, valid, mod, own, send_own, send_ctl, valid_pad, hid, sem,
):
    pairs = [
        (latent_h, latent),
        (own_h, own),
        (mod_h, mod),
        (w_h.at[:, pl.ds(D, D)], w.at[:, pl.ds(D, D)]),
        (w_h.at[:, pl.ds(2 * D, D)], w.at[:, pl.ds(2 * D, D)]),
        (control_h.at[pl.ds(0, 1)], control.at[pl.ds(0, 1)]),
        (control_h.at[pl.ds(3, 1)], control.at[pl.ds(1, 1)]),
        (valid_h, valid),
        (send_own_h, send_own),
        (send_ctl_h, send_ctl),
        (valid_pad_h, valid_pad),
        (w_h.at[:, pl.ds(0, D)], w.at[:, pl.ds(0, D)]),
    ]
    copies = [pltpu.make_async_copy(src, dst, sem.at[i]) for i, (src, dst) in enumerate(pairs)]
    for copy in copies:
        copy.start()
    for copy in copies[:3]:
        copy.wait()
    rows = hidden_rows(dot(own[...], latent[...]), mod)
    hid[:224] = rows[0]
    hid[224:] = rows[1]
    for c in (0, 1):
        copies[3 + c].wait()
        out = dot(hid[...], w[:, (c + 1) * D : (c + 2) * D])
        kv[c] = out.astype(BF).reshape(2, 7, 32, D)
    for copy in copies[5:]:
        copy.wait()
    rows = lax.broadcasted_iota(jnp.int32, (32, 1), 0)
    val = valid[...].astype(F32)
    for i, tile, rim in ((0, 0, 2 * SIDE + 1), (1, 3, 2 * SIDE + 10)):
        msg[i, :64] = dot(send_own[i], latent[...]).astype(BF)
        own_row = val[tile : tile + 1]
        ctl = dot((send_ctl[i].astype(F32) * own_row).astype(BF), control[i])
        row = dot(eight(own_row * own_row[:, rim : rim + 1]), valid_pad[...])
        msg[i, 64:, 256:] = ctl[:, 256:].astype(BF)
        msg[i, 64:, :256] = jnp.where(rows == 31, row[0:1], ctl[:, :256]).astype(BF)


def pack_kernel(msg, above, below, send_rim, west, east):
    for i, out in ((0, west), (1, east)):
        rim = dot(send_rim[i, :, :64], above[...]) + dot(send_rim[i, :, 64:], below[...])
        out[:64] = (msg[i, :64].astype(F32) + rim).astype(BF)
        out[64:] = msg[i, 64:]


def middle_kernel(radius, latent, above, below, valid, mod, w, kv_own, middle, dist, key, second, kv_rim, attn, hid, qs, bias):
    x = dot(middle[:, :256], latent[...]) + dot(middle[:, 256:320], above[...]) + dot(middle[:, 320:], below[...])
    rows = hidden_rows(x, mod)
    for g in (0, 1):
        hid[g * 112 : (g + 1) * 112] = rows[g][:112]
        hid[224 + g * 384 : 224 + (g + 1) * 384] = rows[g][112:]
    qs[...] = dot(hid[224:], w[:, :D]).astype(BF).reshape(2, 3, 128, D)
    for c in (0, 1):
        kv_rim[c] = dot(hid[:224], w[:, (c + 1) * D : (c + 2) * D]).astype(BF).reshape(2, 7, 16, D)
    val = valid[...].astype(F32)
    for u in range(3):
        fill_bias(bias, u, dist[u], key[u, 0], key[u, 1], second[u], val[u : u + 1], val[u + 1 : u + 2])

    @pl.loop(0, 6)
    def _(i):
        u, g = i // 2, i % 2
        first = u + jnp.minimum(u, 1)
        keys = inner_window(kv_own, kv_rim, 0, g, first, 4)
        values = inner_window(kv_own, kv_rim, 1, g, first, 4)
        attend(
            qs.at[g, u],
            lambda lanes: jnp.concatenate(keys(lanes), axis=0),
            lambda lanes: jnp.concatenate(values(lanes), axis=0),
            lambda r: bias[u, r],
            radius,
            attn.at[u, g],
        )


def valid_rows(valid, west, east):
    val = valid[...].astype(F32)
    side = [ref[80:96, :256].astype(F32)[15:16, :TILE_TOK] for ref in (west, east)]
    return [side[0]] + [val[t : t + 1] for t in range(4)] + [side[1]]


def gather(unit, slot, comb, rows):
    weight = dot(eight(rows[unit]), slot[unit, 0]) + dot(eight(rows[unit + 1]), slot[unit, 1])
    return comb[unit].astype(F32) * weight[:1]


def block_sums(attn_of, rows, x, w_out, mod, control, west, east, slot, comb, ctl, put):
    weights = [gather(u, slot, comb, rows) for u in range(5)]
    number = sum(jnp.sum(w, axis=1, keepdims=True) for w in weights)
    n = number.shape[0]
    attn = [sum(dot_nt(weights[u].astype(BF), attn_of(u, g)) for u in range(5)).astype(BF) for g in (0, 1)]
    proj = dot(jnp.concatenate(attn, axis=0), w_out[...])
    sums = (GUIDE * mod[2, 0:1]) * proj[:n] + ((1.0 - GUIDE) * mod[2, 1:2]) * proj[n:] + number * x
    for tile in range(4):
        sums = sums + dot((ctl[tile].astype(F32) * rows[tile + 1]).astype(BF), control[tile])
    return sums + dot(put[0], west[64:]) + dot(put[1], east[64:]), number


def edge_kernel(
    radius, latent, above, below, west, east, valid, mod, w, kv_own, kv_rim, attn_mid, w_out, control,
    edge, dist, key, second, slot, comb, ctl, put,
    up, down, attn, hid, qs, kv, bias,
):
    x = (
        dot(edge[:, :256], latent[...])
        + dot(edge[:, 256:320], above[...])
        + dot(edge[:, 320:384], below[...])
        + dot(edge[:, 384:480], west[...])
        + dot(edge[:, 480:], east[...])
    )
    normed = hidden_rows(x, mod)
    for g in (0, 1):
        hid[g * 192 : (g + 1) * 192] = normed[g][:192]
        hid[384 + g * 256 : 384 + (g + 1) * 256] = normed[g][192:]
    qs[...] = dot(hid[384:], w[:, :D]).astype(BF).reshape(2, 2, 128, D)
    for c in (0, 1):
        kv[c] = dot(hid[:384], w[:, (c + 1) * D : (c + 2) * D]).astype(BF).reshape(2, 4, 48, D)
    rows = valid_rows(valid, west, east)
    for i, u in ((0, 0), (1, 4)):
        fill_bias(bias, i, dist[i], key[i, 0], key[i, 1], second[i], rows[u], rows[u + 1])

    for i in (0, 1):

        @pl.loop(0, 2)
        def _(g):
            def window(c):
                inner = inner_window(kv_own, kv_rim, c, g, 5 * i, 2)

                def get(lanes):
                    outer = [kv[c, g, 2 * i, :, lanes], kv[c, g, 2 * i + 1, :, lanes]]
                    parts = inner(lanes) + outer if i else outer + inner(lanes)
                    return jnp.concatenate(parts, axis=0)

                return get

            attend(qs.at[g, i], window(0), window(1), lambda r: bias[i, r], radius, attn.at[i, g])

    attn_of = lambda u, g: attn[u // 4, g] if u in (0, 4) else attn_mid[u - 1, g]
    x = jnp.concatenate([above[...], below[...]], axis=0).astype(F32)
    sums, number = block_sums(attn_of, rows, x, w_out, mod, control, west, east, slot, comb, ctl, put)
    row = lax.broadcasted_iota(jnp.int32, (64, 128), 0)
    lane = lax.broadcasted_iota(jnp.int32, (64, 128), 1)
    for at, out in ((0, up), (64, down)):
        out[:64] = sums[at : at + 64].astype(BF)
        tail = jnp.sum(jnp.where(row == lane, number[at : at + 64], 0.0), axis=0, keepdims=True)
        out[64:, :128] = jnp.broadcast_to(tail, (16, 128)).astype(BF)
        out[64:, 128:] = jnp.zeros((16, D - 128), BF)


def core_kernel(
    attn_mid, attn_edge, latent, west, east, valid, mod, w_out, control, slot, comb, ctl, put, out, rest, count, done, sem
):
    rows = valid_rows(valid, west, east)
    attn_of = lambda u, g: attn_edge[u // 4, g] if u in (0, 4) else attn_mid[u - 1, g]
    sums, number = block_sums(
        attn_of, rows, latent[...].astype(F32), w_out, mod, control, west, east, slot, comb, ctl, put
    )
    done[...] = (sums[64:192] / number[64:192]).astype(BF)
    copy = pltpu.make_async_copy(done, out.at[pl.ds(64, 128)], sem)
    copy.start()
    rest[0] = sums[:64]
    rest[1] = sums[192:]
    count[0] = jnp.broadcast_to(number[:64], (64, 128))
    count[1] = jnp.broadcast_to(number[192:], (64, 128))
    copy.wait()


def final_kernel(rest, count, above, below, whole_out, out, done, sem):
    del whole_out
    row = lax.broadcasted_iota(jnp.int32, (64, 128), 0)
    lane = lax.broadcasted_iota(jnp.int32, (64, 128), 1)
    copies = []
    for i, ref in ((0, above), (1, below)):
        tail = ref[64:80, :128].astype(F32)[:1]
        number = jnp.sum(jnp.where(row == lane, tail, 0.0), axis=1, keepdims=True) + count[i][:, :1]
        done[i] = ((rest[i] + ref[:64].astype(F32)) / number).astype(BF)
        copies.append(pltpu.make_async_copy(done.at[i], out.at[pl.ds(192 * i, 64)], sem.at[i]))
        copies[i].start()
    for copy in copies:
        copy.wait()


def call(kernel, outs, args, specs=None, out_specs=None, scratch=(), cost=(1e9, 4e6), aliases=None, limit=VMEM):
    specs = specs or {}
    out_specs = out_specs or {}
    vmem = pl.BlockSpec(memory_space=pltpu.VMEM)
    return pl.pallas_call(
        kernel,
        out_shape=outs,
        in_specs=[specs.get(i, vmem) for i in range(len(args))],
        out_specs=[out_specs.get(i, vmem) for i in range(len(outs))],
        scratch_shapes=scratch,
        input_output_aliases=aliases or {},
        compiler_params=pltpu.CompilerParams(vmem_limit_bytes=limit),
        cost_estimate=pl.CostEstimate(flops=int(cost[0]), bytes_accessed=int(cost[1]), transcendentals=0),
    )(*[jnp.asarray(a) for a in args])


def shape(*dims, dtype=BF):
    return jax.ShapeDtypeStruct(dims, dtype)


def local(latent, control, valid, radius, modulation, w_qkv, w_out):
    t = tables()
    size_r, size_c = lax.axis_size("trow"), lax.axis_size("tcol")
    later_r = [(i, (i + 1) % size_r) for i in range(size_r)]
    sooner_r = [((i + 1) % size_r, i) for i in range(size_r)]
    later_c = [(i, (i + 1) % size_c) for i in range(size_c)]
    sooner_c = [((i + 1) % size_c, i) for i in range(size_c)]

    x = latent.reshape(256, D)
    control = control.reshape(4, TILE_TOK, D)
    valid = valid.reshape(4, TILE_TOK)
    above = lax.ppermute(x[192:], "trow", later_r)
    below = lax.ppermute(x[:64], "trow", sooner_r)
    smem = pl.BlockSpec(memory_space=pltpu.SMEM)
    hbm = pl.BlockSpec(memory_space=pl.ANY)

    mod = modulation.transpose(1, 0, 2)
    far = lambda a: pltpu.with_memory_space_constraint(jnp.asarray(a), pltpu.MemorySpace.HBM)
    first = [x, control, valid, mod, w_qkv, t["own"], t["send_own"], t["send_ctl"], t["valid_pad"]]
    staged = [(256, D, BF), (2, TILE_TOK, D, BF), (4, TILE_TOK, jnp.int32), (3, 2, D, F32)]
    staged += [t[k].shape + (BF,) for k in ("own", "send_own", "send_ctl", "valid_pad")]
    kv_own, msg, w = call(
        own_kernel,
        [shape(2, 2, 7, 32, D), shape(2, 96, D), shape(D, 3 * D)],
        [far(a) for a in first],
        specs={i: hbm for i in range(len(first))},
        scratch=[pltpu.VMEM(s[:-1], s[-1]) for s in staged]
        + [pltpu.VMEM((448, D), BF), pltpu.SemaphoreType.DMA((12,))],
        cost=(3.6e9, 12e6),
    )
    to_west, to_east = call(
        pack_kernel, [shape(96, D), shape(96, D)], [msg, above, below, t["send_rim"]], cost=(1e8, 1e6)
    )
    west = lax.ppermute(to_east, "tcol", later_c)
    east = lax.ppermute(to_west, "tcol", sooner_c)

    mid = slice(1, 4)
    kv_rim, attn_mid = call(
        middle_kernel,
        [shape(2, 2, 7, 16, D), shape(3, 2, D, 128)],
        [
            radius, x, above, below, valid, mod, w, kv_own,
            t["middle"], t["dist"][mid], t["key"][mid], t["second"][mid],
        ],
        specs={0: smem},
        scratch=[
            pltpu.VMEM((992, D), BF),
            pltpu.VMEM((2, 3, 128, D), BF),
            pltpu.VMEM((3, 5, KEYS, 128), F32),
        ],
        cost=(8e9, 14e6),
    )
    ends = slice(0, 5, 4)
    up, down, attn_edge = call(
        edge_kernel,
        [shape(80, D), shape(80, D), shape(2, 2, D, 128)],
        [
            radius, x, above, below, west, east, valid, mod, w, kv_own, kv_rim, attn_mid, w_out, control,
            t["edge"], t["dist"][ends], t["key"][ends], t["second"][ends], t["slot"], t["comb_rim"], t["ctl_rim"], t["put_rim"],
        ],
        specs={0: smem},
        scratch=[
            pltpu.VMEM((896, D), BF),
            pltpu.VMEM((2, 2, 128, D), BF),
            pltpu.VMEM((2, 2, 4, 48, D), BF),
            pltpu.VMEM((2, 5, KEYS, 128), F32),
        ],
        cost=(1e10, 16e6),
    )
    got_below = lax.ppermute(up, "trow", sooner_r)
    got_above = lax.ppermute(down, "trow", later_r)
    out, rest, count = call(
        core_kernel,
        [shape(256, D), shape(2, 64, D, dtype=F32), shape(2, 64, 128, dtype=F32)],
        [
            attn_mid, attn_edge, x, west, east, valid, mod, w_out, control,
            t["slot"], t["comb_core"], t["ctl_core"], t["put_core"],
        ],
        out_specs={0: hbm},
        scratch=[pltpu.VMEM((128, D), BF), pltpu.SemaphoreType.DMA],
        cost=(3e9, 8e6),
    )
    (out,) = call(
        final_kernel,
        [shape(256, D)],
        [rest, count, got_above, got_below, out],
        specs={4: hbm},
        out_specs={0: hbm},
        scratch=[pltpu.VMEM((2, 64, D), BF), pltpu.SemaphoreType.DMA((2,))],
        aliases={4: 0},
        cost=(2e8, 3e6),
    )
    return out.reshape(CORE, 32, D)


def solution(mesh):
    placed = (
        P("trow", "tcol", None),
        P("trow", "tcol", None, None),
        P("trow", "tcol", None),
        P(),
        P(),
        P(),
        P(),
    )
    return jax.shard_map(
        local, mesh=mesh, in_specs=placed, out_specs=P("trow", "tcol", None), check_vma=False
    )
```

```python
import functools

import jax
import jax.numpy as jnp
import numpy as np
from jax import lax
from jax.experimental import pallas as pl
from jax.experimental.pallas import tpu as pltpu
from jax.sharding import PartitionSpec as P

D = 1152
HEADS = 16
HEAD_DIM = 72
CORE = 8
MARGIN = 2
SIDE = 12
TILE_TOK = 144
GUIDE = 4.5
REACH = 5
FAR = 99.0
BF = jnp.bfloat16
F32 = jnp.float32
EXP_SCALE = float(np.log2(np.e) / np.sqrt(72.0))
VMEM = 28 * 1024 * 1024

JR = np.array([j // 4 if j < 32 else (j - 40) // 4 if j < 40 else 8 + (j - 40) // 4 for j in range(48)])
JC = np.arange(48) % 4
FIRST = (-1, 1, 3, 4, 6)
CUTS = (0, 126, 252, 324, 450, 576)
KEYS = 192
GROUP = 4


def one_hot(rows, depth):
    hot = np.zeros((len(rows), depth), np.float32)
    for i, src in enumerate(rows):
        if src is not None:
            hot[i, src] = 1.0
    return hot


def source(row, col):
    if col < 0:
        return 384 + (row + 2) * REACH + col + REACH if col >= -REACH else None
    if col >= 32:
        return 480 + (row + 2) * REACH + col - 32 if col < 32 + REACH else None
    return natural(row, col)


def natural(row, col):
    if row < 0:
        return 256 + (row + 2) * 32 + col
    if row >= 8:
        return 320 + (row - 8) * 32 + col
    return row * 32 + col


def block_tokens(block):
    return [(int(r), int(4 * block - 2 + c)) for r, c in zip(JR, JC)]


def unit_queries(unit):
    entries = [(-1, 0), (-1, 1)]
    for t in range(4):
        entries += [(t, c) for c in range(max(8 * t - 2, 0), min(8 * t + 10, 32))]
    entries += [(4, 30), (4, 31)]
    flat = [(t, r, c) for t, c in entries for r in range(-2, 10)][CUTS[unit] : CUTS[unit + 1]]
    return flat + [None] * (128 - len(flat))


def unit_keys(unit):
    return [p for b in range(FIRST[unit], FIRST[unit] + 4) for p in block_tokens(b)]


def tile_token(tile, row, col):
    r, c = row + 2, col - 8 * tile + 2
    return r * SIDE + c if 0 <= r < SIDE and 0 <= c < SIDE else None


def distances(unit):
    dist = np.full((KEYS, 128), FAR, np.float32)
    for i, query in enumerate(unit_queries(unit)):
        for k, key in enumerate(unit_keys(unit)):
            if query is not None and -REACH <= key[1] < 32 + REACH and tile_token(query[0], *key) is not None:
                dist[k, i] = max(abs(query[1] - key[0]), abs(query[2] - key[1]))
    return dist


@functools.cache
def tables():
    bf = lambda a: np.asarray(a, jnp.bfloat16)
    t = {}
    t["own"] = bf(one_hot([source(*p) for b in range(1, 8) for p in block_tokens(b)[:32]], 256))
    rim = one_hot([source(*p) for b in range(1, 8) for p in block_tokens(b)[32:]], 384)
    queries = [[None if q is None else source(*q[1:]) for q in unit_queries(u)] for u in range(5)]
    middle = np.concatenate([rim, one_hot(queries[1] + queries[2] + queries[3], 384)])
    t["middle"] = bf(middle)
    edge = one_hot([source(*p) for b in (-1, 0, 8, 9) for p in block_tokens(b)], 576)
    t["edge"] = bf(np.concatenate([edge, one_hot(queries[0] + queries[4], 576)]))
    t["dist"] = bf(np.stack([distances(u) for u in range(5)]))
    t["key"] = bf(
        np.stack([[one_hot([tile_token(u + k, *p) for p in unit_keys(u)], TILE_TOK) for k in (-1, 0)] for u in range(5)])
    )
    slot = np.zeros((5, 2, TILE_TOK, 128), np.float32)
    comb = np.zeros((5, 384, 128), np.float32)
    second = np.zeros((5, 1, 128), np.float32)
    for u in range(5):
        for i, q in enumerate(unit_queries(u)):
            if q is not None:
                which = q[0] - u + 1
                assert which in (0, 1)
                slot[u, which, tile_token(*q), i] = 1.0
                second[u, 0, i] = which
                comb[u, natural(*q[1:]), i] = 1.0
    t["slot"], t["second"] = bf(slot), second
    t["comb_core"], t["comb_rim"] = bf(comb[:, :256]), bf(comb[:, 256:])
    send = np.zeros((2, 64, 384), np.float32)
    send_ctl = np.zeros((2, 32, TILE_TOK), np.float32)
    put = np.zeros((2, 384, 32), np.float32)
    for r in range(SIDE):
        for k in range(REACH):
            send[0, r * REACH + k, source(r - 2, k)] = 1.0
            send[1, r * REACH + k, source(r - 2, 32 - REACH + k)] = 1.0
        for k in range(2):
            send_ctl[0, r * 2 + k, r * SIDE + k] = 1.0
            send_ctl[1, r * 2 + k, r * SIDE + 10 + k] = 1.0
            put[0, natural(r - 2, k), r * 2 + k] = 1.0
            put[1, natural(r - 2, 30 + k), r * 2 + k] = 1.0
    t["send_own"], t["send_rim"], t["send_ctl"] = bf(send[:, :, :256]), bf(send[:, :, 256:]), bf(send_ctl)
    t["put_core"], t["put_rim"] = bf(put[:, :256]), bf(put[:, 256:])
    t["valid_pad"] = bf(np.eye(TILE_TOK, 256))
    ctl = np.zeros((4, 384, TILE_TOK), np.float32)
    for tile in range(4):
        for r in range(-2, 10):
            for c in range(max(8 * tile - 2, 0), min(8 * tile + 10, 32)):
                ctl[tile, natural(r, c), tile_token(tile, r, c)] = 1.0
    t["ctl_core"], t["ctl_rim"] = bf(ctl[:, :256]), bf(ctl[:, 256:])
    return t


def dot(a, b):
    return jnp.dot(a, b, preferred_element_type=F32)


def dot_nt(a, b):
    return lax.dot_general(a, b, (((1,), (1,)), ((), ())), preferred_element_type=F32)


def hidden_rows(x, mod_ref):
    mean = jnp.mean(x, axis=-1, keepdims=True)
    centred = x - mean
    var = jnp.mean(centred * centred, axis=-1, keepdims=True)
    normed = centred * lax.rsqrt(var + 1e-6)
    return [(normed * (1.0 + mod_ref[1, g : g + 1, :]) + mod_ref[0, g : g + 1, :]).astype(BF) for g in (0, 1)]


def eight(row):
    return jnp.broadcast_to(row, (8, row.shape[1])).astype(BF)


def fill_bias(bias_ref, unit, dist, key_a, key_b, second, valid_a, valid_b):
    usable_a, usable_b = dot_nt(key_a, eight(valid_a))[:, :1], dot_nt(key_b, eight(valid_b))[:, :1]
    dist = dist.astype(F32)
    usable = (jnp.where(second > 0.5, usable_b, usable_a) > 0.5) | (dist == 0.0)
    dist = jnp.where(usable, dist, FAR)
    for r in range(5):
        bias_ref[unit, r] = jnp.where(dist <= r + 1.0, 0.0, -1e30)


def attend(queries, keys, values, bias, radius_ref, put):
    lane = lax.broadcasted_iota(jnp.int32, (1, 256), 1)

    def score(g, p):
        lanes = slice(128 * p, 128 * p + 256)
        q = queries(g, lanes)
        both = [
            q * ((lane >= 16 * p + at) & (lane < 16 * p + at + HEAD_DIM)).astype(F32).astype(BF) for at in (0, HEAD_DIM)
        ]
        return dot_nt(keys(g, lanes), jnp.concatenate(both, axis=0))

    def soften(p, scores):
        exps, scales = [], []
        for i in (0, 1):
            s = scores[:, 128 * i : 128 * i + 128] + bias(radius_ref[2 * p + i] - 1)
            top = jnp.max(s, axis=0, keepdims=True)
            e = jnp.exp2((s - top) * EXP_SCALE)
            scales.append(1.0 / jnp.sum(e, axis=0, keepdims=True))
            exps.append(e)
        return jnp.concatenate(exps, axis=1).astype(BF), scales

    def collect(g, p, e, scales):
        v = values(g, slice(128 * p, 128 * p + 256)).T[16 * p : 16 * p + 144]
        o = dot(v, e)
        o = jnp.concatenate([o[:72, :128] * scales[0], o[72:, 128:] * scales[1]], axis=0)
        put(g, slice(144 * p, 144 * p + 144), o.astype(BF))

    items = [(g, p) for g in (0, 1) for p in range(8)]
    scores = {k: score(*items[k]) for k in range(GROUP)}
    probs = {}
    for k in range(len(items) + GROUP):
        if k + GROUP < len(items):
            scores[k + GROUP] = score(*items[k + GROUP])
        if k < len(items):
            probs[k] = soften(items[k][1], scores.pop(k))
        if k >= GROUP:
            collect(*items[k - GROUP], *probs.pop(k - GROUP))


def inner_window(own, rim, c, first, count):
    def get(g, lanes):
        parts = []
        for i in range(count):
            parts += [own[c, g, first + i, :, lanes], rim[c, g, first + i, :, lanes]]
        return parts

    return get


def own_kernel(
    latent_h, control_h, valid_h, mod_h, w_h, own_h, send_own_h, send_ctl_h, valid_pad_h,
    kv, msg, w, latent, control, valid, mod, own, send_own, send_ctl, valid_pad, hid, sem,
):
    pairs = [
        (latent_h, latent),
        (own_h, own),
        (mod_h, mod),
        (w_h.at[:, pl.ds(D, D)], w.at[:, pl.ds(D, D)]),
        (w_h.at[:, pl.ds(2 * D, D)], w.at[:, pl.ds(2 * D, D)]),
        (control_h.at[pl.ds(0, 1)], control.at[pl.ds(0, 1)]),
        (control_h.at[pl.ds(3, 1)], control.at[pl.ds(1, 1)]),
        (valid_h, valid),
        (send_own_h, send_own),
        (send_ctl_h, send_ctl),
        (valid_pad_h, valid_pad),
        (w_h.at[:, pl.ds(0, D)], w.at[:, pl.ds(0, D)]),
    ]
    copies = [pltpu.make_async_copy(src, dst, sem.at[i]) for i, (src, dst) in enumerate(pairs)]
    for copy in copies:
        copy.start()
    for copy in copies[:3]:
        copy.wait()
    rows = hidden_rows(dot(own[...], latent[...]), mod)
    hid[:224] = rows[0]
    hid[224:] = rows[1]
    for c in (0, 1):
        copies[3 + c].wait()
        out = dot(hid[...], w[:, (c + 1) * D : (c + 2) * D])
        kv[c] = out.astype(BF).reshape(2, 7, 32, D)
    for copy in copies[5:]:
        copy.wait()
    rows = lax.broadcasted_iota(jnp.int32, (32, 1), 0)
    val = valid[...].astype(F32)
    for i, tile, rim in ((0, 0, 2 * SIDE + 1), (1, 3, 2 * SIDE + 10)):
        msg[i, :64] = dot(send_own[i], latent[...]).astype(BF)
        own_row = val[tile : tile + 1]
        ctl = dot((send_ctl[i].astype(F32) * own_row).astype(BF), control[i])
        row = dot(eight(own_row * own_row[:, rim : rim + 1]), valid_pad[...])
        msg[i, 64:, 256:] = ctl[:, 256:].astype(BF)
        msg[i, 64:, :256] = jnp.where(rows == 31, row[0:1], ctl[:, :256]).astype(BF)


def pack_kernel(msg, above, below, send_rim, west, east):
    for i, out in ((0, west), (1, east)):
        rim = dot(send_rim[i, :, :64], above[...]) + dot(send_rim[i, :, 64:], below[...])
        out[:64] = (msg[i, :64].astype(F32) + rim).astype(BF)
        out[64:] = msg[i, 64:]


def middle_kernel(
    radius, latent, above, below, valid, mod, w, kv_own, middle, dist, key, second, kv_rim, attn, near, hid, qs, bias
):
    near[:256] = latent[...]
    near[256:320] = above[...]
    near[320:] = below[...]
    rows = hidden_rows(dot(middle[...], near[...]), mod)
    for g in (0, 1):
        hid[g * 112 : (g + 1) * 112] = rows[g][:112]
        hid[224 + g * 384 : 224 + (g + 1) * 384] = rows[g][112:]
    qs[...] = dot(hid[224:], w[:, :D]).astype(BF).reshape(2, 3, 128, D)
    for c in (0, 1):
        kv_rim[c] = dot(hid[:224], w[:, (c + 1) * D : (c + 2) * D]).astype(BF).reshape(2, 7, 16, D)
    val = valid[...].astype(F32)
    for u in range(3):
        fill_bias(bias, u, dist[u], key[u, 0], key[u, 1], second[u], val[u : u + 1], val[u + 1 : u + 2])

    @pl.loop(0, 3)
    def _(u):
        first = u + jnp.minimum(u, 1)
        keys = inner_window(kv_own, kv_rim, 0, first, 4)
        values = inner_window(kv_own, kv_rim, 1, first, 4)

        def put(g, rows, o):
            attn[g, rows, pl.ds(pl.multiple_of(u * 128, 128), 128)] = o

        attend(
            lambda g, lanes: qs[g, u, :, lanes],
            lambda g, lanes: jnp.concatenate(keys(g, lanes), axis=0),
            lambda g, lanes: jnp.concatenate(values(g, lanes), axis=0),
            lambda r: bias[u, r],
            radius,
            put,
        )


def valid_rows(valid, west, east):
    val = valid[...].astype(F32)
    side = [ref[80:96, :256].astype(F32)[15:16, :TILE_TOK] for ref in (west, east)]
    return [side[0]] + [val[t : t + 1] for t in range(4)] + [side[1]]


def gather(unit, slot, comb, rows):
    weight = dot(eight(rows[unit]), slot[unit, 0]) + dot(eight(rows[unit + 1]), slot[unit, 1])
    return comb[unit].astype(F32) * weight[:1]


def block_sums(attn_mid, attn_edge, rows, x, w_out, mod, control, west, east, slot, comb, ctl, put):
    weights = [gather(u, slot, comb, rows) for u in range(5)]
    number = sum(jnp.sum(w, axis=1, keepdims=True) for w in weights)
    n = number.shape[0]
    inner = jnp.concatenate(weights[1:4], axis=1).astype(BF)
    outer = jnp.concatenate([weights[0], weights[4]], axis=1).astype(BF)
    attn = [(dot_nt(inner, attn_mid[g]) + dot_nt(outer, attn_edge[g])).astype(BF) for g in (0, 1)]
    proj = dot(jnp.concatenate(attn, axis=0), w_out[...])
    sums = (GUIDE * mod[2, 0:1]) * proj[:n] + ((1.0 - GUIDE) * mod[2, 1:2]) * proj[n:] + number * x
    for tile in range(4):
        sums = sums + dot((ctl[tile].astype(F32) * rows[tile + 1]).astype(BF), control[tile])
    return sums + dot(put[0], west[64:]) + dot(put[1], east[64:]), number


def edge_kernel(
    radius, latent, above, below, west, east, valid, mod, w, kv_own, kv_rim, attn_mid, w_out, control,
    edge, dist, key, second, slot, comb, ctl, put_ctl,
    up, down, attn, near, hid, qs, kv, bias,
):
    at = 0
    for ref in (latent, above, below, west, east):
        near[at : at + ref.shape[0]] = ref[...]
        at += ref.shape[0]
    x = dot(edge[...], near[...])
    normed = hidden_rows(x, mod)
    for g in (0, 1):
        hid[g * 192 : (g + 1) * 192] = normed[g][:192]
        hid[384 + g * 256 : 384 + (g + 1) * 256] = normed[g][192:]
    qs[...] = dot(hid[384:], w[:, :D]).astype(BF).reshape(2, 2, 128, D)
    for c in (0, 1):
        kv[c] = dot(hid[:384], w[:, (c + 1) * D : (c + 2) * D]).astype(BF).reshape(2, 4, 48, D)
    rows = valid_rows(valid, west, east)
    for i, u in ((0, 0), (1, 4)):
        fill_bias(bias, i, dist[i], key[i, 0], key[i, 1], second[i], rows[u], rows[u + 1])

    for i in (0, 1):

        def window(c):
            inner = inner_window(kv_own, kv_rim, c, 5 * i, 2)

            def get(g, lanes):
                outer = [kv[c, g, 2 * i, :, lanes], kv[c, g, 2 * i + 1, :, lanes]]
                parts = inner(g, lanes) + outer if i else outer + inner(g, lanes)
                return jnp.concatenate(parts, axis=0)

            return get

        def put(g, rows, o):
            attn[g, rows, 128 * i : 128 * i + 128] = o

        attend(lambda g, lanes: qs[g, i, :, lanes], window(0), window(1), lambda r: bias[i, r], radius, put)

    x = jnp.concatenate([above[...], below[...]], axis=0).astype(F32)
    sums, number = block_sums(attn_mid, attn, rows, x, w_out, mod, control, west, east, slot, comb, ctl, put_ctl)
    row = lax.broadcasted_iota(jnp.int32, (64, 128), 0)
    lane = lax.broadcasted_iota(jnp.int32, (64, 128), 1)
    for at, out in ((0, up), (64, down)):
        out[:64] = sums[at : at + 64].astype(BF)
        tail = jnp.sum(jnp.where(row == lane, number[at : at + 64], 0.0), axis=0, keepdims=True)
        out[64:, :128] = jnp.broadcast_to(tail, (16, 128)).astype(BF)
        out[64:, 128:] = jnp.zeros((16, D - 128), BF)


def core_kernel(
    attn_mid, attn_edge, latent, west, east, valid, mod, w_out, control, slot, comb, ctl, put, out, rest, count, done, sem
):
    rows = valid_rows(valid, west, east)
    sums, number = block_sums(
        attn_mid, attn_edge, rows, latent[...].astype(F32), w_out, mod, control, west, east, slot, comb, ctl, put
    )
    done[...] = (sums[64:192] / number[64:192]).astype(BF)
    copy = pltpu.make_async_copy(done, out.at[pl.ds(64, 128)], sem)
    copy.start()
    rest[0] = sums[:64]
    rest[1] = sums[192:]
    count[0] = jnp.broadcast_to(number[:64], (64, 128))
    count[1] = jnp.broadcast_to(number[192:], (64, 128))
    copy.wait()


def final_kernel(rest, count, above, below, whole_out, out, done, sem):
    del whole_out
    row = lax.broadcasted_iota(jnp.int32, (64, 128), 0)
    lane = lax.broadcasted_iota(jnp.int32, (64, 128), 1)
    copies = []
    for i, ref in ((0, above), (1, below)):
        tail = ref[64:80, :128].astype(F32)[:1]
        number = jnp.sum(jnp.where(row == lane, tail, 0.0), axis=1, keepdims=True) + count[i][:, :1]
        done[i] = ((rest[i] + ref[:64].astype(F32)) / number).astype(BF)
        copies.append(pltpu.make_async_copy(done.at[i], out.at[pl.ds(192 * i, 64)], sem.at[i]))
        copies[i].start()
    for copy in copies:
        copy.wait()


def call(kernel, outs, args, specs=None, out_specs=None, scratch=(), cost=(1e9, 4e6), aliases=None, limit=VMEM):
    specs = specs or {}
    out_specs = out_specs or {}
    vmem = pl.BlockSpec(memory_space=pltpu.VMEM)
    return pl.pallas_call(
        kernel,
        out_shape=outs,
        in_specs=[specs.get(i, vmem) for i in range(len(args))],
        out_specs=[out_specs.get(i, vmem) for i in range(len(outs))],
        scratch_shapes=scratch,
        input_output_aliases=aliases or {},
        compiler_params=pltpu.CompilerParams(vmem_limit_bytes=limit),
        cost_estimate=pl.CostEstimate(flops=int(cost[0]), bytes_accessed=int(cost[1]), transcendentals=0),
    )(*[jnp.asarray(a) for a in args])


def shape(*dims, dtype=BF):
    return jax.ShapeDtypeStruct(dims, dtype)


def local(latent, control, valid, radius, modulation, w_qkv, w_out):
    t = tables()
    size_r, size_c = lax.axis_size("trow"), lax.axis_size("tcol")
    later_r = [(i, (i + 1) % size_r) for i in range(size_r)]
    sooner_r = [((i + 1) % size_r, i) for i in range(size_r)]
    later_c = [(i, (i + 1) % size_c) for i in range(size_c)]
    sooner_c = [((i + 1) % size_c, i) for i in range(size_c)]

    x = latent.reshape(256, D)
    control = control.reshape(4, TILE_TOK, D)
    valid = valid.reshape(4, TILE_TOK)
    above = lax.ppermute(x[192:], "trow", later_r)
    below = lax.ppermute(x[:64], "trow", sooner_r)
    smem = pl.BlockSpec(memory_space=pltpu.SMEM)
    hbm = pl.BlockSpec(memory_space=pl.ANY)

    mod = modulation.transpose(1, 0, 2)
    far = lambda a: pltpu.with_memory_space_constraint(jnp.asarray(a), pltpu.MemorySpace.HBM)
    first = [x, control, valid, mod, w_qkv, t["own"], t["send_own"], t["send_ctl"], t["valid_pad"]]
    staged = [(256, D, BF), (2, TILE_TOK, D, BF), (4, TILE_TOK, jnp.int32), (3, 2, D, F32)]
    staged += [t[k].shape + (BF,) for k in ("own", "send_own", "send_ctl", "valid_pad")]
    kv_own, msg, w = call(
        own_kernel,
        [shape(2, 2, 7, 32, D), shape(2, 96, D), shape(D, 3 * D)],
        [far(a) for a in first],
        specs={i: hbm for i in range(len(first))},
        scratch=[pltpu.VMEM(s[:-1], s[-1]) for s in staged]
        + [pltpu.VMEM((448, D), BF), pltpu.SemaphoreType.DMA((12,))],
        cost=(3.6e9, 12e6),
    )
    to_west, to_east = call(
        pack_kernel, [shape(96, D), shape(96, D)], [msg, above, below, t["send_rim"]], cost=(1e8, 1e6)
    )
    west = lax.ppermute(to_east, "tcol", later_c)
    east = lax.ppermute(to_west, "tcol", sooner_c)

    mid = slice(1, 4)
    kv_rim, attn_mid = call(
        middle_kernel,
        [shape(2, 2, 7, 16, D), shape(2, D, 384)],
        [
            radius, x, above, below, valid, mod, w, kv_own,
            t["middle"], t["dist"][mid], t["key"][mid], t["second"][mid],
        ],
        specs={0: smem},
        scratch=[
            pltpu.VMEM((384, D), BF),
            pltpu.VMEM((992, D), BF),
            pltpu.VMEM((2, 3, 128, D), BF),
            pltpu.VMEM((3, 5, KEYS, 128), F32),
        ],
        cost=(8e9, 14e6),
    )
    ends = slice(0, 5, 4)
    up, down, attn_edge = call(
        edge_kernel,
        [shape(80, D), shape(80, D), shape(2, D, 256)],
        [
            radius, x, above, below, west, east, valid, mod, w, kv_own, kv_rim, attn_mid, w_out, control,
            t["edge"], t["dist"][ends], t["key"][ends], t["second"][ends], t["slot"], t["comb_rim"], t["ctl_rim"], t["put_rim"],
        ],
        specs={0: smem},
        scratch=[
            pltpu.VMEM((576, D), BF),
            pltpu.VMEM((896, D), BF),
            pltpu.VMEM((2, 2, 128, D), BF),
            pltpu.VMEM((2, 2, 4, 48, D), BF),
            pltpu.VMEM((2, 5, KEYS, 128), F32),
        ],
        cost=(1e10, 16e6),
    )
    got_below = lax.ppermute(up, "trow", sooner_r)
    got_above = lax.ppermute(down, "trow", later_r)
    out, rest, count = call(
        core_kernel,
        [shape(256, D), shape(2, 64, D, dtype=F32), shape(2, 64, 128, dtype=F32)],
        [
            attn_mid, attn_edge, x, west, east, valid, mod, w_out, control,
            t["slot"], t["comb_core"], t["ctl_core"], t["put_core"],
        ],
        out_specs={0: hbm},
        scratch=[pltpu.VMEM((128, D), BF), pltpu.SemaphoreType.DMA],
        cost=(3e9, 8e6),
    )
    (out,) = call(
        final_kernel,
        [shape(256, D)],
        [rest, count, got_above, got_below, out],
        specs={4: hbm},
        out_specs={0: hbm},
        scratch=[pltpu.VMEM((2, 64, D), BF), pltpu.SemaphoreType.DMA((2,))],
        aliases={4: 0},
        cost=(2e8, 3e6),
    )
    return out.reshape(CORE, 32, D)


def solution(mesh):
    placed = (
        P("trow", "tcol", None),
        P("trow", "tcol", None, None),
        P("trow", "tcol", None),
        P(),
        P(),
        P(),
        P(),
    )
    return jax.shard_map(
        local, mesh=mesh, in_specs=placed, out_specs=P("trow", "tcol", None), check_vma=False
    )
```

```python
import functools

import jax
import jax.numpy as jnp
import numpy as np
from jax import lax
from jax.experimental import pallas as pl
from jax.experimental.pallas import tpu as pltpu
from jax.sharding import PartitionSpec as P

D = 1152
HEADS = 16
HEAD_DIM = 72
CORE = 8
MARGIN = 2
SIDE = 12
TILE_TOK = 144
GUIDE = 4.5
REACH = 5
FAR = 99.0
BF = jnp.bfloat16
F32 = jnp.float32
EXP_SCALE = float(np.log2(np.e) / np.sqrt(72.0))
VMEM = 28 * 1024 * 1024

JR = np.array([j // 4 if j < 32 else (j - 40) // 4 if j < 40 else 8 + (j - 40) // 4 for j in range(48)])
JC = np.arange(48) % 4
FIRST = (-1, 1, 3, 4, 6)
CUTS = (0, 126, 252, 324, 450, 576)
KEYS = 192
GROUP = 4


def one_hot(rows, depth):
    hot = np.zeros((len(rows), depth), np.float32)
    for i, src in enumerate(rows):
        if src is not None:
            hot[i, src] = 1.0
    return hot


def source(row, col):
    if col < 0:
        return 384 + (row + 2) * REACH + col + REACH if col >= -REACH else None
    if col >= 32:
        return 480 + (row + 2) * REACH + col - 32 if col < 32 + REACH else None
    return natural(row, col)


def beside(side, row, col):
    if col < 0 or col >= 32:
        place = source(row, col)
        return None if place is None else 192 + place - (384 if side == 0 else 480)
    line = row if 0 <= row < 8 else row + 10 if row < 0 else row + 2
    return line * 16 + col - 16 * side


def natural(row, col):
    if row < 0:
        return 256 + (row + 2) * 32 + col
    if row >= 8:
        return 320 + (row - 8) * 32 + col
    return row * 32 + col


def block_tokens(block):
    return [(int(r), int(4 * block - 2 + c)) for r, c in zip(JR, JC)]


def unit_queries(unit):
    entries = [(-1, 0), (-1, 1)]
    for t in range(4):
        entries += [(t, c) for c in range(max(8 * t - 2, 0), min(8 * t + 10, 32))]
    entries += [(4, 30), (4, 31)]
    flat = [(t, r, c) for t, c in entries for r in range(-2, 10)][CUTS[unit] : CUTS[unit + 1]]
    return flat + [None] * (128 - len(flat))


def unit_keys(unit):
    return [p for b in range(FIRST[unit], FIRST[unit] + 4) for p in block_tokens(b)]


def tile_token(tile, row, col):
    r, c = row + 2, col - 8 * tile + 2
    return r * SIDE + c if 0 <= r < SIDE and 0 <= c < SIDE else None


def distances(unit):
    dist = np.full((KEYS, 128), FAR, np.float32)
    for i, query in enumerate(unit_queries(unit)):
        for k, key in enumerate(unit_keys(unit)):
            if query is not None and -REACH <= key[1] < 32 + REACH and tile_token(query[0], *key) is not None:
                dist[k, i] = max(abs(query[1] - key[0]), abs(query[2] - key[1]))
    return dist


@functools.cache
def tables():
    bf = lambda a: np.asarray(a, jnp.bfloat16)
    t = {}
    t["own"] = bf(one_hot([source(*p) for b in range(1, 8) for p in block_tokens(b)[:32]], 256))
    rim = one_hot([source(*p) for b in range(1, 8) for p in block_tokens(b)[32:]], 384)
    queries = [[None if q is None else source(*q[1:]) for q in unit_queries(u)] for u in range(5)]
    middle = np.concatenate([rim, one_hot(queries[1] + queries[2][:80] + queries[3], 384)])
    t["middle"] = bf(middle)
    t["edge"] = bf(
        np.stack(
            [
                one_hot([beside(i, *p) for b in blocks for p in block_tokens(b)], 256).tolist()
                + one_hot([None if q is None else beside(i, *q[1:]) for q in unit_queries(u)], 256).tolist()
                for i, (blocks, u) in enumerate((((-1, 0), 0), ((8, 9), 4)))
            ]
        )
    )
    t["dist"] = bf(np.stack([distances(u) for u in range(5)]))
    t["key"] = bf(
        np.stack([[one_hot([tile_token(u + k, *p) for p in unit_keys(u)], TILE_TOK) for k in (-1, 0)] for u in range(5)])
    )
    slot = np.zeros((5, 2, TILE_TOK, 128), np.float32)
    comb = np.zeros((5, 384, 128), np.float32)
    second = np.zeros((5, 1, 128), np.float32)
    for u in range(5):
        for i, q in enumerate(unit_queries(u)):
            if q is not None:
                which = q[0] - u + 1
                assert which in (0, 1)
                slot[u, which, tile_token(*q), i] = 1.0
                second[u, 0, i] = which
                comb[u, natural(*q[1:]), i] = 1.0
    t["slot"], t["second"] = bf(slot), second
    t["comb_core"], t["comb_rim"] = bf(comb[:, :256]), bf(comb[:, 256:])
    send = np.zeros((2, 64, 384), np.float32)
    send_ctl = np.zeros((2, 32, TILE_TOK), np.float32)
    put = np.zeros((2, 384, 32), np.float32)
    for r in range(SIDE):
        for k in range(REACH):
            send[0, r * REACH + k, source(r - 2, k)] = 1.0
            send[1, r * REACH + k, source(r - 2, 32 - REACH + k)] = 1.0
        for k in range(2):
            send_ctl[0, r * 2 + k, r * SIDE + k] = 1.0
            send_ctl[1, r * 2 + k, r * SIDE + 10 + k] = 1.0
            put[0, natural(r - 2, k), r * 2 + k] = 1.0
            put[1, natural(r - 2, 30 + k), r * 2 + k] = 1.0
    t["send_own"], t["send_rim"], t["send_ctl"] = bf(send[:, :, :256]), bf(send[:, :, 256:]), bf(send_ctl)
    put = np.concatenate([put[0], put[1]], axis=1)
    t["put_core"], t["put_rim"] = bf(put[:256]), bf(put[256:])
    t["valid_pad"] = bf(np.eye(TILE_TOK, 256))
    ctl = np.zeros((4, 384, TILE_TOK), np.float32)
    for tile in range(4):
        for r in range(-2, 10):
            for c in range(max(8 * tile - 2, 0), min(8 * tile + 10, 32)):
                ctl[tile, natural(r, c), tile_token(tile, r, c)] = 1.0
    t["ctl_core"] = bf(ctl[:, :256])
    ends = [np.r_[0:32, 112:144] for _ in range(4)]
    t["ctl_rim"] = bf(np.concatenate([ctl[i, 256:][:, e] for i, e in enumerate(ends)], axis=1))
    t["ctl_pick"] = bf(
        np.stack([np.concatenate([np.eye(TILE_TOK)[:, e] * (i == k) for k, e in enumerate(ends)], axis=1) for i in range(4)])
    )
    return t


def dot(a, b):
    return jnp.dot(a, b, preferred_element_type=F32)


def dot_nt(a, b):
    return lax.dot_general(a, b, (((1,), (1,)), ((), ())), preferred_element_type=F32)


def hidden_rows(x, mod_ref):
    mean = jnp.mean(x, axis=-1, keepdims=True)
    centred = x - mean
    var = jnp.mean(centred * centred, axis=-1, keepdims=True)
    normed = centred * lax.rsqrt(var + 1e-6)
    return [(normed * (1.0 + mod_ref[1, g : g + 1, :]) + mod_ref[0, g : g + 1, :]).astype(BF) for g in (0, 1)]


def eight(row):
    return jnp.broadcast_to(row, (8, row.shape[1])).astype(BF)


def fill_bias(bias_ref, unit, dist, key_a, key_b, second, valid_a, valid_b):
    usable_a, usable_b = dot_nt(key_a, eight(valid_a))[:, :1], dot_nt(key_b, eight(valid_b))[:, :1]
    dist = dist.astype(F32)
    usable = (jnp.where(second > 0.5, usable_b, usable_a) > 0.5) | (dist == 0.0)
    dist = jnp.where(usable, dist, FAR)
    for r in range(5):
        bias_ref[unit, r] = jnp.where(dist <= r + 1.0, 0.0, -1e30)


def attend(queries, keys, values, bias, radius_ref, put):
    lane = lax.broadcasted_iota(jnp.int32, (1, 256), 1)

    def score(g, p):
        lanes = slice(128 * p, 128 * p + 256)
        q = queries(g, lanes)
        both = [
            q * ((lane >= 16 * p + at) & (lane < 16 * p + at + HEAD_DIM)).astype(F32).astype(BF) for at in (0, HEAD_DIM)
        ]
        return dot_nt(keys(g, lanes), jnp.concatenate(both, axis=0))

    def soften(p, scores):
        exps, scales = [], []
        for i in (0, 1):
            s = scores[:, 128 * i : 128 * i + 128] + bias(radius_ref[2 * p + i] - 1)
            top = jnp.max(s, axis=0, keepdims=True)
            e = jnp.exp2((s - top) * EXP_SCALE)
            scales.append(1.0 / jnp.sum(e, axis=0, keepdims=True))
            exps.append(e)
        return jnp.concatenate(exps, axis=1).astype(BF), scales

    def collect(g, p, e, scales):
        v = values(g, slice(128 * p, 128 * p + 256)).T[16 * p : 16 * p + 144]
        o = dot(v, e)
        o = jnp.concatenate([o[:72, :128] * scales[0], o[72:, 128:] * scales[1]], axis=0)
        put(g, slice(144 * p, 144 * p + 144), o.astype(BF))

    items = [(g, p) for g in (0, 1) for p in range(8)]
    scores = {k: score(*items[k]) for k in range(GROUP)}
    probs = {}
    for k in range(len(items) + GROUP):
        if k + GROUP < len(items):
            scores[k + GROUP] = score(*items[k + GROUP])
        if k < len(items):
            probs[k] = soften(items[k][1], scores.pop(k))
        if k >= GROUP:
            collect(*items[k - GROUP], *probs.pop(k - GROUP))


def inner_window(own, rim, c, first, count):
    def get(g, lanes):
        parts = []
        for i in range(count):
            parts += [own[c, g, first + i, :, lanes], rim[c, g, first + i, :, lanes]]
        return parts

    return get


def own_kernel(
    latent_h, control_h, valid_h, mod_h, w_h, own_h, send_own_h, send_ctl_h, valid_pad_h,
    kv, msg, w, latent, control, valid, mod, own, send_own, send_ctl, valid_pad, hid, sem,
):
    pairs = [
        (latent_h, latent),
        (own_h, own),
        (mod_h, mod),
        (w_h.at[:, pl.ds(D, D)], w.at[:, pl.ds(D, D)]),
        (w_h.at[:, pl.ds(2 * D, D)], w.at[:, pl.ds(2 * D, D)]),
        (control_h.at[pl.ds(0, 1)], control.at[pl.ds(0, 1)]),
        (control_h.at[pl.ds(3, 1)], control.at[pl.ds(1, 1)]),
        (valid_h, valid),
        (send_own_h, send_own),
        (send_ctl_h, send_ctl),
        (valid_pad_h, valid_pad),
        (w_h.at[:, pl.ds(0, D)], w.at[:, pl.ds(0, D)]),
    ]
    copies = [pltpu.make_async_copy(src, dst, sem.at[i]) for i, (src, dst) in enumerate(pairs)]
    for copy in copies:
        copy.start()
    for copy in copies[:3]:
        copy.wait()
    rows = hidden_rows(dot(own[...], latent[...]), mod)
    hid[:224] = rows[0]
    hid[224:] = rows[1]
    for c in (0, 1):
        copies[3 + c].wait()
        out = dot(hid[...], w[:, (c + 1) * D : (c + 2) * D])
        kv[c] = out.astype(BF).reshape(2, 7, 32, D)
    for copy in copies[5:]:
        copy.wait()
    rows = lax.broadcasted_iota(jnp.int32, (32, 1), 0)
    val = valid[...].astype(F32)
    for i, tile, rim in ((0, 0, 2 * SIDE + 1), (1, 3, 2 * SIDE + 10)):
        msg[i, :64] = dot(send_own[i], latent[...]).astype(BF)
        own_row = val[tile : tile + 1]
        ctl = dot((send_ctl[i].astype(F32) * own_row).astype(BF), control[i])
        row = dot(eight(own_row * own_row[:, rim : rim + 1]), valid_pad[...])
        msg[i, 64:, 256:] = ctl[:, 256:].astype(BF)
        msg[i, 64:, :256] = jnp.where(rows == 31, row[0:1], ctl[:, :256]).astype(BF)


def pack_kernel(msg, above, below, send_rim, west, east):
    for i, out in ((0, west), (1, east)):
        rim = dot(send_rim[i, :, :64], above[...]) + dot(send_rim[i, :, 64:], below[...])
        out[:64] = (msg[i, :64].astype(F32) + rim).astype(BF)
        out[64:] = msg[i, 64:]


def middle_kernel(
    radius, latent, above, below, valid, mod, w, kv_own, middle, dist, key, second, kv_rim, attn, near, hid, qs, bias
):
    near[:256] = latent[...]
    near[256:320] = above[...]
    near[320:] = below[...]
    rows = hidden_rows(dot(middle[...], near[...]), mod)
    for g in (0, 1):
        hid[g * 112 : (g + 1) * 112] = rows[g][:112]
        hid[224 + g * 336 : 224 + (g + 1) * 336] = rows[g][112:]
    qs[...] = dot(hid[224:], w[:, :D]).astype(BF).reshape(2, 336, D)
    out = dot(hid[:224], w[:, D:]).astype(BF)
    for c in (0, 1):
        kv_rim[c] = out[:, c * D : (c + 1) * D].reshape(2, 7, 16, D)
    val = valid[...].astype(F32)
    for u in range(3):
        fill_bias(bias, u, dist[u], key[u, 0], key[u, 1], second[u], val[u : u + 1], val[u + 1 : u + 2])

    for u in range(3):
        first = u + min(u, 1)
        start = 128 * u - 48 * (u // 2)
        keys = inner_window(kv_own, kv_rim, 0, first, 4)
        values = inner_window(kv_own, kv_rim, 1, first, 4)

        def put(g, rows, o, u=u):
            attn[g, rows, 128 * u : 128 * u + 128] = o

        attend(
            lambda g, lanes: qs[g, pl.ds(start, 128), lanes],
            lambda g, lanes: jnp.concatenate(keys(g, lanes), axis=0),
            lambda g, lanes: jnp.concatenate(values(g, lanes), axis=0),
            lambda r: bias[u, r],
            radius,
            put,
        )


def valid_rows(valid, west, east):
    val = valid[...].astype(F32)
    side = [ref[80:96, :256].astype(F32)[15:16, :TILE_TOK] for ref in (west, east)]
    return [side[0]] + [val[t : t + 1] for t in range(4)] + [side[1]]


def gather(unit, slot, comb, rows):
    weight = dot(eight(rows[unit]), slot[unit, 0]) + dot(eight(rows[unit + 1]), slot[unit, 1])
    return comb[unit].astype(F32) * weight[:1]


def block_sums(attn_mid, attn_edge, rows, x, w_out, mod, west, east, slot, comb, ctl, put):
    weights = [gather(u, slot, comb, rows) for u in range(5)]
    number = sum(jnp.sum(w, axis=1, keepdims=True) for w in weights)
    n = number.shape[0]
    inner = jnp.concatenate(weights[1:4], axis=1).astype(BF)
    outer = jnp.concatenate([weights[0], weights[4]], axis=1).astype(BF)
    attn = [(dot_nt(inner, attn_mid[g]) + dot_nt(outer, attn_edge[g])).astype(BF) for g in (0, 1)]
    proj = dot(jnp.concatenate(attn, axis=0), w_out[...])
    sums = (GUIDE * mod[2, 0:1]) * proj[:n] + ((1.0 - GUIDE) * mod[2, 1:2]) * proj[n:] + number * x
    return sums + ctl + dot(put[...], jnp.concatenate([west[64:], east[64:]], axis=0)), number


def edge_kernel(
    radius, latent, above, below, west, east, valid, mod, w, kv_own, kv_rim, attn_mid, w_out, control,
    edge, dist, key, second, slot, comb, ctl, ctl_pick, put_ctl,
    up, down, attn, near, hid, qs, kv, bias,
):
    parts = []
    for i, message in ((0, west), (1, east)):
        at = 0
        for ref, lines in ((latent, 8), (above, 2), (below, 2)):
            for line in range(lines):
                near[i, at : at + 16] = ref[32 * line + 16 * i : 32 * line + 16 * i + 16]
                at += 16
        near[i, at:] = message[:64]
        parts.append(dot(edge[i], near[i]))
    x = jnp.concatenate([p[:96] for p in parts] + [p[96:] for p in parts], axis=0)
    normed = hidden_rows(x, mod)
    for g in (0, 1):
        hid[g * 192 : (g + 1) * 192] = normed[g][:192]
        hid[384 + g * 256 : 384 + (g + 1) * 256] = normed[g][192:]
    qs[...] = dot(hid[384:], w[:, :D]).astype(BF).reshape(2, 2, 128, D)
    out = dot(hid[:384], w[:, D:]).astype(BF)
    for c in (0, 1):
        kv[c] = out[:, c * D : (c + 1) * D].reshape(2, 4, 48, D)
    rows = valid_rows(valid, west, east)
    for i, u in ((0, 0), (1, 4)):
        fill_bias(bias, i, dist[i], key[i, 0], key[i, 1], second[i], rows[u], rows[u + 1])

    for i in (0, 1):

        def window(c):
            inner = inner_window(kv_own, kv_rim, c, 5 * i, 2)

            def get(g, lanes):
                outer = [kv[c, g, 2 * i, :, lanes], kv[c, g, 2 * i + 1, :, lanes]]
                parts = inner(g, lanes) + outer if i else outer + inner(g, lanes)
                return jnp.concatenate(parts, axis=0)

            return get

        def put(g, rows, o):
            attn[g, rows, 128 * i : 128 * i + 128] = o

        attend(lambda g, lanes: qs[g, i, :, lanes], window(0), window(1), lambda r: bias[i, r], radius, put)

    x = jnp.concatenate([above[...], below[...]], axis=0).astype(F32)
    weight = sum(dot(eight(rows[tile + 1]), ctl_pick[tile]) for tile in range(4))[:1]
    ends = [control[tile, at : at + 32] for tile in range(4) for at in (0, 112)]
    extra = dot((ctl[...].astype(F32) * weight).astype(BF), jnp.concatenate(ends, axis=0))
    sums, number = block_sums(attn_mid, attn, rows, x, w_out, mod, west, east, slot, comb, extra, put_ctl)
    row = lax.broadcasted_iota(jnp.int32, (64, 128), 0)
    lane = lax.broadcasted_iota(jnp.int32, (64, 128), 1)
    for at, out in ((0, up), (64, down)):
        out[:64] = sums[at : at + 64].astype(BF)
        tail = jnp.sum(jnp.where(row == lane, number[at : at + 64], 0.0), axis=0, keepdims=True)
        out[64:, :128] = jnp.broadcast_to(tail, (16, 128)).astype(BF)
        out[64:, 128:] = jnp.zeros((16, D - 128), BF)


def core_kernel(
    attn_mid, attn_edge, latent, west, east, valid, mod, w_out, control, slot, comb, ctl, put, out, rest, count, done, sem
):
    rows = valid_rows(valid, west, east)
    extra = sum(dot((ctl[tile].astype(F32) * rows[tile + 1]).astype(BF), control[tile]) for tile in range(4))
    x = latent[...].astype(F32)
    sums, number = block_sums(attn_mid, attn_edge, rows, x, w_out, mod, west, east, slot, comb, extra, put)
    done[...] = (sums[64:192] / number[64:192]).astype(BF)
    copy = pltpu.make_async_copy(done, out.at[pl.ds(64, 128)], sem)
    copy.start()
    rest[0] = sums[:64]
    rest[1] = sums[192:]
    count[0] = jnp.broadcast_to(number[:64], (64, 128))
    count[1] = jnp.broadcast_to(number[192:], (64, 128))
    copy.wait()


def final_kernel(rest, count, above, below, whole_out, out, done, sem):
    del whole_out
    row = lax.broadcasted_iota(jnp.int32, (64, 128), 0)
    lane = lax.broadcasted_iota(jnp.int32, (64, 128), 1)
    copies = []
    for i, ref in ((0, above), (1, below)):
        tail = ref[64:80, :128].astype(F32)[:1]
        number = jnp.sum(jnp.where(row == lane, tail, 0.0), axis=1, keepdims=True) + count[i][:, :1]
        done[i] = ((rest[i] + ref[:64].astype(F32)) / number).astype(BF)
        copies.append(pltpu.make_async_copy(done.at[i], out.at[pl.ds(192 * i, 64)], sem.at[i]))
        copies[i].start()
    for copy in copies:
        copy.wait()


def call(kernel, outs, args, specs=None, out_specs=None, scratch=(), cost=(1e9, 4e6), aliases=None, limit=VMEM):
    specs = specs or {}
    out_specs = out_specs or {}
    vmem = pl.BlockSpec(memory_space=pltpu.VMEM)
    return pl.pallas_call(
        kernel,
        out_shape=outs,
        in_specs=[specs.get(i, vmem) for i in range(len(args))],
        out_specs=[out_specs.get(i, vmem) for i in range(len(outs))],
        scratch_shapes=scratch,
        input_output_aliases=aliases or {},
        compiler_params=pltpu.CompilerParams(vmem_limit_bytes=limit),
        cost_estimate=pl.CostEstimate(flops=int(cost[0]), bytes_accessed=int(cost[1]), transcendentals=0),
    )(*[jnp.asarray(a) for a in args])


def shape(*dims, dtype=BF):
    return jax.ShapeDtypeStruct(dims, dtype)


def local(latent, control, valid, radius, modulation, w_qkv, w_out):
    t = tables()
    size_r, size_c = lax.axis_size("trow"), lax.axis_size("tcol")
    later_r = [(i, (i + 1) % size_r) for i in range(size_r)]
    sooner_r = [((i + 1) % size_r, i) for i in range(size_r)]
    later_c = [(i, (i + 1) % size_c) for i in range(size_c)]
    sooner_c = [((i + 1) % size_c, i) for i in range(size_c)]

    x = latent.reshape(256, D)
    control = control.reshape(4, TILE_TOK, D)
    valid = valid.reshape(4, TILE_TOK)
    above = lax.ppermute(x[192:], "trow", later_r)
    below = lax.ppermute(x[:64], "trow", sooner_r)
    smem = pl.BlockSpec(memory_space=pltpu.SMEM)
    hbm = pl.BlockSpec(memory_space=pl.ANY)

    mod = modulation.transpose(1, 0, 2)
    far = lambda a: pltpu.with_memory_space_constraint(jnp.asarray(a), pltpu.MemorySpace.HBM)
    first = [x, control, valid, mod, w_qkv, t["own"], t["send_own"], t["send_ctl"], t["valid_pad"]]
    staged = [(256, D, BF), (2, TILE_TOK, D, BF), (4, TILE_TOK, jnp.int32), (3, 2, D, F32)]
    staged += [t[k].shape + (BF,) for k in ("own", "send_own", "send_ctl", "valid_pad")]
    kv_own, msg, w = call(
        own_kernel,
        [shape(2, 2, 7, 32, D), shape(2, 96, D), shape(D, 3 * D)],
        [far(a) for a in first],
        specs={i: hbm for i in range(len(first))},
        scratch=[pltpu.VMEM(s[:-1], s[-1]) for s in staged]
        + [pltpu.VMEM((448, D), BF), pltpu.SemaphoreType.DMA((12,))],
        cost=(3.6e9, 12e6),
    )
    to_west, to_east = call(
        pack_kernel, [shape(96, D), shape(96, D)], [msg, above, below, t["send_rim"]], cost=(1e8, 1e6)
    )
    west = lax.ppermute(to_east, "tcol", later_c)
    east = lax.ppermute(to_west, "tcol", sooner_c)

    mid = slice(1, 4)
    kv_rim, attn_mid = call(
        middle_kernel,
        [shape(2, 2, 7, 16, D), shape(2, D, 384)],
        [
            radius, x, above, below, valid, mod, w, kv_own,
            t["middle"], t["dist"][mid], t["key"][mid], t["second"][mid],
        ],
        specs={0: smem},
        scratch=[
            pltpu.VMEM((384, D), BF),
            pltpu.VMEM((896, D), BF),
            pltpu.VMEM((2, 336, D), BF),
            pltpu.VMEM((3, 5, KEYS, 128), F32),
        ],
        cost=(8e9, 14e6),
    )
    ends = slice(0, 5, 4)
    up, down, attn_edge = call(
        edge_kernel,
        [shape(80, D), shape(80, D), shape(2, D, 256)],
        [
            radius, x, above, below, west, east, valid, mod, w, kv_own, kv_rim, attn_mid, w_out, control,
            t["edge"], t["dist"][ends], t["key"][ends], t["second"][ends], t["slot"], t["comb_rim"], t["ctl_rim"], t["ctl_pick"], t["put_rim"],
        ],
        specs={0: smem},
        scratch=[
            pltpu.VMEM((2, 256, D), BF),
            pltpu.VMEM((896, D), BF),
            pltpu.VMEM((2, 2, 128, D), BF),
            pltpu.VMEM((2, 2, 4, 48, D), BF),
            pltpu.VMEM((2, 5, KEYS, 128), F32),
        ],
        cost=(1e10, 16e6),
    )
    got_below = lax.ppermute(up, "trow", sooner_r)
    got_above = lax.ppermute(down, "trow", later_r)
    out, rest, count = call(
        core_kernel,
        [shape(256, D), shape(2, 64, D, dtype=F32), shape(2, 64, 128, dtype=F32)],
        [
            attn_mid, attn_edge, x, west, east, valid, mod, w_out, control,
            t["slot"], t["comb_core"], t["ctl_core"], t["put_core"],
        ],
        out_specs={0: hbm},
        scratch=[pltpu.VMEM((128, D), BF), pltpu.SemaphoreType.DMA],
        cost=(3e9, 8e6),
    )
    (out,) = call(
        final_kernel,
        [shape(256, D)],
        [rest, count, got_above, got_below, out],
        specs={4: hbm},
        out_specs={0: hbm},
        scratch=[pltpu.VMEM((2, 64, D), BF), pltpu.SemaphoreType.DMA((2,))],
        aliases={4: 0},
        cost=(2e8, 3e6),
    )
    return out.reshape(CORE, 32, D)


def solution(mesh):
    placed = (
        P("trow", "tcol", None),
        P("trow", "tcol", None, None),
        P("trow", "tcol", None),
        P(),
        P(),
        P(),
        P(),
    )
    return jax.shard_map(
        local, mesh=mesh, in_specs=placed, out_specs=P("trow", "tcol", None), check_vma=False
    )
```

```python
import functools

import jax
import jax.numpy as jnp
import numpy as np
from jax import lax
from jax.experimental import pallas as pl
from jax.experimental.pallas import tpu as pltpu
from jax.sharding import PartitionSpec as P

D = 1152
HEADS = 16
HEAD_DIM = 72
CORE = 8
MARGIN = 2
SIDE = 12
TILE_TOK = 144
GUIDE = 4.5
REACH = 5
FAR = 99.0
BF = jnp.bfloat16
F32 = jnp.float32
EXP_SCALE = float(np.log2(np.e) / np.sqrt(72.0))
VMEM = 28 * 1024 * 1024

JR = np.array([j // 4 if j < 32 else (j - 40) // 4 if j < 40 else 8 + (j - 40) // 4 for j in range(48)])
JC = np.arange(48) % 4
FIRST = (-1, 1, 2, 4, 6)
COUNT = (4, 4, 5, 4, 4)
KEYS = 192
LATE_KEYS = 240
LATE_ROWS = 80
GROUP = 4


def one_hot(rows, depth):
    hot = np.zeros((len(rows), depth), np.float32)
    for i, src in enumerate(rows):
        if src is not None:
            hot[i, src] = 1.0
    return hot


def source(row, col):
    if col < 0:
        return 384 + (row + 2) * REACH + col + REACH if col >= -REACH else None
    if col >= 32:
        return 480 + (row + 2) * REACH + col - 32 if col < 32 + REACH else None
    return natural(row, col)


def beside(side, row, col):
    if col < 0 or col >= 32:
        place = source(row, col)
        return None if place is None else 192 + place - (384 if side == 0 else 480)
    line = row if 0 <= row < 8 else row + 10 if row < 0 else row + 2
    return line * 16 + col - 16 * side


def natural(row, col):
    if row < 0:
        return 256 + (row + 2) * 32 + col
    if row >= 8:
        return 320 + (row - 8) * 32 + col
    return row * 32 + col


def block_tokens(block):
    return [(int(r), int(4 * block - 2 + c)) for r, c in zip(JR, JC)]


def unit_queries(unit):
    entries = [(-1, 0), (-1, 1)]
    for t in range(4):
        entries += [(t, c) for c in range(max(8 * t - 2, 0), min(8 * t + 10, 32))]
    entries += [(4, 30), (4, 31)]
    flat = [(t, r, c) for t, c in entries for r in range(-2, 10)]
    left, right = flat[126:288], flat[288:450]
    rim = [[q for q in half if not 0 <= q[1] < CORE] for half in (left, right)]
    core = [[q for q in half if 0 <= q[1] < CORE] for half in (left, right)]
    units = [flat[:126], rim[0] + core[0][:74], core[0][74:] + core[1][:34], rim[1] + core[1][34:], flat[450:]]
    assert sum(len(u) for u in units) == 576
    return units[unit] + [None] * (128 - len(units[unit]))


def unit_keys(unit):
    return [p for b in range(FIRST[unit], FIRST[unit] + COUNT[unit]) for p in block_tokens(b)]


def tile_token(tile, row, col):
    r, c = row + 2, col - 8 * tile + 2
    return r * SIDE + c if 0 <= r < SIDE and 0 <= c < SIDE else None


def distances(unit):
    dist = np.full((48 * COUNT[unit], 128), FAR, np.float32)
    for i, query in enumerate(unit_queries(unit)):
        for k, key in enumerate(unit_keys(unit)):
            if query is not None and -REACH <= key[1] < 32 + REACH and tile_token(query[0], *key) is not None:
                dist[k, i] = max(abs(query[1] - key[0]), abs(query[2] - key[1]))
    return dist


@functools.cache
def tables():
    bf = lambda a: np.asarray(a, jnp.bfloat16)
    t = {}
    t["own"] = bf(one_hot([source(*p) for b in range(1, 8) for p in block_tokens(b)[:32]], 256))
    rim = one_hot([source(*p) for b in range(1, 8) for p in block_tokens(b)[32:]], 384)
    queries = [[None if q is None else source(*q[1:]) for q in unit_queries(u)] for u in range(5)]
    middle = np.concatenate([rim, one_hot(queries[1] + queries[3], 384)])
    t["middle"] = bf(middle)
    t["edge"] = bf(
        np.stack(
            [
                one_hot([beside(i, *p) for b in blocks for p in block_tokens(b)], 256).tolist()
                + one_hot([None if q is None else beside(i, *q[1:]) for q in unit_queries(u)], 256).tolist()
                for i, (blocks, u) in enumerate((((-1, 0), 0), ((8, 9), 4)))
            ]
        )
    )
    t["late"] = bf(one_hot(queries[2][:LATE_ROWS], 256))
    for name, members in (("edge", (0, 4)), ("mid", (1, 3)), ("late", (2,))):
        t["dist_" + name] = bf(np.stack([distances(u) for u in members]))
        t["key_" + name] = bf(
            np.stack([[one_hot([tile_token(u + k, *p) for p in unit_keys(u)], TILE_TOK) for k in (-1, 0)] for u in members])
        )
    slot = np.zeros((5, 2, TILE_TOK, 128), np.float32)
    comb = np.zeros((5, 384, 128), np.float32)
    second = np.zeros((5, 1, 128), np.float32)
    for u in range(5):
        for i, q in enumerate(unit_queries(u)):
            if q is not None:
                which = q[0] - u + 1
                assert which in (0, 1)
                slot[u, which, tile_token(*q), i] = 1.0
                second[u, 0, i] = which
                comb[u, natural(*q[1:]), i] = 1.0
    t["slot"], t["second"] = bf(slot), second
    t["comb_core"], t["comb_rim"] = bf(comb[:, :256]), bf(comb[:, 256:])
    send = np.zeros((2, 64, 384), np.float32)
    send_ctl = np.zeros((2, 32, TILE_TOK), np.float32)
    put = np.zeros((2, 384, 32), np.float32)
    for r in range(SIDE):
        for k in range(REACH):
            send[0, r * REACH + k, source(r - 2, k)] = 1.0
            send[1, r * REACH + k, source(r - 2, 32 - REACH + k)] = 1.0
        for k in range(2):
            send_ctl[0, r * 2 + k, r * SIDE + k] = 1.0
            send_ctl[1, r * 2 + k, r * SIDE + 10 + k] = 1.0
            put[0, natural(r - 2, k), r * 2 + k] = 1.0
            put[1, natural(r - 2, 30 + k), r * 2 + k] = 1.0
    t["send_own"], t["send_rim"], t["send_ctl"] = bf(send[:, :, :256]), bf(send[:, :, 256:]), bf(send_ctl)
    put = np.concatenate([put[0], put[1]], axis=1)
    t["put_core"], t["put_rim"] = bf(put[:256]), bf(put[256:])
    t["valid_pad"] = bf(np.eye(TILE_TOK, 256))
    ctl = np.zeros((4, 384, TILE_TOK), np.float32)
    for tile in range(4):
        for r in range(-2, 10):
            for c in range(max(8 * tile - 2, 0), min(8 * tile + 10, 32)):
                ctl[tile, natural(r, c), tile_token(tile, r, c)] = 1.0
    t["ctl_core"] = bf(ctl[:, :256])
    ends = [np.r_[0:32, 112:144] for _ in range(4)]
    t["ctl_rim"] = bf(np.concatenate([ctl[i, 256:][:, e] for i, e in enumerate(ends)], axis=1))
    t["ctl_pick"] = bf(
        np.stack([np.concatenate([np.eye(TILE_TOK)[:, e] * (i == k) for k, e in enumerate(ends)], axis=1) for i in range(4)])
    )
    return t


def dot(a, b):
    return jnp.dot(a, b, preferred_element_type=F32)


def dot_nt(a, b):
    return lax.dot_general(a, b, (((1,), (1,)), ((), ())), preferred_element_type=F32)


def hidden_rows(x, mod_ref):
    mean = jnp.mean(x, axis=-1, keepdims=True)
    centred = x - mean
    var = jnp.mean(centred * centred, axis=-1, keepdims=True)
    normed = centred * lax.rsqrt(var + 1e-6)
    return [(normed * (1.0 + mod_ref[1, g : g + 1, :]) + mod_ref[0, g : g + 1, :]).astype(BF) for g in (0, 1)]


def eight(row):
    return jnp.broadcast_to(row, (8, row.shape[1])).astype(BF)


def fill_bias(bias_ref, unit, dist, key_a, key_b, second, valid_a, valid_b):
    usable_a, usable_b = dot_nt(key_a, eight(valid_a))[:, :1], dot_nt(key_b, eight(valid_b))[:, :1]
    dist = dist.astype(F32)
    usable = (jnp.where(second > 0.5, usable_b, usable_a) > 0.5) | (dist == 0.0)
    dist = jnp.where(usable, dist, FAR)
    for r in range(5):
        bias_ref[unit, r] = jnp.where(dist <= r + 1.0, 0.0, -1e30)


def attend(queries, keys, values, bias, radius_ref, put):
    lane = lax.broadcasted_iota(jnp.int32, (1, 256), 1)

    def score(g, p):
        lanes = slice(128 * p, 128 * p + 256)
        q = queries(g, lanes)
        both = [
            q * ((lane >= 16 * p + at) & (lane < 16 * p + at + HEAD_DIM)).astype(F32).astype(BF) for at in (0, HEAD_DIM)
        ]
        return dot_nt(keys(g, lanes), jnp.concatenate(both, axis=0))

    def soften(p, scores):
        exps, scales = [], []
        for i in (0, 1):
            s = scores[:, 128 * i : 128 * i + 128] + bias(radius_ref[2 * p + i] - 1)
            top = jnp.max(s, axis=0, keepdims=True)
            e = jnp.exp2((s - top) * EXP_SCALE)
            scales.append(1.0 / jnp.sum(e, axis=0, keepdims=True))
            exps.append(e)
        return jnp.concatenate(exps, axis=1).astype(BF), scales

    def collect(g, p, e, scales):
        v = values(g, slice(128 * p, 128 * p + 256)).T[16 * p : 16 * p + 144]
        o = dot(v, e)
        o = jnp.concatenate([o[:72, :128] * scales[0], o[72:, 128:] * scales[1]], axis=0)
        put(g, slice(144 * p, 144 * p + 144), o.astype(BF))

    items = [(g, p) for g in (0, 1) for p in range(8)]
    scores = {k: score(*items[k]) for k in range(GROUP)}
    probs = {}
    for k in range(len(items) + GROUP):
        if k + GROUP < len(items):
            scores[k + GROUP] = score(*items[k + GROUP])
        if k < len(items):
            probs[k] = soften(items[k][1], scores.pop(k))
        if k >= GROUP:
            collect(*items[k - GROUP], *probs.pop(k - GROUP))


def inner_window(own, rim, c, first, count):
    def get(g, lanes):
        parts = []
        for i in range(count):
            parts += [own[c, g, first + i, :, lanes], rim[c, g, first + i, :, lanes]]
        return parts

    return get


def own_kernel(
    latent_h, control_h, valid_h, mod_h, w_h, own_h, send_own_h, send_ctl_h, valid_pad_h,
    kv, msg, w, latent, control, valid, mod, own, send_own, send_ctl, valid_pad, hid, sem,
):
    pairs = [
        (latent_h, latent),
        (own_h, own),
        (mod_h, mod),
        (w_h.at[:, pl.ds(D, D)], w.at[:, pl.ds(D, D)]),
        (w_h.at[:, pl.ds(2 * D, D)], w.at[:, pl.ds(2 * D, D)]),
        (control_h.at[pl.ds(0, 1)], control.at[pl.ds(0, 1)]),
        (control_h.at[pl.ds(3, 1)], control.at[pl.ds(1, 1)]),
        (valid_h, valid),
        (send_own_h, send_own),
        (send_ctl_h, send_ctl),
        (valid_pad_h, valid_pad),
        (w_h.at[:, pl.ds(0, D)], w.at[:, pl.ds(0, D)]),
    ]
    copies = [pltpu.make_async_copy(src, dst, sem.at[i]) for i, (src, dst) in enumerate(pairs)]
    for copy in copies:
        copy.start()
    for copy in copies[:3]:
        copy.wait()
    rows = hidden_rows(dot(own[...], latent[...]), mod)
    hid[:224] = rows[0]
    hid[224:] = rows[1]
    for c in (0, 1):
        copies[3 + c].wait()
        out = dot(hid[...], w[:, (c + 1) * D : (c + 2) * D])
        kv[c] = out.astype(BF).reshape(2, 7, 32, D)
    for copy in copies[5:]:
        copy.wait()
    rows = lax.broadcasted_iota(jnp.int32, (32, 1), 0)
    val = valid[...].astype(F32)
    for i, tile, rim in ((0, 0, 2 * SIDE + 1), (1, 3, 2 * SIDE + 10)):
        msg[i, :64] = dot(send_own[i], latent[...]).astype(BF)
        own_row = val[tile : tile + 1]
        ctl = dot((send_ctl[i].astype(F32) * own_row).astype(BF), control[i])
        row = dot(eight(own_row * own_row[:, rim : rim + 1]), valid_pad[...])
        msg[i, 64:, 256:] = ctl[:, 256:].astype(BF)
        msg[i, 64:, :256] = jnp.where(rows == 31, row[0:1], ctl[:, :256]).astype(BF)


def pack_kernel(msg, above, below, send_rim, west, east):
    for i, out in ((0, west), (1, east)):
        rim = dot(send_rim[i, :, :64], above[...]) + dot(send_rim[i, :, 64:], below[...])
        out[:64] = (msg[i, :64].astype(F32) + rim).astype(BF)
        out[64:] = msg[i, 64:]


def middle_kernel(
    radius, latent, above, below, valid, mod, w, kv_own, middle, dist, key, second, kv_rim, attn, near, hid, qs, bias
):
    near[:256] = latent[...]
    near[256:320] = above[...]
    near[320:] = below[...]
    rows = hidden_rows(dot(middle[...], near[...]), mod)
    for g in (0, 1):
        hid[g * 112 : (g + 1) * 112] = rows[g][:112]
        hid[224 + g * 256 : 224 + (g + 1) * 256] = rows[g][112:]
    qs[...] = dot(hid[224:], w[:, :D]).astype(BF).reshape(2, 2, 128, D)
    out = dot(hid[:224], w[:, D:]).astype(BF)
    for c in (0, 1):
        kv_rim[c] = out[:, c * D : (c + 1) * D].reshape(2, 7, 16, D)
    val = valid[...].astype(F32)
    for i in (0, 1):
        fill_bias(bias, i, dist[i], key[i, 0], key[i, 1], second[i], val[2 * i : 2 * i + 1], val[2 * i + 1 : 2 * i + 2])

    for i in (0, 1):
        keys = inner_window(kv_own, kv_rim, 0, 3 * i, 4)
        values = inner_window(kv_own, kv_rim, 1, 3 * i, 4)

        def put(g, rows, o):
            attn[g, rows, 128 * i : 128 * i + 128] = o

        attend(
            lambda g, lanes: qs[g, i, :, lanes],
            lambda g, lanes: jnp.concatenate(keys(g, lanes), axis=0),
            lambda g, lanes: jnp.concatenate(values(g, lanes), axis=0),
            lambda r: bias[i, r],
            radius,
            put,
        )


def valid_rows(valid, west, east):
    val = valid[...].astype(F32)
    side = [ref[80:96, :256].astype(F32)[15:16, :TILE_TOK] for ref in (west, east)]
    return [side[0]] + [val[t : t + 1] for t in range(4)] + [side[1]]


def gather(unit, slot, comb, rows):
    weight = dot(eight(rows[unit]), slot[unit, 0]) + dot(eight(rows[unit + 1]), slot[unit, 1])
    return comb[unit].astype(F32) * weight[:1]


def block_sums(parts, rows, x, w_out, mod, west, east, slot, comb, ctl, put):
    weights = {u: gather(u, slot, comb, rows) for units, _ in parts for u in units}
    number = sum(jnp.sum(w, axis=1, keepdims=True) for w in weights.values())
    n = number.shape[0]
    attn = [0.0, 0.0]
    for units, ref in parts:
        weight = jnp.concatenate([weights[u] for u in units], axis=1).astype(BF)
        attn = [attn[g] + dot_nt(weight, ref[g]) for g in (0, 1)]
    attn = [a.astype(BF) for a in attn]
    proj = dot(jnp.concatenate(attn, axis=0), w_out[...])
    sums = (GUIDE * mod[2, 0:1]) * proj[:n] + ((1.0 - GUIDE) * mod[2, 1:2]) * proj[n:] + number * x
    return sums + ctl + dot(put[...], jnp.concatenate([west[64:], east[64:]], axis=0)), number


def edge_kernel(
    radius, latent, above, below, west, east, valid, mod, w, kv_own, kv_rim, attn_mid, w_out, control,
    edge, dist, key, second, slot, comb, ctl, ctl_pick, put_ctl,
    up, down, attn, near, hid, qs, kv, bias,
):
    parts = []
    for i, message in ((0, west), (1, east)):
        at = 0
        for ref, lines in ((latent, 8), (above, 2), (below, 2)):
            for line in range(lines):
                near[i, at : at + 16] = ref[32 * line + 16 * i : 32 * line + 16 * i + 16]
                at += 16
        near[i, at:] = message[:64]
        parts.append(dot(edge[i], near[i]))
    x = jnp.concatenate([p[:96] for p in parts] + [p[96:] for p in parts], axis=0)
    normed = hidden_rows(x, mod)
    for g in (0, 1):
        hid[g * 192 : (g + 1) * 192] = normed[g][:192]
        hid[384 + g * 256 : 384 + (g + 1) * 256] = normed[g][192:]
    qs[...] = dot(hid[384:], w[:, :D]).astype(BF).reshape(2, 2, 128, D)
    out = dot(hid[:384], w[:, D:]).astype(BF)
    for c in (0, 1):
        kv[c] = out[:, c * D : (c + 1) * D].reshape(2, 4, 48, D)
    rows = valid_rows(valid, west, east)
    for i, u in ((0, 0), (1, 4)):
        fill_bias(bias, i, dist[i], key[i, 0], key[i, 1], second[i], rows[u], rows[u + 1])

    for i in (0, 1):

        def window(c):
            inner = inner_window(kv_own, kv_rim, c, 5 * i, 2)

            def get(g, lanes):
                outer = [kv[c, g, 2 * i, :, lanes], kv[c, g, 2 * i + 1, :, lanes]]
                parts = inner(g, lanes) + outer if i else outer + inner(g, lanes)
                return jnp.concatenate(parts, axis=0)

            return get

        def put(g, rows, o):
            attn[g, rows, 128 * i : 128 * i + 128] = o

        attend(lambda g, lanes: qs[g, i, :, lanes], window(0), window(1), lambda r: bias[i, r], radius, put)

    x = jnp.concatenate([above[...], below[...]], axis=0).astype(F32)
    weight = sum(dot(eight(rows[tile + 1]), ctl_pick[tile]) for tile in range(4))[:1]
    ends = [control[tile, at : at + 32] for tile in range(4) for at in (0, 112)]
    extra = dot((ctl[...].astype(F32) * weight).astype(BF), jnp.concatenate(ends, axis=0))
    sums, number = block_sums((((1, 3), attn_mid), ((0, 4), attn)), rows, x, w_out, mod, west, east, slot, comb, extra, put_ctl)
    row = lax.broadcasted_iota(jnp.int32, (64, 128), 0)
    lane = lax.broadcasted_iota(jnp.int32, (64, 128), 1)
    for at, out in ((0, up), (64, down)):
        out[:64] = sums[at : at + 64].astype(BF)
        tail = jnp.sum(jnp.where(row == lane, number[at : at + 64], 0.0), axis=0, keepdims=True)
        out[64:, :128] = jnp.broadcast_to(tail, (16, 128)).astype(BF)
        out[64:, 128:] = jnp.zeros((16, D - 128), BF)


def core_kernel(
    radius, attn_mid, attn_edge, latent, west, east, valid, mod, w, kv_own, kv_rim, w_out, control,
    late, dist, key, second, slot, comb, ctl, put,
    out, rest, count, done, hid, qs, bias, attn, sem,
):
    rows = valid_rows(valid, west, east)
    normed = hidden_rows(dot(late[...], latent[...]), mod)
    for g in (0, 1):
        hid[g * LATE_ROWS : (g + 1) * LATE_ROWS] = normed[g]
    asked = dot(hid[...], w[:, :D]).astype(BF)
    for g in (0, 1):
        qs[g, :LATE_ROWS] = asked[g * LATE_ROWS : (g + 1) * LATE_ROWS]
        qs[g, LATE_ROWS:] = jnp.zeros((128 - LATE_ROWS, D), BF)
    fill_bias(bias, 0, dist[0], key[0, 0], key[0, 1], second[0], rows[2], rows[3])
    keys = inner_window(kv_own, kv_rim, 0, 1, 5)
    values = inner_window(kv_own, kv_rim, 1, 1, 5)

    def keep(g, lines, o):
        attn[g, lines, :] = o

    attend(
        lambda g, lanes: qs[g, :, lanes],
        lambda g, lanes: jnp.concatenate(keys(g, lanes), axis=0),
        lambda g, lanes: jnp.concatenate(values(g, lanes), axis=0),
        lambda r: bias[0, r],
        radius,
        keep,
    )
    extra = sum(dot((ctl[tile].astype(F32) * rows[tile + 1]).astype(BF), control[tile]) for tile in range(4))
    x = latent[...].astype(F32)
    sums, number = block_sums(
        (((1, 3), attn_mid), ((0, 4), attn_edge), ((2,), attn)), rows, x, w_out, mod, west, east, slot, comb, extra, put
    )
    done[...] = (sums[64:192] / number[64:192]).astype(BF)
    copy = pltpu.make_async_copy(done, out.at[pl.ds(64, 128)], sem)
    copy.start()
    rest[0] = sums[:64]
    rest[1] = sums[192:]
    count[0] = jnp.broadcast_to(number[:64], (64, 128))
    count[1] = jnp.broadcast_to(number[192:], (64, 128))
    copy.wait()


def final_kernel(rest, count, above, below, whole_out, out, done, sem):
    del whole_out
    row = lax.broadcasted_iota(jnp.int32, (64, 128), 0)
    lane = lax.broadcasted_iota(jnp.int32, (64, 128), 1)
    copies = []
    for i, ref in ((0, above), (1, below)):
        tail = ref[64:80, :128].astype(F32)[:1]
        number = jnp.sum(jnp.where(row == lane, tail, 0.0), axis=1, keepdims=True) + count[i][:, :1]
        done[i] = ((rest[i] + ref[:64].astype(F32)) / number).astype(BF)
        copies.append(pltpu.make_async_copy(done.at[i], out.at[pl.ds(192 * i, 64)], sem.at[i]))
        copies[i].start()
    for copy in copies:
        copy.wait()


def call(kernel, outs, args, specs=None, out_specs=None, scratch=(), cost=(1e9, 4e6), aliases=None, limit=VMEM):
    specs = specs or {}
    out_specs = out_specs or {}
    vmem = pl.BlockSpec(memory_space=pltpu.VMEM)
    return pl.pallas_call(
        kernel,
        out_shape=outs,
        in_specs=[specs.get(i, vmem) for i in range(len(args))],
        out_specs=[out_specs.get(i, vmem) for i in range(len(outs))],
        scratch_shapes=scratch,
        input_output_aliases=aliases or {},
        compiler_params=pltpu.CompilerParams(vmem_limit_bytes=limit),
        cost_estimate=pl.CostEstimate(flops=int(cost[0]), bytes_accessed=int(cost[1]), transcendentals=0),
    )(*[jnp.asarray(a) for a in args])


def shape(*dims, dtype=BF):
    return jax.ShapeDtypeStruct(dims, dtype)


def local(latent, control, valid, radius, modulation, w_qkv, w_out):
    t = tables()
    size_r, size_c = lax.axis_size("trow"), lax.axis_size("tcol")
    later_r = [(i, (i + 1) % size_r) for i in range(size_r)]
    sooner_r = [((i + 1) % size_r, i) for i in range(size_r)]
    later_c = [(i, (i + 1) % size_c) for i in range(size_c)]
    sooner_c = [((i + 1) % size_c, i) for i in range(size_c)]

    x = latent.reshape(256, D)
    control = control.reshape(4, TILE_TOK, D)
    valid = valid.reshape(4, TILE_TOK)
    above = lax.ppermute(x[192:], "trow", later_r)
    below = lax.ppermute(x[:64], "trow", sooner_r)
    smem = pl.BlockSpec(memory_space=pltpu.SMEM)
    hbm = pl.BlockSpec(memory_space=pl.ANY)

    mod = modulation.transpose(1, 0, 2)
    far = lambda a: pltpu.with_memory_space_constraint(jnp.asarray(a), pltpu.MemorySpace.HBM)
    first = [x, control, valid, mod, w_qkv, t["own"], t["send_own"], t["send_ctl"], t["valid_pad"]]
    staged = [(256, D, BF), (2, TILE_TOK, D, BF), (4, TILE_TOK, jnp.int32), (3, 2, D, F32)]
    staged += [t[k].shape + (BF,) for k in ("own", "send_own", "send_ctl", "valid_pad")]
    kv_own, msg, w = call(
        own_kernel,
        [shape(2, 2, 7, 32, D), shape(2, 96, D), shape(D, 3 * D)],
        [far(a) for a in first],
        specs={i: hbm for i in range(len(first))},
        scratch=[pltpu.VMEM(s[:-1], s[-1]) for s in staged]
        + [pltpu.VMEM((448, D), BF), pltpu.SemaphoreType.DMA((12,))],
        cost=(3.6e9, 12e6),
    )
    to_west, to_east = call(
        pack_kernel, [shape(96, D), shape(96, D)], [msg, above, below, t["send_rim"]], cost=(1e8, 1e6)
    )
    west = lax.ppermute(to_east, "tcol", later_c)
    east = lax.ppermute(to_west, "tcol", sooner_c)

    mid, ends, late = slice(1, 4, 2), slice(0, 5, 4), slice(2, 3)
    kv_rim, attn_mid = call(
        middle_kernel,
        [shape(2, 2, 7, 16, D), shape(2, D, 256)],
        [
            radius, x, above, below, valid, mod, w, kv_own,
            t["middle"], t["dist_mid"], t["key_mid"], t["second"][mid],
        ],
        specs={0: smem},
        scratch=[
            pltpu.VMEM((384, D), BF),
            pltpu.VMEM((736, D), BF),
            pltpu.VMEM((2, 2, 128, D), BF),
            pltpu.VMEM((2, 5, KEYS, 128), F32),
        ],
        cost=(8e9, 14e6),
    )
    up, down, attn_edge = call(
        edge_kernel,
        [shape(80, D), shape(80, D), shape(2, D, 256)],
        [
            radius, x, above, below, west, east, valid, mod, w, kv_own, kv_rim, attn_mid, w_out, control,
            t["edge"], t["dist_edge"], t["key_edge"], t["second"][ends], t["slot"], t["comb_rim"], t["ctl_rim"], t["ctl_pick"], t["put_rim"],
        ],
        specs={0: smem},
        scratch=[
            pltpu.VMEM((2, 256, D), BF),
            pltpu.VMEM((896, D), BF),
            pltpu.VMEM((2, 2, 128, D), BF),
            pltpu.VMEM((2, 2, 4, 48, D), BF),
            pltpu.VMEM((2, 5, KEYS, 128), F32),
        ],
        cost=(1e10, 16e6),
    )
    got_below = lax.ppermute(up, "trow", sooner_r)
    got_above = lax.ppermute(down, "trow", later_r)
    out, rest, count = call(
        core_kernel,
        [shape(256, D), shape(2, 64, D, dtype=F32), shape(2, 64, 128, dtype=F32)],
        [
            radius, attn_mid, attn_edge, x, west, east, valid, mod, w, kv_own, kv_rim, w_out, control,
            t["late"], t["dist_late"], t["key_late"], t["second"][late], t["slot"], t["comb_core"], t["ctl_core"], t["put_core"],
        ],
        specs={0: smem},
        out_specs={0: hbm},
        scratch=[
            pltpu.VMEM((128, D), BF),
            pltpu.VMEM((2 * LATE_ROWS, D), BF),
            pltpu.VMEM((2, 128, D), BF),
            pltpu.VMEM((1, 5, LATE_KEYS, 128), F32),
            pltpu.VMEM((2, D, 128), BF),
            pltpu.SemaphoreType.DMA,
        ],
        cost=(4e9, 8e6),
    )
    (out,) = call(
        final_kernel,
        [shape(256, D)],
        [rest, count, got_above, got_below, out],
        specs={4: hbm},
        out_specs={0: hbm},
        scratch=[pltpu.VMEM((2, 64, D), BF), pltpu.SemaphoreType.DMA((2,))],
        aliases={4: 0},
        cost=(2e8, 3e6),
    )
    return out.reshape(CORE, 32, D)


def solution(mesh):
    placed = (
        P("trow", "tcol", None),
        P("trow", "tcol", None, None),
        P("trow", "tcol", None),
        P(),
        P(),
        P(),
        P(),
    )
    return jax.shard_map(
        local, mesh=mesh, in_specs=placed, out_specs=P("trow", "tcol", None), check_vma=False
    )
```

```python
import functools

import jax
import jax.numpy as jnp
import numpy as np
from jax import lax
from jax.experimental import pallas as pl
from jax.experimental.pallas import tpu as pltpu
from jax.sharding import PartitionSpec as P

D = 1152
HEADS = 16
HEAD_DIM = 72
CORE = 8
MARGIN = 2
SIDE = 12
TILE_TOK = 144
GUIDE = 4.5
REACH = 5
FAR = 99.0
BF = jnp.bfloat16
F32 = jnp.float32
EXP_SCALE = float(np.log2(np.e) / np.sqrt(72.0))
VMEM = 28 * 1024 * 1024

JR = np.array([j // 4 if j < 32 else (j - 40) // 4 if j < 40 else 8 + (j - 40) // 4 for j in range(48)])
JC = np.arange(48) % 4
FIRST = (-1, 1, 2, 4, 6)
COUNT = (4, 4, 5, 4, 4)
KEYS = 192
LATE_KEYS = 240
LATE_ROWS = 80
GROUP = 4


def one_hot(rows, depth):
    hot = np.zeros((len(rows), depth), np.float32)
    for i, src in enumerate(rows):
        if src is not None:
            hot[i, src] = 1.0
    return hot


def source(row, col):
    if col < 0:
        return 384 + (row + 2) * REACH + col + REACH if col >= -REACH else None
    if col >= 32:
        return 480 + (row + 2) * REACH + col - 32 if col < 32 + REACH else None
    return natural(row, col)


def beside(side, row, col):
    if col < 0 or col >= 32:
        place = source(row, col)
        return None if place is None else 192 + place - (384 if side == 0 else 480)
    line = row if 0 <= row < 8 else row + 10 if row < 0 else row + 2
    return line * 16 + col - 16 * side


def natural(row, col):
    if row < 0:
        return 256 + (row + 2) * 32 + col
    if row >= 8:
        return 320 + (row - 8) * 32 + col
    return row * 32 + col


def block_tokens(block):
    return [(int(r), int(4 * block - 2 + c)) for r, c in zip(JR, JC)]


def unit_queries(unit):
    entries = [(-1, 0), (-1, 1)]
    for t in range(4):
        entries += [(t, c) for c in range(max(8 * t - 2, 0), min(8 * t + 10, 32))]
    entries += [(4, 30), (4, 31)]
    flat = [(t, r, c) for t, c in entries for r in range(-2, 10)]
    left, right = flat[126:288], flat[288:450]
    rim = [[q for q in half if not 0 <= q[1] < CORE] for half in (left, right)]
    core = [[q for q in half if 0 <= q[1] < CORE] for half in (left, right)]
    units = [flat[:126], rim[0] + core[0][:74], core[0][74:] + core[1][:34], rim[1] + core[1][34:], flat[450:]]
    assert sum(len(u) for u in units) == 576
    return units[unit] + [None] * (128 - len(units[unit]))


def unit_keys(unit):
    return [p for b in range(FIRST[unit], FIRST[unit] + COUNT[unit]) for p in block_tokens(b)]


def tile_token(tile, row, col):
    r, c = row + 2, col - 8 * tile + 2
    return r * SIDE + c if 0 <= r < SIDE and 0 <= c < SIDE else None


def distances(unit):
    dist = np.full((48 * COUNT[unit], 128), FAR, np.float32)
    for i, query in enumerate(unit_queries(unit)):
        for k, key in enumerate(unit_keys(unit)):
            if query is not None and -REACH <= key[1] < 32 + REACH and tile_token(query[0], *key) is not None:
                dist[k, i] = max(abs(query[1] - key[0]), abs(query[2] - key[1]))
    return dist


@functools.cache
def tables():
    bf = lambda a: np.asarray(a, jnp.bfloat16)
    t = {}
    t["own"] = bf(one_hot([source(*p) for b in range(1, 8) for p in block_tokens(b)[:32]], 256))
    rim = one_hot([source(*p) for b in range(1, 8) for p in block_tokens(b)[32:]], 384)
    queries = [[None if q is None else source(*q[1:]) for q in unit_queries(u)] for u in range(5)]
    middle = np.concatenate([rim, one_hot(queries[1] + queries[3], 384)])
    t["middle"] = bf(middle)
    t["edge"] = bf(
        np.stack(
            [
                one_hot([beside(i, *p) for b in blocks for p in block_tokens(b)], 256).tolist()
                + one_hot([None if q is None else beside(i, *q[1:]) for q in unit_queries(u)], 256).tolist()
                for i, (blocks, u) in enumerate((((-1, 0), 0), ((8, 9), 4)))
            ]
        )
    )
    t["late"] = bf(one_hot(queries[2][:LATE_ROWS], 256))
    for name, members in (("edge", (0, 4)), ("mid", (1, 3)), ("late", (2,))):
        t["dist_" + name] = bf(np.stack([distances(u) for u in members]))
        t["key_" + name] = bf(
            np.stack([[one_hot([tile_token(u + k, *p) for p in unit_keys(u)], TILE_TOK) for k in (-1, 0)] for u in members])
        )
    slot = np.zeros((5, 2, TILE_TOK, 128), np.float32)
    comb = np.zeros((5, 384, 128), np.float32)
    second = np.zeros((5, 1, 128), np.float32)
    for u in range(5):
        for i, q in enumerate(unit_queries(u)):
            if q is not None:
                which = q[0] - u + 1
                assert which in (0, 1)
                slot[u, which, tile_token(*q), i] = 1.0
                second[u, 0, i] = which
                comb[u, natural(*q[1:]), i] = 1.0
    t["slot"], t["second"] = bf(slot), second
    t["comb_core"], t["comb_rim"] = bf(comb[:, :256]), bf(comb[:, 256:])
    send = np.zeros((2, 64, 384), np.float32)
    send_ctl = np.zeros((2, 32, TILE_TOK), np.float32)
    put = np.zeros((2, 384, 32), np.float32)
    for r in range(SIDE):
        for k in range(REACH):
            send[0, r * REACH + k, source(r - 2, k)] = 1.0
            send[1, r * REACH + k, source(r - 2, 32 - REACH + k)] = 1.0
        for k in range(2):
            send_ctl[0, r * 2 + k, r * SIDE + k] = 1.0
            send_ctl[1, r * 2 + k, r * SIDE + 10 + k] = 1.0
            put[0, natural(r - 2, k), r * 2 + k] = 1.0
            put[1, natural(r - 2, 30 + k), r * 2 + k] = 1.0
    t["send_own"], t["send_rim"], t["send_ctl"] = bf(send[:, :, :256]), bf(send[:, :, 256:]), bf(send_ctl)
    put = np.concatenate([put[0], put[1]], axis=1)
    t["put_core"], t["put_rim"] = bf(put[:256]), bf(put[256:])
    t["valid_pad"] = bf(np.eye(TILE_TOK, 256))
    ctl = np.zeros((4, 384, TILE_TOK), np.float32)
    for tile in range(4):
        for r in range(-2, 10):
            for c in range(max(8 * tile - 2, 0), min(8 * tile + 10, 32)):
                ctl[tile, natural(r, c), tile_token(tile, r, c)] = 1.0
    t["ctl_core"] = bf(ctl[:, :256])
    ends = [np.r_[0:32, 112:144] for _ in range(4)]
    t["ctl_rim"] = bf(np.concatenate([ctl[i, 256:][:, e] for i, e in enumerate(ends)], axis=1))
    t["ctl_pick"] = bf(
        np.stack([np.concatenate([np.eye(TILE_TOK)[:, e] * (i == k) for k, e in enumerate(ends)], axis=1) for i in range(4)])
    )
    return t


def dot(a, b):
    return jnp.dot(a, b, preferred_element_type=F32)


def dot_nt(a, b):
    return lax.dot_general(a, b, (((1,), (1,)), ((), ())), preferred_element_type=F32)


def hidden_rows(x, mod_ref):
    mean = jnp.mean(x, axis=-1, keepdims=True)
    centred = x - mean
    var = jnp.mean(centred * centred, axis=-1, keepdims=True)
    normed = centred * lax.rsqrt(var + 1e-6)
    return [(normed * (1.0 + mod_ref[1, g : g + 1, :]) + mod_ref[0, g : g + 1, :]).astype(BF) for g in (0, 1)]


def eight(row):
    return jnp.broadcast_to(row, (8, row.shape[1])).astype(BF)


def fill_bias(bias_ref, unit, dist, key_a, key_b, second, valid_a, valid_b):
    usable_a, usable_b = dot_nt(key_a, eight(valid_a))[:, :1], dot_nt(key_b, eight(valid_b))[:, :1]
    dist = dist.astype(F32)
    usable = (jnp.where(second > 0.5, usable_b, usable_a) > 0.5) | (dist == 0.0)
    dist = jnp.where(usable, dist, FAR)
    for r in range(5):
        bias_ref[unit, r] = jnp.where(dist <= r + 1.0, 0.0, -1e30)


def attend(queries, keys, values, bias, radius_ref, put):
    lane = lax.broadcasted_iota(jnp.int32, (1, 256), 1)

    def score(g, p):
        lanes = slice(128 * p, 128 * p + 256)
        q = queries(g, lanes)
        both = [
            q * ((lane >= 16 * p + at) & (lane < 16 * p + at + HEAD_DIM)).astype(F32).astype(BF) for at in (0, HEAD_DIM)
        ]
        return dot_nt(keys(g, lanes), jnp.concatenate(both, axis=0))

    def soften(p, scores):
        exps, scales = [], []
        for i in (0, 1):
            s = scores[:, 128 * i : 128 * i + 128] + bias(radius_ref[2 * p + i] - 1)
            top = jnp.max(s, axis=0, keepdims=True)
            e = jnp.exp2((s - top) * EXP_SCALE)
            scales.append(1.0 / jnp.sum(e, axis=0, keepdims=True))
            exps.append(e)
        return jnp.concatenate(exps, axis=1).astype(BF), scales

    def collect(g, p, e, scales):
        v = values(g, slice(128 * p, 128 * p + 256)).T[16 * p : 16 * p + 144]
        o = dot(v, e)
        o = jnp.concatenate([o[:72, :128] * scales[0], o[72:, 128:] * scales[1]], axis=0)
        put(g, slice(144 * p, 144 * p + 144), o.astype(BF))

    items = [(g, p) for g in (0, 1) for p in range(8)]
    scores = {k: score(*items[k]) for k in range(GROUP)}
    probs = {}
    for k in range(len(items) + GROUP):
        if k + GROUP < len(items):
            scores[k + GROUP] = score(*items[k + GROUP])
        if k < len(items):
            probs[k] = soften(items[k][1], scores.pop(k))
        if k >= GROUP:
            collect(*items[k - GROUP], *probs.pop(k - GROUP))


def inner_window(own, rim, c, first, count):
    def get(g, lanes):
        parts = []
        for i in range(count):
            parts += [own[c, g, first + i, :, lanes], rim[c, g, first + i, :, lanes]]
        return parts

    return get


def own_kernel(
    latent_h, control_h, valid_h, mod_h, w_h, own_h, send_own_h, send_ctl_h, valid_pad_h,
    kv, msg, w, latent, control, valid, mod, own, send_own, send_ctl, valid_pad, hid, sem,
):
    pairs = [
        (latent_h, latent),
        (own_h, own),
        (mod_h, mod),
        (w_h.at[:, pl.ds(D, D)], w.at[:, pl.ds(D, D)]),
        (w_h.at[:, pl.ds(2 * D, D)], w.at[:, pl.ds(2 * D, D)]),
        (control_h.at[pl.ds(0, 1)], control.at[pl.ds(0, 1)]),
        (control_h.at[pl.ds(3, 1)], control.at[pl.ds(1, 1)]),
        (valid_h, valid),
        (send_own_h, send_own),
        (send_ctl_h, send_ctl),
        (valid_pad_h, valid_pad),
        (w_h.at[:, pl.ds(0, D)], w.at[:, pl.ds(0, D)]),
    ]
    copies = [pltpu.make_async_copy(src, dst, sem.at[i]) for i, (src, dst) in enumerate(pairs)]
    for copy in copies:
        copy.start()
    for copy in copies[:3]:
        copy.wait()
    rows = hidden_rows(dot(own[...], latent[...]), mod)
    hid[:224] = rows[0]
    hid[224:] = rows[1]
    for c in (0, 1):
        copies[3 + c].wait()
        out = dot(hid[...], w[:, (c + 1) * D : (c + 2) * D])
        kv[c] = out.astype(BF).reshape(2, 7, 32, D)
    for copy in copies[5:]:
        copy.wait()
    rows = lax.broadcasted_iota(jnp.int32, (32, 1), 0)
    val = valid[...].astype(F32)
    for i, tile, rim in ((0, 0, 2 * SIDE + 1), (1, 3, 2 * SIDE + 10)):
        msg[i, :64] = dot(send_own[i], latent[...]).astype(BF)
        own_row = val[tile : tile + 1]
        ctl = dot((send_ctl[i].astype(F32) * own_row).astype(BF), control[i])
        row = dot(eight(own_row * own_row[:, rim : rim + 1]), valid_pad[...])
        msg[i, 64:, 256:] = ctl[:, 256:].astype(BF)
        msg[i, 64:, :256] = jnp.where(rows == 31, row[0:1], ctl[:, :256]).astype(BF)


def choose(odd, a, b):
    return jnp.where(odd > 0.5, a.astype(F32), b.astype(F32))


def pack_kernel(odd, msg, got_a, got_b, send_rim, out_a, out_b, above, below):
    row_odd, col_odd = odd[0][:1, :1], odd[1][:1, :1]
    above[...] = choose(row_odd, got_a[...], got_b[...]).astype(BF)
    below[...] = choose(row_odd, got_b[...], got_a[...]).astype(BF)
    messages = []
    for i in (0, 1):
        rim = dot(send_rim[i, :, :64], above[...]) + dot(send_rim[i, :, 64:], below[...])
        messages.append(msg[i, :64].astype(F32) + rim)
    out_a[:64] = choose(col_odd, messages[0], messages[1]).astype(BF)
    out_b[:64] = choose(col_odd, messages[1], messages[0]).astype(BF)
    out_a[64:] = choose(col_odd, msg[0, 64:], msg[1, 64:]).astype(BF)
    out_b[64:] = choose(col_odd, msg[1, 64:], msg[0, 64:]).astype(BF)


def middle_kernel(
    radius, latent, above, below, valid, mod, w, kv_own, middle, dist, key, second, kv_rim, attn, near, hid, qs, bias
):
    near[:256] = latent[...]
    near[256:320] = above[...]
    near[320:] = below[...]
    rows = hidden_rows(dot(middle[...], near[...]), mod)
    for g in (0, 1):
        hid[g * 112 : (g + 1) * 112] = rows[g][:112]
        hid[224 + g * 256 : 224 + (g + 1) * 256] = rows[g][112:]
    qs[...] = dot(hid[224:], w[:, :D]).astype(BF).reshape(2, 2, 128, D)
    out = dot(hid[:224], w[:, D:]).astype(BF)
    for c in (0, 1):
        kv_rim[c] = out[:, c * D : (c + 1) * D].reshape(2, 7, 16, D)
    val = valid[...].astype(F32)
    for i in (0, 1):
        fill_bias(bias, i, dist[i], key[i, 0], key[i, 1], second[i], val[2 * i : 2 * i + 1], val[2 * i + 1 : 2 * i + 2])

    for i in (0, 1):
        keys = inner_window(kv_own, kv_rim, 0, 3 * i, 4)
        values = inner_window(kv_own, kv_rim, 1, 3 * i, 4)

        def put(g, rows, o):
            attn[g, rows, 128 * i : 128 * i + 128] = o

        attend(
            lambda g, lanes: qs[g, i, :, lanes],
            lambda g, lanes: jnp.concatenate(keys(g, lanes), axis=0),
            lambda g, lanes: jnp.concatenate(values(g, lanes), axis=0),
            lambda r: bias[i, r],
            radius,
            put,
        )


def valid_rows(valid, west, east):
    val = valid[...].astype(F32)
    side = [ref[80:96, :256].astype(F32)[15:16, :TILE_TOK] for ref in (west, east)]
    return [side[0]] + [val[t : t + 1] for t in range(4)] + [side[1]]


def gather(unit, slot, comb, rows):
    weight = dot(eight(rows[unit]), slot[unit, 0]) + dot(eight(rows[unit + 1]), slot[unit, 1])
    return comb[unit].astype(F32) * weight[:1]


def block_sums(parts, rows, x, w_out, mod, west, east, slot, comb, ctl, put):
    weights = {u: gather(u, slot, comb, rows) for units, _ in parts for u in units}
    number = sum(jnp.sum(w, axis=1, keepdims=True) for w in weights.values())
    n = number.shape[0]
    attn = [0.0, 0.0]
    for units, ref in parts:
        weight = jnp.concatenate([weights[u] for u in units], axis=1).astype(BF)
        attn = [attn[g] + dot_nt(weight, ref[g]) for g in (0, 1)]
    attn = [a.astype(BF) for a in attn]
    proj = dot(jnp.concatenate(attn, axis=0), w_out[...])
    sums = (GUIDE * mod[2, 0:1]) * proj[:n] + ((1.0 - GUIDE) * mod[2, 1:2]) * proj[n:] + number * x
    return sums + ctl + dot(put[...], jnp.concatenate([west[64:], east[64:]], axis=0)), number


def edge_kernel(
    radius, odd, latent, above, below, got_a, got_b, valid, mod, w, kv_own, kv_rim, attn_mid, w_out, control,
    edge, dist, key, second, slot, comb, ctl, ctl_pick, put_ctl,
    out_a, out_b, attn, west, east, near, hid, qs, kv, bias,
):
    row_odd, col_odd = odd[0] == 1, odd[1] == 1
    west[...] = jnp.where(col_odd, got_a[...], got_b[...])
    east[...] = jnp.where(col_odd, got_b[...], got_a[...])
    parts = []
    for i, message in ((0, west), (1, east)):
        at = 0
        for ref, lines in ((latent, 8), (above, 2), (below, 2)):
            for line in range(lines):
                near[i, at : at + 16] = ref[32 * line + 16 * i : 32 * line + 16 * i + 16]
                at += 16
        near[i, at:] = message[:64]
        parts.append(dot(edge[i], near[i]))
    x = jnp.concatenate([p[:96] for p in parts] + [p[96:] for p in parts], axis=0)
    normed = hidden_rows(x, mod)
    for g in (0, 1):
        hid[g * 192 : (g + 1) * 192] = normed[g][:192]
        hid[384 + g * 256 : 384 + (g + 1) * 256] = normed[g][192:]
    qs[...] = dot(hid[384:], w[:, :D]).astype(BF).reshape(2, 2, 128, D)
    out = dot(hid[:384], w[:, D:]).astype(BF)
    for c in (0, 1):
        kv[c] = out[:, c * D : (c + 1) * D].reshape(2, 4, 48, D)
    rows = valid_rows(valid, west, east)
    for i, u in ((0, 0), (1, 4)):
        fill_bias(bias, i, dist[i], key[i, 0], key[i, 1], second[i], rows[u], rows[u + 1])

    for i in (0, 1):

        def window(c):
            inner = inner_window(kv_own, kv_rim, c, 5 * i, 2)

            def get(g, lanes):
                outer = [kv[c, g, 2 * i, :, lanes], kv[c, g, 2 * i + 1, :, lanes]]
                parts = inner(g, lanes) + outer if i else outer + inner(g, lanes)
                return jnp.concatenate(parts, axis=0)

            return get

        def put(g, rows, o):
            attn[g, rows, 128 * i : 128 * i + 128] = o

        attend(lambda g, lanes: qs[g, i, :, lanes], window(0), window(1), lambda r: bias[i, r], radius, put)

    x = jnp.concatenate([above[...], below[...]], axis=0).astype(F32)
    weight = sum(dot(eight(rows[tile + 1]), ctl_pick[tile]) for tile in range(4))[:1]
    ends = [control[tile, at : at + 32] for tile in range(4) for at in (0, 112)]
    extra = dot((ctl[...].astype(F32) * weight).astype(BF), jnp.concatenate(ends, axis=0))
    sums, number = block_sums((((1, 3), attn_mid), ((0, 4), attn)), rows, x, w_out, mod, west, east, slot, comb, extra, put_ctl)
    row = lax.broadcasted_iota(jnp.int32, (64, 128), 0)
    lane = lax.broadcasted_iota(jnp.int32, (64, 128), 1)
    tails = []
    for at in (0, 64):
        tails.append(jnp.sum(jnp.where(row == lane, number[at : at + 64], 0.0), axis=0, keepdims=True))
    for out, upward in ((out_a, row_odd), (out_b, jnp.logical_not(row_odd))):
        out[:64] = jnp.where(upward, sums[:64], sums[64:]).astype(BF)
        out[64:, :128] = jnp.broadcast_to(jnp.where(upward, tails[0], tails[1]), (16, 128)).astype(BF)
        out[64:, 128:] = jnp.zeros((16, D - 128), BF)


def core_kernel(
    radius, attn_mid, attn_edge, latent, west, east, valid, mod, w, kv_own, kv_rim, w_out, control,
    late, dist, key, second, slot, comb, ctl, put,
    out, rest, count, done, hid, qs, bias, attn, sem,
):
    rows = valid_rows(valid, west, east)
    normed = hidden_rows(dot(late[...], latent[...]), mod)
    for g in (0, 1):
        hid[g * LATE_ROWS : (g + 1) * LATE_ROWS] = normed[g]
    asked = dot(hid[...], w[:, :D]).astype(BF)
    for g in (0, 1):
        qs[g, :LATE_ROWS] = asked[g * LATE_ROWS : (g + 1) * LATE_ROWS]
        qs[g, LATE_ROWS:] = jnp.zeros((128 - LATE_ROWS, D), BF)
    fill_bias(bias, 0, dist[0], key[0, 0], key[0, 1], second[0], rows[2], rows[3])
    keys = inner_window(kv_own, kv_rim, 0, 1, 5)
    values = inner_window(kv_own, kv_rim, 1, 1, 5)

    def keep(g, lines, o):
        attn[g, lines, :] = o

    attend(
        lambda g, lanes: qs[g, :, lanes],
        lambda g, lanes: jnp.concatenate(keys(g, lanes), axis=0),
        lambda g, lanes: jnp.concatenate(values(g, lanes), axis=0),
        lambda r: bias[0, r],
        radius,
        keep,
    )
    extra = sum(dot((ctl[tile].astype(F32) * rows[tile + 1]).astype(BF), control[tile]) for tile in range(4))
    x = latent[...].astype(F32)
    sums, number = block_sums(
        (((1, 3), attn_mid), ((0, 4), attn_edge), ((2,), attn)), rows, x, w_out, mod, west, east, slot, comb, extra, put
    )
    done[...] = (sums[64:192] / number[64:192]).astype(BF)
    copy = pltpu.make_async_copy(done, out.at[pl.ds(64, 128)], sem)
    copy.start()
    rest[0] = sums[:64]
    rest[1] = sums[192:]
    count[0] = jnp.broadcast_to(number[:64], (64, 128))
    count[1] = jnp.broadcast_to(number[192:], (64, 128))
    copy.wait()


def final_kernel(odd, rest, count, got_a, got_b, whole_out, out, done, sem):
    del whole_out
    row = lax.broadcasted_iota(jnp.int32, (64, 128), 0)
    lane = lax.broadcasted_iota(jnp.int32, (64, 128), 1)
    copies = []
    for i in (0, 1):
        first, second = (got_a, got_b) if i == 0 else (got_b, got_a)
        got = choose(odd[0][:1, :1], first[...], second[...])
        tail = got[64:65, :128]
        number = jnp.sum(jnp.where(row == lane, tail, 0.0), axis=1, keepdims=True) + count[i][:, :1]
        done[i] = ((rest[i] + got[:64]) / number).astype(BF)
        copies.append(pltpu.make_async_copy(done.at[i], out.at[pl.ds(192 * i, 64)], sem.at[i]))
        copies[i].start()
    for copy in copies:
        copy.wait()


def swaps(size_r, size_c, by_row, turn):
    perm = []
    for r in range(size_r):
        for c in range(size_c):
            here, size = (r, size_r) if by_row else (c, size_c)
            there = ((here + turn) ^ 1) - turn
            if 0 <= there < size:
                to = (there, c) if by_row else (r, there)
            else:
                to = (r, min(c ^ 1, size_c - 1)) if by_row else (min(r ^ 1, size_r - 1), c)
            perm.append((r * size_c + c, to[0] * size_c + to[1]))
    return perm


def call(kernel, outs, args, specs=None, out_specs=None, scratch=(), cost=(1e9, 4e6), aliases=None, limit=VMEM):
    specs = specs or {}
    out_specs = out_specs or {}
    vmem = pl.BlockSpec(memory_space=pltpu.VMEM)
    return pl.pallas_call(
        kernel,
        out_shape=outs,
        in_specs=[specs.get(i, vmem) for i in range(len(args))],
        out_specs=[out_specs.get(i, vmem) for i in range(len(outs))],
        scratch_shapes=scratch,
        input_output_aliases=aliases or {},
        compiler_params=pltpu.CompilerParams(vmem_limit_bytes=limit),
        cost_estimate=pl.CostEstimate(flops=int(cost[0]), bytes_accessed=int(cost[1]), transcendentals=0),
    )(*[jnp.asarray(a) for a in args])


def shape(*dims, dtype=BF):
    return jax.ShapeDtypeStruct(dims, dtype)


def local(latent, control, valid, radius, modulation, w_qkv, w_out):
    t = tables()
    size_r, size_c = lax.axis_size("trow"), lax.axis_size("tcol")
    x = latent.reshape(256, D)
    control = control.reshape(4, TILE_TOK, D)
    valid = valid.reshape(4, TILE_TOK)
    row, col = lax.axis_index("trow") % 2, lax.axis_index("tcol") % 2
    odd = jnp.stack([row, col]).astype(jnp.int32)
    mark = jnp.broadcast_to(odd.astype(F32)[:, None, None], (2, 8, 128))
    axes = ("trow", "tcol")
    by_row = [swaps(size_r, size_c, True, turn) for turn in (0, 1)]
    by_col = [swaps(size_r, size_c, False, turn) for turn in (0, 1)]
    near_a = lax.ppermute(lax.dynamic_slice_in_dim(x, 192 * (1 - row), 64, 0), axes, by_row[0])
    near_b = lax.ppermute(lax.dynamic_slice_in_dim(x, 192 * row, 64, 0), axes, by_row[1])
    smem = pl.BlockSpec(memory_space=pltpu.SMEM)
    hbm = pl.BlockSpec(memory_space=pl.ANY)

    mod = modulation.transpose(1, 0, 2)
    far = lambda a: pltpu.with_memory_space_constraint(jnp.asarray(a), pltpu.MemorySpace.HBM)
    first = [x, control, valid, mod, w_qkv, t["own"], t["send_own"], t["send_ctl"], t["valid_pad"]]
    staged = [(256, D, BF), (2, TILE_TOK, D, BF), (4, TILE_TOK, jnp.int32), (3, 2, D, F32)]
    staged += [t[k].shape + (BF,) for k in ("own", "send_own", "send_ctl", "valid_pad")]
    kv_own, msg, w = call(
        own_kernel,
        [shape(2, 2, 7, 32, D), shape(2, 96, D), shape(D, 3 * D)],
        [far(a) for a in first],
        specs={i: hbm for i in range(len(first))},
        scratch=[pltpu.VMEM(s[:-1], s[-1]) for s in staged]
        + [pltpu.VMEM((448, D), BF), pltpu.SemaphoreType.DMA((12,))],
        cost=(3.6e9, 12e6),
    )
    side_a, side_b, above, below = call(
        pack_kernel,
        [shape(96, D), shape(96, D), shape(64, D), shape(64, D)],
        [mark, msg, near_a, near_b, t["send_rim"]],
        cost=(1e8, 1e6),
    )
    side_a = lax.ppermute(side_a, axes, by_col[0])
    side_b = lax.ppermute(side_b, axes, by_col[1])

    mid, ends, late = slice(1, 4, 2), slice(0, 5, 4), slice(2, 3)
    kv_rim, attn_mid = call(
        middle_kernel,
        [shape(2, 2, 7, 16, D), shape(2, D, 256)],
        [
            radius, x, above, below, valid, mod, w, kv_own,
            t["middle"], t["dist_mid"], t["key_mid"], t["second"][mid],
        ],
        specs={0: smem},
        scratch=[
            pltpu.VMEM((384, D), BF),
            pltpu.VMEM((736, D), BF),
            pltpu.VMEM((2, 2, 128, D), BF),
            pltpu.VMEM((2, 5, KEYS, 128), F32),
        ],
        cost=(8e9, 14e6),
    )
    sums_a, sums_b, attn_edge, west, east = call(
        edge_kernel,
        [shape(80, D), shape(80, D), shape(2, D, 256), shape(96, D), shape(96, D)],
        [
            radius, odd, x, above, below, side_a, side_b, valid, mod, w, kv_own, kv_rim, attn_mid, w_out, control,
            t["edge"], t["dist_edge"], t["key_edge"], t["second"][ends], t["slot"], t["comb_rim"], t["ctl_rim"], t["ctl_pick"], t["put_rim"],
        ],
        specs={0: smem, 1: smem},
        scratch=[
            pltpu.VMEM((2, 256, D), BF),
            pltpu.VMEM((896, D), BF),
            pltpu.VMEM((2, 2, 128, D), BF),
            pltpu.VMEM((2, 2, 4, 48, D), BF),
            pltpu.VMEM((2, 5, KEYS, 128), F32),
        ],
        cost=(1e10, 16e6),
    )
    sums_a = lax.ppermute(sums_a, axes, by_row[0])
    sums_b = lax.ppermute(sums_b, axes, by_row[1])
    out, rest, count = call(
        core_kernel,
        [shape(256, D), shape(2, 64, D, dtype=F32), shape(2, 64, 128, dtype=F32)],
        [
            radius, attn_mid, attn_edge, x, west, east, valid, mod, w, kv_own, kv_rim, w_out, control,
            t["late"], t["dist_late"], t["key_late"], t["second"][late], t["slot"], t["comb_core"], t["ctl_core"], t["put_core"],
        ],
        specs={0: smem},
        out_specs={0: hbm},
        scratch=[
            pltpu.VMEM((128, D), BF),
            pltpu.VMEM((2 * LATE_ROWS, D), BF),
            pltpu.VMEM((2, 128, D), BF),
            pltpu.VMEM((1, 5, LATE_KEYS, 128), F32),
            pltpu.VMEM((2, D, 128), BF),
            pltpu.SemaphoreType.DMA,
        ],
        cost=(4e9, 8e6),
    )
    (out,) = call(
        final_kernel,
        [shape(256, D)],
        [mark, rest, count, sums_a, sums_b, out],
        specs={5: hbm},
        out_specs={0: hbm},
        scratch=[pltpu.VMEM((2, 64, D), BF), pltpu.SemaphoreType.DMA((2,))],
        aliases={5: 0},
        cost=(2e8, 3e6),
    )
    return out.reshape(CORE, 32, D)


def solution(mesh):
    placed = (
        P("trow", "tcol", None),
        P("trow", "tcol", None, None),
        P("trow", "tcol", None),
        P(),
        P(),
        P(),
        P(),
    )
    return jax.shard_map(
        local, mesh=mesh, in_specs=placed, out_specs=P("trow", "tcol", None), check_vma=False
    )
```

```python
import functools

import jax
import jax.numpy as jnp
import numpy as np
from jax import lax
from jax.experimental import pallas as pl
from jax.experimental.pallas import tpu as pltpu
from jax.sharding import PartitionSpec as P

D = 1152
HEADS = 16
HEAD_DIM = 72
CORE = 8
MARGIN = 2
SIDE = 12
TILE_TOK = 144
GUIDE = 4.5
REACH = 5
FAR = 99.0
BF = jnp.bfloat16
F32 = jnp.float32
EXP_SCALE = float(np.log2(np.e) / np.sqrt(72.0))
VMEM = 28 * 1024 * 1024

JR = np.array([j // 4 if j < 32 else (j - 40) // 4 if j < 40 else 8 + (j - 40) // 4 for j in range(48)])
JC = np.arange(48) % 4
FIRST = (-1, 1, 2, 4, 6)
COUNT = (4, 4, 5, 4, 4)
KEYS = 192
LATE_KEYS = 240
LATE_ROWS = 80
GROUP = 4


def one_hot(rows, depth):
    hot = np.zeros((len(rows), depth), np.float32)
    for i, src in enumerate(rows):
        if src is not None:
            hot[i, src] = 1.0
    return hot


def source(row, col):
    if col < 0:
        return 384 + (row + 2) * REACH + col + REACH if col >= -REACH else None
    if col >= 32:
        return 480 + (row + 2) * REACH + col - 32 if col < 32 + REACH else None
    return natural(row, col)


def beside(side, row, col):
    if col < 0 or col >= 32:
        place = source(row, col)
        return None if place is None else 192 + place - (384 if side == 0 else 480)
    line = row if 0 <= row < 8 else row + 10 if row < 0 else row + 2
    return line * 16 + col - 16 * side


def natural(row, col):
    if row < 0:
        return 256 + (row + 2) * 32 + col
    if row >= 8:
        return 320 + (row - 8) * 32 + col
    return row * 32 + col


def block_tokens(block):
    return [(int(r), int(4 * block - 2 + c)) for r, c in zip(JR, JC)]


def unit_queries(unit):
    entries = [(-1, 0), (-1, 1)]
    for t in range(4):
        entries += [(t, c) for c in range(max(8 * t - 2, 0), min(8 * t + 10, 32))]
    entries += [(4, 30), (4, 31)]
    flat = [(t, r, c) for t, c in entries for r in range(-2, 10)]
    left, right = flat[126:288], flat[288:450]
    rim = [[q for q in half if not 0 <= q[1] < CORE] for half in (left, right)]
    core = [[q for q in half if 0 <= q[1] < CORE] for half in (left, right)]
    units = [flat[:126], rim[0] + core[0][:74], core[0][74:] + core[1][:34], rim[1] + core[1][34:], flat[450:]]
    assert sum(len(u) for u in units) == 576
    return units[unit] + [None] * (128 - len(units[unit]))


def unit_keys(unit):
    return [p for b in range(FIRST[unit], FIRST[unit] + COUNT[unit]) for p in block_tokens(b)]


def tile_token(tile, row, col):
    r, c = row + 2, col - 8 * tile + 2
    return r * SIDE + c if 0 <= r < SIDE and 0 <= c < SIDE else None


def distances(unit):
    dist = np.full((48 * COUNT[unit], 128), FAR, np.float32)
    for i, query in enumerate(unit_queries(unit)):
        for k, key in enumerate(unit_keys(unit)):
            if query is not None and -REACH <= key[1] < 32 + REACH and tile_token(query[0], *key) is not None:
                dist[k, i] = max(abs(query[1] - key[0]), abs(query[2] - key[1]))
    return dist


@functools.cache
def tables():
    bf = lambda a: np.asarray(a, jnp.bfloat16)
    t = {}
    t["own"] = bf(one_hot([source(*p) for b in range(1, 8) for p in block_tokens(b)[:32]], 256))
    rim = one_hot([source(*p) for b in range(1, 8) for p in block_tokens(b)[32:]], 384)
    queries = [[None if q is None else source(*q[1:]) for q in unit_queries(u)] for u in range(5)]
    middle = np.concatenate([rim, one_hot(queries[1] + queries[3], 384)])
    t["middle"] = bf(middle)
    t["edge"] = bf(
        np.stack(
            [
                one_hot([beside(i, *p) for b in blocks for p in block_tokens(b)], 256).tolist()
                + one_hot([None if q is None else beside(i, *q[1:]) for q in unit_queries(u)], 256).tolist()
                for i, (blocks, u) in enumerate((((-1, 0), 0), ((8, 9), 4)))
            ]
        )
    )
    t["late"] = bf(one_hot(queries[2][:LATE_ROWS], 256))
    for name, members in (("edge", (0, 4)), ("mid", (1, 3)), ("late", (2,))):
        t["dist_" + name] = bf(np.stack([distances(u) for u in members]))
        t["key_" + name] = bf(
            np.stack([[one_hot([tile_token(u + k, *p) for p in unit_keys(u)], TILE_TOK) for k in (-1, 0)] for u in members])
        )
    slot = np.zeros((5, 2, TILE_TOK, 128), np.float32)
    comb = np.zeros((5, 384, 128), np.float32)
    second = np.zeros((5, 1, 128), np.float32)
    for u in range(5):
        for i, q in enumerate(unit_queries(u)):
            if q is not None:
                which = q[0] - u + 1
                assert which in (0, 1)
                slot[u, which, tile_token(*q), i] = 1.0
                second[u, 0, i] = which
                comb[u, natural(*q[1:]), i] = 1.0
    t["slot"], t["second"] = bf(slot), second
    t["comb_core"], t["comb_rim"] = bf(comb[:, :256]), bf(comb[:, 256:])
    send = np.zeros((2, 64, 384), np.float32)
    send_ctl = np.zeros((2, 32, TILE_TOK), np.float32)
    put = np.zeros((2, 384, 32), np.float32)
    for r in range(SIDE):
        for k in range(REACH):
            send[0, r * REACH + k, source(r - 2, k)] = 1.0
            send[1, r * REACH + k, source(r - 2, 32 - REACH + k)] = 1.0
        for k in range(2):
            send_ctl[0, r * 2 + k, r * SIDE + k] = 1.0
            send_ctl[1, r * 2 + k, r * SIDE + 10 + k] = 1.0
            put[0, natural(r - 2, k), r * 2 + k] = 1.0
            put[1, natural(r - 2, 30 + k), r * 2 + k] = 1.0
    t["send_own"], t["send_rim"], t["send_ctl"] = bf(send[:, :, :256]), bf(send[:, :, 256:]), bf(send_ctl)
    put = np.concatenate([put[0], put[1]], axis=1)
    t["put_core"], t["put_rim"] = bf(put[:256]), bf(put[256:])
    t["valid_pad"] = bf(np.eye(TILE_TOK, 256))
    ctl = np.zeros((4, 384, TILE_TOK), np.float32)
    for tile in range(4):
        for r in range(-2, 10):
            for c in range(max(8 * tile - 2, 0), min(8 * tile + 10, 32)):
                ctl[tile, natural(r, c), tile_token(tile, r, c)] = 1.0
    t["ctl_core"] = bf(ctl[:, :256])
    ends = [np.r_[0:32, 112:144] for _ in range(4)]
    t["ctl_rim"] = bf(np.concatenate([ctl[i, 256:][:, e] for i, e in enumerate(ends)], axis=1))
    t["ctl_pick"] = bf(
        np.stack([np.concatenate([np.eye(TILE_TOK)[:, e] * (i == k) for k, e in enumerate(ends)], axis=1) for i in range(4)])
    )
    return t


def dot(a, b):
    return jnp.dot(a, b, preferred_element_type=F32)


def dot_nt(a, b):
    return lax.dot_general(a, b, (((1,), (1,)), ((), ())), preferred_element_type=F32)


def hidden_rows(x, mod_ref):
    mean = jnp.mean(x, axis=-1, keepdims=True)
    centred = x - mean
    var = jnp.mean(centred * centred, axis=-1, keepdims=True)
    normed = centred * lax.rsqrt(var + 1e-6)
    return [(normed * (1.0 + mod_ref[1, g : g + 1, :]) + mod_ref[0, g : g + 1, :]).astype(BF) for g in (0, 1)]


def eight(row):
    return jnp.broadcast_to(row, (8, row.shape[1])).astype(BF)


def fill_bias(bias_ref, unit, dist, key_a, key_b, second, valid_a, valid_b):
    usable_a, usable_b = dot_nt(key_a, eight(valid_a))[:, :1], dot_nt(key_b, eight(valid_b))[:, :1]
    dist = dist.astype(F32)
    usable = (jnp.where(second > 0.5, usable_b, usable_a) > 0.5) | (dist == 0.0)
    dist = jnp.where(usable, dist, FAR)
    for r in range(5):
        bias_ref[unit, r] = jnp.where(dist <= r + 1.0, 0.0, -1e30)


def attend(queries, keys, values, bias, radius_ref, put):
    lane = lax.broadcasted_iota(jnp.int32, (1, 256), 1)

    def score(g, p):
        lanes = slice(128 * p, 128 * p + 256)
        q = queries(g, lanes)
        both = [
            q * ((lane >= 16 * p + at) & (lane < 16 * p + at + HEAD_DIM)).astype(F32).astype(BF) for at in (0, HEAD_DIM)
        ]
        return dot_nt(keys(g, lanes), jnp.concatenate(both, axis=0))

    def soften(p, scores):
        exps, scales = [], []
        for i in (0, 1):
            s = scores[:, 128 * i : 128 * i + 128] + bias(radius_ref[2 * p + i] - 1)
            top = jnp.max(s, axis=0, keepdims=True)
            e = jnp.exp2((s - top) * EXP_SCALE)
            scales.append(1.0 / jnp.sum(e, axis=0, keepdims=True))
            exps.append(e)
        return jnp.concatenate(exps, axis=1).astype(BF), scales

    def collect(g, p, e, scales):
        v = values(g, slice(128 * p, 128 * p + 256)).T[16 * p : 16 * p + 144]
        o = dot(v, e)
        o = jnp.concatenate([o[:72, :128] * scales[0], o[72:, 128:] * scales[1]], axis=0)
        put(g, slice(144 * p, 144 * p + 144), o.astype(BF))

    items = [(g, p) for g in (0, 1) for p in range(8)]
    scores = {k: score(*items[k]) for k in range(GROUP)}
    probs = {}
    for k in range(len(items) + GROUP):
        if k + GROUP < len(items):
            scores[k + GROUP] = score(*items[k + GROUP])
        if k < len(items):
            probs[k] = soften(items[k][1], scores.pop(k))
        if k >= GROUP:
            collect(*items[k - GROUP], *probs.pop(k - GROUP))


def inner_window(own, rim, c, first, count):
    def get(g, lanes):
        parts = []
        for i in range(count):
            parts += [own[c, g, first + i, :, lanes], rim[c, g, first + i, :, lanes]]
        return parts

    return get


def own_kernel(
    latent_h, control_h, valid_h, mod_h, w_h, own_h, send_own_h, send_ctl_h, valid_pad_h, mark,
    kv, msg, w, odd, latent, control, valid, mod, own, send_own, send_ctl, valid_pad, hid, sem,
):
    odd[...] = mark[...]
    pairs = [
        (latent_h, latent),
        (own_h, own),
        (mod_h, mod),
        (w_h.at[:, pl.ds(D, D)], w.at[:, pl.ds(D, D)]),
        (w_h.at[:, pl.ds(2 * D, D)], w.at[:, pl.ds(2 * D, D)]),
        (control_h.at[pl.ds(0, 1)], control.at[pl.ds(0, 1)]),
        (control_h.at[pl.ds(3, 1)], control.at[pl.ds(1, 1)]),
        (valid_h, valid),
        (send_own_h, send_own),
        (send_ctl_h, send_ctl),
        (valid_pad_h, valid_pad),
        (w_h.at[:, pl.ds(0, D)], w.at[:, pl.ds(0, D)]),
    ]
    copies = [pltpu.make_async_copy(src, dst, sem.at[i]) for i, (src, dst) in enumerate(pairs)]
    for copy in copies:
        copy.start()
    for copy in copies[:3]:
        copy.wait()
    rows = hidden_rows(dot(own[...], latent[...]), mod)
    hid[:224] = rows[0]
    hid[224:] = rows[1]
    for c in (0, 1):
        copies[3 + c].wait()
        out = dot(hid[...], w[:, (c + 1) * D : (c + 2) * D])
        kv[c] = out.astype(BF).reshape(2, 7, 32, D)
    for copy in copies[5:]:
        copy.wait()
    rows = lax.broadcasted_iota(jnp.int32, (32, 1), 0)
    val = valid[...].astype(F32)
    for i, tile, rim in ((0, 0, 2 * SIDE + 1), (1, 3, 2 * SIDE + 10)):
        msg[i, :64] = dot(send_own[i], latent[...]).astype(BF)
        own_row = val[tile : tile + 1]
        ctl = dot((send_ctl[i].astype(F32) * own_row).astype(BF), control[i])
        row = dot(eight(own_row * own_row[:, rim : rim + 1]), valid_pad[...])
        msg[i, 64:, 256:] = ctl[:, 256:].astype(BF)
        msg[i, 64:, :256] = jnp.where(rows == 31, row[0:1], ctl[:, :256]).astype(BF)


def choose(odd, a, b):
    return jnp.where(odd > 0.5, a.astype(F32), b.astype(F32))


def pack_kernel(odd, msg, got_a, got_b, send_rim, out_a, out_b, above, below):
    row_odd, col_odd = odd[0][:1, :1], odd[1][:1, :1]
    above[...] = choose(row_odd, got_a[...], got_b[...]).astype(BF)
    below[...] = choose(row_odd, got_b[...], got_a[...]).astype(BF)
    messages = []
    for i in (0, 1):
        rim = dot(send_rim[i, :, :64], above[...]) + dot(send_rim[i, :, 64:], below[...])
        messages.append(msg[i, :64].astype(F32) + rim)
    out_a[:64] = choose(col_odd, messages[0], messages[1]).astype(BF)
    out_b[:64] = choose(col_odd, messages[1], messages[0]).astype(BF)
    out_a[64:] = choose(col_odd, msg[0, 64:], msg[1, 64:]).astype(BF)
    out_b[64:] = choose(col_odd, msg[1, 64:], msg[0, 64:]).astype(BF)


def middle_kernel(
    radius, latent, above, below, valid, mod, w, kv_own, middle, dist, key, second, kv_rim, attn, near, hid, qs, bias
):
    near[:256] = latent[...]
    near[256:320] = above[...]
    near[320:] = below[...]
    rows = hidden_rows(dot(middle[...], near[...]), mod)
    for g in (0, 1):
        hid[g * 112 : (g + 1) * 112] = rows[g][:112]
        hid[224 + g * 256 : 224 + (g + 1) * 256] = rows[g][112:]
    qs[...] = dot(hid[224:], w[:, :D]).astype(BF).reshape(2, 2, 128, D)
    out = dot(hid[:224], w[:, D:]).astype(BF)
    for c in (0, 1):
        kv_rim[c] = out[:, c * D : (c + 1) * D].reshape(2, 7, 16, D)
    val = valid[...].astype(F32)
    for i in (0, 1):
        fill_bias(bias, i, dist[i], key[i, 0], key[i, 1], second[i], val[2 * i : 2 * i + 1], val[2 * i + 1 : 2 * i + 2])

    for i in (0, 1):
        keys = inner_window(kv_own, kv_rim, 0, 3 * i, 4)
        values = inner_window(kv_own, kv_rim, 1, 3 * i, 4)

        def put(g, rows, o):
            attn[g, rows, 128 * i : 128 * i + 128] = o

        attend(
            lambda g, lanes: qs[g, i, :, lanes],
            lambda g, lanes: jnp.concatenate(keys(g, lanes), axis=0),
            lambda g, lanes: jnp.concatenate(values(g, lanes), axis=0),
            lambda r: bias[i, r],
            radius,
            put,
        )


def valid_rows(valid, west, east):
    val = valid[...].astype(F32)
    side = [ref[80:96, :256].astype(F32)[15:16, :TILE_TOK] for ref in (west, east)]
    return [side[0]] + [val[t : t + 1] for t in range(4)] + [side[1]]


def gather(unit, slot, comb, rows):
    weight = dot(eight(rows[unit]), slot[unit, 0]) + dot(eight(rows[unit + 1]), slot[unit, 1])
    return comb[unit].astype(F32) * weight[:1]


def block_sums(parts, rows, x, w_out, mod, west, east, slot, comb, ctl, put):
    weights = {u: gather(u, slot, comb, rows) for units, _ in parts for u in units}
    number = sum(jnp.sum(w, axis=1, keepdims=True) for w in weights.values())
    n = number.shape[0]
    attn = [0.0, 0.0]
    for units, ref in parts:
        weight = jnp.concatenate([weights[u] for u in units], axis=1).astype(BF)
        attn = [attn[g] + dot_nt(weight, ref[g]) for g in (0, 1)]
    attn = [a.astype(BF) for a in attn]
    proj = dot(jnp.concatenate(attn, axis=0), w_out[...])
    sums = (GUIDE * mod[2, 0:1]) * proj[:n] + ((1.0 - GUIDE) * mod[2, 1:2]) * proj[n:] + number * x
    return sums + ctl + dot(put[...], jnp.concatenate([west[64:], east[64:]], axis=0)), number


def edge_kernel(
    radius, odd, latent, above, below, got_a, got_b, valid, mod, w, kv_own, kv_rim, attn_mid, w_out, control,
    edge, dist, key, second, slot, comb, ctl, ctl_pick, put_ctl,
    out_a, out_b, attn, west, east, near, hid, qs, kv, bias,
):
    row_odd, col_odd = odd[0][:1, :1], odd[1][:1, :1]
    west[...] = choose(col_odd, got_a[...], got_b[...]).astype(BF)
    east[...] = choose(col_odd, got_b[...], got_a[...]).astype(BF)
    parts = []
    for i, message in ((0, west), (1, east)):
        at = 0
        for ref, lines in ((latent, 8), (above, 2), (below, 2)):
            for line in range(lines):
                near[i, at : at + 16] = ref[32 * line + 16 * i : 32 * line + 16 * i + 16]
                at += 16
        near[i, at:] = message[:64]
        parts.append(dot(edge[i], near[i]))
    x = jnp.concatenate([p[:96] for p in parts] + [p[96:] for p in parts], axis=0)
    normed = hidden_rows(x, mod)
    for g in (0, 1):
        hid[g * 192 : (g + 1) * 192] = normed[g][:192]
        hid[384 + g * 256 : 384 + (g + 1) * 256] = normed[g][192:]
    qs[...] = dot(hid[384:], w[:, :D]).astype(BF).reshape(2, 2, 128, D)
    out = dot(hid[:384], w[:, D:]).astype(BF)
    for c in (0, 1):
        kv[c] = out[:, c * D : (c + 1) * D].reshape(2, 4, 48, D)
    rows = valid_rows(valid, west, east)
    for i, u in ((0, 0), (1, 4)):
        fill_bias(bias, i, dist[i], key[i, 0], key[i, 1], second[i], rows[u], rows[u + 1])

    for i in (0, 1):

        def window(c):
            inner = inner_window(kv_own, kv_rim, c, 5 * i, 2)

            def get(g, lanes):
                outer = [kv[c, g, 2 * i, :, lanes], kv[c, g, 2 * i + 1, :, lanes]]
                parts = inner(g, lanes) + outer if i else outer + inner(g, lanes)
                return jnp.concatenate(parts, axis=0)

            return get

        def put(g, rows, o):
            attn[g, rows, 128 * i : 128 * i + 128] = o

        attend(lambda g, lanes: qs[g, i, :, lanes], window(0), window(1), lambda r: bias[i, r], radius, put)

    x = jnp.concatenate([above[...], below[...]], axis=0).astype(F32)
    weight = sum(dot(eight(rows[tile + 1]), ctl_pick[tile]) for tile in range(4))[:1]
    ends = [control[tile, at : at + 32] for tile in range(4) for at in (0, 112)]
    extra = dot((ctl[...].astype(F32) * weight).astype(BF), jnp.concatenate(ends, axis=0))
    sums, number = block_sums((((1, 3), attn_mid), ((0, 4), attn)), rows, x, w_out, mod, west, east, slot, comb, extra, put_ctl)
    row = lax.broadcasted_iota(jnp.int32, (64, 128), 0)
    lane = lax.broadcasted_iota(jnp.int32, (64, 128), 1)
    tails = []
    for at in (0, 64):
        tails.append(jnp.sum(jnp.where(row == lane, number[at : at + 64], 0.0), axis=0, keepdims=True))
    for out, upward in ((out_a, row_odd), (out_b, 1.0 - row_odd)):
        out[:64] = choose(upward, sums[:64], sums[64:]).astype(BF)
        out[64:, :128] = jnp.broadcast_to(choose(upward, tails[0], tails[1]), (16, 128)).astype(BF)
        out[64:, 128:] = jnp.zeros((16, D - 128), BF)


def core_kernel(
    radius, attn_mid, attn_edge, latent, west, east, valid, mod, w, kv_own, kv_rim, w_out, control,
    late, dist, key, second, slot, comb, ctl, put,
    out, rest, count, done, hid, qs, bias, attn, sem,
):
    rows = valid_rows(valid, west, east)
    normed = hidden_rows(dot(late[...], latent[...]), mod)
    for g in (0, 1):
        hid[g * LATE_ROWS : (g + 1) * LATE_ROWS] = normed[g]
    asked = dot(hid[...], w[:, :D]).astype(BF)
    for g in (0, 1):
        qs[g, :LATE_ROWS] = asked[g * LATE_ROWS : (g + 1) * LATE_ROWS]
        qs[g, LATE_ROWS:] = jnp.zeros((128 - LATE_ROWS, D), BF)
    fill_bias(bias, 0, dist[0], key[0, 0], key[0, 1], second[0], rows[2], rows[3])
    keys = inner_window(kv_own, kv_rim, 0, 1, 5)
    values = inner_window(kv_own, kv_rim, 1, 1, 5)

    def keep(g, lines, o):
        attn[g, lines, :] = o

    attend(
        lambda g, lanes: qs[g, :, lanes],
        lambda g, lanes: jnp.concatenate(keys(g, lanes), axis=0),
        lambda g, lanes: jnp.concatenate(values(g, lanes), axis=0),
        lambda r: bias[0, r],
        radius,
        keep,
    )
    extra = sum(dot((ctl[tile].astype(F32) * rows[tile + 1]).astype(BF), control[tile]) for tile in range(4))
    x = latent[...].astype(F32)
    sums, number = block_sums(
        (((1, 3), attn_mid), ((0, 4), attn_edge), ((2,), attn)), rows, x, w_out, mod, west, east, slot, comb, extra, put
    )
    done[...] = (sums[64:192] / number[64:192]).astype(BF)
    copy = pltpu.make_async_copy(done, out.at[pl.ds(64, 128)], sem)
    copy.start()
    rest[0] = sums[:64]
    rest[1] = sums[192:]
    count[0] = jnp.broadcast_to(number[:64], (64, 128))
    count[1] = jnp.broadcast_to(number[192:], (64, 128))
    copy.wait()


def final_kernel(odd, rest, count, got_a, got_b, whole_out, out, done, sem):
    del whole_out
    row = lax.broadcasted_iota(jnp.int32, (64, 128), 0)
    lane = lax.broadcasted_iota(jnp.int32, (64, 128), 1)
    copies = []
    for i in (0, 1):
        first, second = (got_a, got_b) if i == 0 else (got_b, got_a)
        got = choose(odd[0][:1, :1], first[...], second[...])
        tail = got[64:65, :128]
        number = jnp.sum(jnp.where(row == lane, tail, 0.0), axis=1, keepdims=True) + count[i][:, :1]
        done[i] = ((rest[i] + got[:64]) / number).astype(BF)
        copies.append(pltpu.make_async_copy(done.at[i], out.at[pl.ds(192 * i, 64)], sem.at[i]))
        copies[i].start()
    for copy in copies:
        copy.wait()


def swaps(size_r, size_c, by_row, turn):
    perm = []
    for r in range(size_r):
        for c in range(size_c):
            here, size = (r, size_r) if by_row else (c, size_c)
            there = ((here + turn) ^ 1) - turn
            if 0 <= there < size:
                to = (there, c) if by_row else (r, there)
            else:
                to = (r, min(c ^ 1, size_c - 1)) if by_row else (min(r ^ 1, size_r - 1), c)
            perm.append((r * size_c + c, to[0] * size_c + to[1]))
    return perm


def call(kernel, outs, args, specs=None, out_specs=None, scratch=(), cost=(1e9, 4e6), aliases=None, limit=VMEM):
    specs = specs or {}
    out_specs = out_specs or {}
    vmem = pl.BlockSpec(memory_space=pltpu.VMEM)
    return pl.pallas_call(
        kernel,
        out_shape=outs,
        in_specs=[specs.get(i, vmem) for i in range(len(args))],
        out_specs=[out_specs.get(i, vmem) for i in range(len(outs))],
        scratch_shapes=scratch,
        input_output_aliases=aliases or {},
        compiler_params=pltpu.CompilerParams(vmem_limit_bytes=limit),
        cost_estimate=pl.CostEstimate(flops=int(cost[0]), bytes_accessed=int(cost[1]), transcendentals=0),
    )(*[jnp.asarray(a) for a in args])


def shape(*dims, dtype=BF):
    return jax.ShapeDtypeStruct(dims, dtype)


def local(latent, control, valid, radius, modulation, w_qkv, w_out):
    t = tables()
    size_r, size_c = lax.axis_size("trow"), lax.axis_size("tcol")
    x = latent.reshape(256, D)
    control = control.reshape(4, TILE_TOK, D)
    valid = valid.reshape(4, TILE_TOK)
    row, col = lax.axis_index("trow") % 2, lax.axis_index("tcol") % 2
    mark = jnp.broadcast_to(jnp.stack([row, col]).astype(F32)[:, None, None], (2, 8, 128))
    axes = ("trow", "tcol")
    by_row = [swaps(size_r, size_c, True, turn) for turn in (0, 1)]
    by_col = [swaps(size_r, size_c, False, turn) for turn in (0, 1)]
    near_a = lax.ppermute(lax.dynamic_slice_in_dim(x, 192 * (1 - row), 64, 0), axes, by_row[0])
    near_b = lax.ppermute(lax.dynamic_slice_in_dim(x, 192 * row, 64, 0), axes, by_row[1])
    smem = pl.BlockSpec(memory_space=pltpu.SMEM)
    hbm = pl.BlockSpec(memory_space=pl.ANY)

    mod = modulation.transpose(1, 0, 2)
    far = lambda a: pltpu.with_memory_space_constraint(jnp.asarray(a), pltpu.MemorySpace.HBM)
    first = [x, control, valid, mod, w_qkv, t["own"], t["send_own"], t["send_ctl"], t["valid_pad"]]
    staged = [(256, D, BF), (2, TILE_TOK, D, BF), (4, TILE_TOK, jnp.int32), (3, 2, D, F32)]
    staged += [t[k].shape + (BF,) for k in ("own", "send_own", "send_ctl", "valid_pad")]
    kv_own, msg, w, mark = call(
        own_kernel,
        [shape(2, 2, 7, 32, D), shape(2, 96, D), shape(D, 3 * D), shape(2, 8, 128, dtype=F32)],
        [far(a) for a in first] + [mark],
        specs={i: hbm for i in range(len(first))},
        scratch=[pltpu.VMEM(s[:-1], s[-1]) for s in staged]
        + [pltpu.VMEM((448, D), BF), pltpu.SemaphoreType.DMA((12,))],
        cost=(3.6e9, 12e6),
    )
    side_a, side_b, above, below = call(
        pack_kernel,
        [shape(96, D), shape(96, D), shape(64, D), shape(64, D)],
        [mark, msg, near_a, near_b, t["send_rim"]],
        cost=(1e8, 1e6),
    )
    side_a = lax.ppermute(side_a, axes, by_col[0])
    side_b = lax.ppermute(side_b, axes, by_col[1])

    mid, ends, late = slice(1, 4, 2), slice(0, 5, 4), slice(2, 3)
    kv_rim, attn_mid = call(
        middle_kernel,
        [shape(2, 2, 7, 16, D), shape(2, D, 256)],
        [
            radius, x, above, below, valid, mod, w, kv_own,
            t["middle"], t["dist_mid"], t["key_mid"], t["second"][mid],
        ],
        specs={0: smem},
        scratch=[
            pltpu.VMEM((384, D), BF),
            pltpu.VMEM((736, D), BF),
            pltpu.VMEM((2, 2, 128, D), BF),
            pltpu.VMEM((2, 5, KEYS, 128), F32),
        ],
        cost=(8e9, 14e6),
    )
    sums_a, sums_b, attn_edge, west, east = call(
        edge_kernel,
        [shape(80, D), shape(80, D), shape(2, D, 256), shape(96, D), shape(96, D)],
        [
            radius, mark, x, above, below, side_a, side_b, valid, mod, w, kv_own, kv_rim, attn_mid, w_out, control,
            t["edge"], t["dist_edge"], t["key_edge"], t["second"][ends], t["slot"], t["comb_rim"], t["ctl_rim"], t["ctl_pick"], t["put_rim"],
        ],
        specs={0: smem},
        scratch=[
            pltpu.VMEM((2, 256, D), BF),
            pltpu.VMEM((896, D), BF),
            pltpu.VMEM((2, 2, 128, D), BF),
            pltpu.VMEM((2, 2, 4, 48, D), BF),
            pltpu.VMEM((2, 5, KEYS, 128), F32),
        ],
        cost=(1e10, 16e6),
    )
    sums_a = lax.ppermute(sums_a, axes, by_row[0])
    sums_b = lax.ppermute(sums_b, axes, by_row[1])
    out, rest, count = call(
        core_kernel,
        [shape(256, D), shape(2, 64, D, dtype=F32), shape(2, 64, 128, dtype=F32)],
        [
            radius, attn_mid, attn_edge, x, west, east, valid, mod, w, kv_own, kv_rim, w_out, control,
            t["late"], t["dist_late"], t["key_late"], t["second"][late], t["slot"], t["comb_core"], t["ctl_core"], t["put_core"],
        ],
        specs={0: smem},
        out_specs={0: hbm},
        scratch=[
            pltpu.VMEM((128, D), BF),
            pltpu.VMEM((2 * LATE_ROWS, D), BF),
            pltpu.VMEM((2, 128, D), BF),
            pltpu.VMEM((1, 5, LATE_KEYS, 128), F32),
            pltpu.VMEM((2, D, 128), BF),
            pltpu.SemaphoreType.DMA,
        ],
        cost=(4e9, 8e6),
    )
    (out,) = call(
        final_kernel,
        [shape(256, D)],
        [mark, rest, count, sums_a, sums_b, out],
        specs={5: hbm},
        out_specs={0: hbm},
        scratch=[pltpu.VMEM((2, 64, D), BF), pltpu.SemaphoreType.DMA((2,))],
        aliases={5: 0},
        cost=(2e8, 3e6),
    )
    return out.reshape(CORE, 32, D)


def solution(mesh):
    placed = (
        P("trow", "tcol", None),
        P("trow", "tcol", None, None),
        P("trow", "tcol", None),
        P(),
        P(),
        P(),
        P(),
    )
    return jax.shard_map(
        local, mesh=mesh, in_specs=placed, out_specs=P("trow", "tcol", None), check_vma=False
    )
```
